32 devices in a mesh: dp: 8 (over z, x), segment: 4 (over y, core).
Axes of the slice: x: 2, y: 2, z: 4, core: 2. Of those that a mesh axis runs over, the one named last changes fastest.
Arguments:
- query_cache: bfloat16 [256, 4096], P(('dp', 'segment')), may hold values from -0.125 to 0.125, as said below
- passage_cache: bfloat16 [256, 4096], P(('dp', 'segment')), may hold values from -0.125 to 0.125, as said below
- hard_offsets: int32 [256, 1], P(('dp', 'segment')), may hold values from 0 to 127
- passage_lengths: int32 [8], replicated, may hold values from 1 to 64, 128 in all
- segment_inputs: bfloat16 [4, 128, 4096], P('segment', 'dp'), may hold values from -6 to 6
- segment_cotangents: bfloat16 [4, 128, 4096], P('segment', 'dp'), may hold values from -6 to 6
- norm_gain: float32 [4, 4096], P('segment'), may hold values from 0.5 to 1.5
- gate_weight: bfloat16 [4, 4096, 14336], P('segment', None, 'dp'), may hold values from -0.09375 to 0.09375
- up_weight: bfloat16 [4, 4096, 14336], P('segment', None, 'dp'), may hold values from -0.09375 to 0.09375
- down_weight: bfloat16 [4, 14336, 4096], P('segment', 'dp'), may hold values from -0.046875 to 0.046875
Outputs:
- query_grads: bfloat16 [256, 4096], P(('dp', 'segment'))
- passage_grads: bfloat16 [256, 4096], P(('dp', 'segment'))
- input_grads: bfloat16 [4, 128, 4096], P('segment', 'dp')
- gate_grads: bfloat16 [4, 4096, 14336], P('segment', None, 'dp')
- up_grads: bfloat16 [4, 4096, 14336], P('segment', None, 'dp')
- down_grads: bfloat16 [4, 14336, 4096], P('segment', 'dp')
- gain_grads: float32 [4, 4096], P('segment')
The draws below stay inside these ranges and needn't reach their ends.
Inputs may be any that keep to these rules, and one draw needn't show every extreme that they name: Query i's hard negative k is passage (i // 128) * 128 + hard_offsets[i, k]. `passage_lengths`: the lengths sum to 128; the longest is exactly 64. `query_cache`: cached query embeddings, no row zero. `passage_cache`: cached passage embeddings, no row zero.
All inputs are finite; a program needn't handle non-finite values.
Results may differ from the reference program's by a relative error of at most 0.0071.
Values may be sent and summed in bfloat16 or wider, within the bound.
No kernel may reach another device: no remote copies, remote signals or barrier semaphores. Data moves between devices by JAX's collectives and lax.ppermute only.
A program may use at most 192 MiB of HBM per device.

```python
import math
import jax
import jax.numpy as jnp
import numpy as np
from jax import lax

D = 4096
FF = 14336
PAIR_DEV = 8
NEG = 1
HN_BLOCK = 128
PAIRS = 256
SEGMENT_TOK = 128
MB_PASS = 8
N_SEGMENT = 4


def shared_parts(key):
    base_key = jax.random.fold_in(key, 4711)
    topic_key = jax.random.fold_in(base_key, 1)
    label_key = jax.random.fold_in(base_key, 2)
    noise_key = jax.random.fold_in(base_key, 3)
    topics = jax.random.normal(topic_key, (8, D), jnp.float32)
    labels = jax.random.randint(label_key, (PAIRS,), 0, 8)
    common = jax.random.normal(noise_key, (PAIRS, D), jnp.float32)
    strength = 0.7
    return (jnp.take(topics, labels, axis=0) * strength, common)


def own_noise_rows(key):
    return jax.random.normal(key, (PAIRS, D), jnp.float32)


def finish_rows(key, row_values):
    scaled = row_values / math.sqrt(D)
    clip_bound = 8.0 / math.sqrt(D)
    return jnp.clip(scaled, -clip_bound, clip_bound).astype(jnp.bfloat16)


def draw_query_cache(key, part):
    topic_rows, common = shared_parts(key)
    return finish_rows(jax.random.fold_in(key, 11), topic_rows + common)


def draw_passage_cache(key, part):
    topic_rows, common = shared_parts(key)
    own_noise = own_noise_rows(jax.random.fold_in(key, 12))
    return finish_rows(jax.random.fold_in(key, 13), topic_rows + 0.05 * common + own_noise)


def plant(values, rng, least, high):
    extent = values.shape
    index_at = [jax.random.randint(jax.random.fold_in(rng, axis), (), 0, extent[axis]) for axis in range(len(extent))]
    values = values.at[tuple(index_at)].set(least)
    longest = extent.index(max(extent))
    index_at[longest] = (index_at[longest] + 1) % extent[longest]
    return values.at[tuple(index_at)].set(high)


def levels(stream_key, shape, cuts, smallest, largest):
    def one(axis_at, parts):
        steps = jax.random.uniform(jax.random.fold_in(jax.random.fold_in(stream_key, 6), axis_at), (parts,), jnp.float32, smallest / len(cuts), largest / len(cuts))
        return jnp.repeat(jnp.exp(steps), shape[axis_at] // parts).reshape((-1,) + (1,) * (len(shape) - axis_at - 1))

    loudness = one(*cuts[0])
    for cut in cuts[1:]:
        loudness = loudness * one(*cut)
    return loudness


def length_profile(count, total, limit, lean):
    loads = [(1 << 20) // math.isqrt(standing ** lean) + 1 for standing in range(2, count + 1)]
    spare, holding = total - limit - (count - 1), [1] * (count - 1)
    while spare > 0:
        free = [i for i in range(count - 1) if holding[i] < limit]
        pool, left = sum([loads[i] for i in free]), spare
        for i in free:
            more = min(limit - holding[i], max(1, left * loads[i] // pool), spare)
            holding[i] = holding[i] + more
            spare = spare - more
    return np.array([limit] + holding)


def ragged(key, number_of, total, limit, slope):
    if number_of == 2:
        one = jax.random.randint(key, (), max(1, total - limit), min(limit, total - 1) + 1)
        return jnp.stack([one, total - one])
    sizes = jnp.asarray(length_profile(number_of, total, limit, slope), jnp.int32)
    couples = (number_of - 1) // 2
    giver, taker = sizes[1:1 + 2 * couples:2], sizes[2:2 + 2 * couples:2]
    margin = jnp.minimum(giver - 1, limit - taker)
    shifted = jax.random.randint(jax.random.fold_in(key, 1), (couples,), 0, 1 << 20) % (margin + 1)
    sizes = sizes.at[1:1 + 2 * couples:2].set(giver - shifted).at[2:2 + 2 * couples:2].set(taker + shifted)
    return sizes[jax.random.permutation(jax.random.fold_in(key, 2), number_of)]


def bell_draw(stream_key, shape, scale, bound, pieces=(), kind=jnp.bfloat16):
    result = scale * jax.random.normal(stream_key, shape, jnp.float32)
    if pieces:
        result = result * levels(stream_key, shape, pieces, -0.22, 0.18)
    return jnp.clip(result, -bound, bound).astype(kind)


def setup_inputs(seed: int = 0) -> dict:
    keys = jax.random.split(jax.random.key(seed), 11)
    return {
        "query_cache": draw_query_cache(jax.random.fold_in(keys[10], 71), 0),
        "passage_cache": draw_passage_cache(jax.random.fold_in(keys[10], 71), 0),
        "hard_offsets": plant(jax.random.randint(keys[2], (PAIRS, NEG), 0, HN_BLOCK), jax.random.fold_in(keys[2], 1), 0, HN_BLOCK - 1).astype(jnp.int32),
        "passage_lengths": ragged(keys[3], MB_PASS, SEGMENT_TOK, SEGMENT_TOK // 2, 2).astype(jnp.int32),
        "segment_inputs": bell_draw(keys[4], (N_SEGMENT, SEGMENT_TOK, D), 1.0, 6.0, ((0, 4), (1, 8))),
        "segment_cotangents": bell_draw(keys[5], (N_SEGMENT, SEGMENT_TOK, D), 1.0, 6.0, ((0, 4), (1, 8))),
        "norm_gain": jnp.clip(1.0 + 0.1 * jax.random.normal(keys[6], (N_SEGMENT, D), jnp.float32), 0.5, 1.5),
        "gate_weight": bell_draw(keys[7], (N_SEGMENT, D, FF), D ** -0.5, 0.09375, ((0, 4), (2, 8))),
        "up_weight": bell_draw(keys[8], (N_SEGMENT, D, FF), D ** -0.5, 0.09375, ((0, 4), (2, 8))),
        "down_weight": bell_draw(keys[9], (N_SEGMENT, FF, D), FF ** -0.5, 0.046875, ((0, 4), (1, 8))),
    }


TAU = 0.02
HN_WEIGHT = 64.0
EPS_NORM = 1e-06
EPS_RMS = 1e-05

def unit_rows(values):
    widened = values.astype(jnp.float32)
    inverse = lax.rsqrt(lax.optimization_barrier(jnp.sum(widened * widened, axis=-1, keepdims=True)) + EPS_NORM)
    return (widened * inverse, inverse)

def unit_back(gradient, unit_value, inverse):
    return inverse * (gradient - unit_value * lax.optimization_barrier(jnp.sum(gradient * unit_value, axis=-1, keepdims=True)))

def hard_weights(hard_offsets, first_row, column_index):
    row_index = first_row + jnp.arange(hard_offsets.shape[0], dtype=jnp.int32)
    picked = row_index // HN_BLOCK * HN_BLOCK
    picked = picked[:, None] + hard_offsets
    tallies = jnp.zeros((hard_offsets.shape[0], column_index.shape[0]), jnp.float32)
    for column in range(hard_offsets.shape[1]):
        tallies = tallies + (picked[:, column:column + 1] == column_index[None, :]).astype(jnp.float32)
    return 1.0 + HN_WEIGHT * tallies

def mean_pool_back(passage_lengths, token_index, rows):
    last_tokens = jnp.cumsum(passage_lengths).astype(jnp.int32) - 1
    first_tokens = last_tokens - passage_lengths + 1
    member = (token_index[:, None] >= first_tokens[None, :]) & (token_index[:, None] <= last_tokens[None, :])
    selector = member.astype(jnp.float32) / passage_lengths.astype(jnp.float32)[None, :]
    return jnp.dot(selector, rows.astype(jnp.float32), precision=lax.Precision.HIGHEST).astype(jnp.bfloat16)

def layer_grads(inputs, cotangent, gain_row, gate_matrix, up_matrix, down_matrix):
    widened = inputs.astype(jnp.float32)
    inverse = lax.rsqrt(lax.optimization_barrier(jnp.mean(widened * widened, axis=-1, keepdims=True)) + EPS_RMS)
    unit_value = widened * inverse
    normed = (unit_value * gain_row).astype(jnp.bfloat16)
    gate_value = jnp.dot(normed, gate_matrix, preferred_element_type=jnp.float32)
    up_value = jnp.dot(normed, up_matrix, preferred_element_type=jnp.float32)
    sigmoid_gate = jax.nn.sigmoid(gate_value)
    activation = gate_value * sigmoid_gate
    hidden = (activation * up_value).astype(jnp.bfloat16)
    hidden_delta = jnp.dot(cotangent, down_matrix.T, preferred_element_type=jnp.float32)
    up_delta = (hidden_delta * activation).astype(jnp.bfloat16)
    gate_delta = (hidden_delta * up_value * sigmoid_gate * (1.0 + gate_value * (1.0 - sigmoid_gate))).astype(jnp.bfloat16)
    down_grad = jnp.dot(hidden.T, cotangent, preferred_element_type=jnp.float32).astype(jnp.bfloat16)
    gate_grad = jnp.dot(normed.T, gate_delta, preferred_element_type=jnp.float32).astype(jnp.bfloat16)
    up_grad = jnp.dot(normed.T, up_delta, preferred_element_type=jnp.float32).astype(jnp.bfloat16)
    normed_delta = jnp.dot(gate_delta, gate_matrix.T, preferred_element_type=jnp.float32) + jnp.dot(up_delta, up_matrix.T, preferred_element_type=jnp.float32)
    gain_grad = lax.optimization_barrier(jnp.sum(normed_delta * unit_value, axis=0))
    scaled_delta = normed_delta * gain_row
    input_grad = cotangent.astype(jnp.float32) + inverse * (scaled_delta - unit_value * lax.optimization_barrier(jnp.mean(scaled_delta * unit_value, axis=-1, keepdims=True)))
    return (input_grad.astype(jnp.bfloat16), gate_grad, up_grad, down_grad, gain_grad)

def reference(query_cache, passage_cache, hard_offsets, passage_lengths, segment_inputs, segment_cotangents, norm_gain, gate_weight, up_weight, down_weight):
    query_unit, query_inverse = unit_rows(query_cache)
    passage_unit, passage_inverse = unit_rows(passage_cache)
    query_low = query_unit.astype(jnp.bfloat16)
    passage_low = passage_unit.astype(jnp.bfloat16)
    scores = jnp.dot(query_low, passage_low.T, preferred_element_type=jnp.float32) / TAU
    column_index = jnp.arange(PAIRS, dtype=jnp.int32)
    weights = hard_weights(hard_offsets, 0, column_index)
    weighted = weights * jnp.exp(scores)
    totals = lax.optimization_barrier(jnp.sum(weighted, axis=1, keepdims=True))
    positive = (column_index[:, None] == column_index[None, :]).astype(jnp.float32)
    dscore = (weighted / totals - positive).astype(jnp.bfloat16)
    query_dir = jnp.dot(dscore, passage_low, preferred_element_type=jnp.float32) / TAU
    passage_dir = jnp.dot(dscore.T, query_low, preferred_element_type=jnp.float32) / TAU
    query_grads = unit_back(query_dir, query_unit, query_inverse).astype(jnp.bfloat16)
    passage_grads = unit_back(passage_dir, passage_unit, passage_inverse).astype(jnp.bfloat16)
    first_pass = (N_SEGMENT - 1) * PAIR_DEV
    batch_rows = passage_grads[first_pass:first_pass + MB_PASS]
    token_index = jnp.arange(SEGMENT_TOK, dtype=jnp.int32)
    pooled = mean_pool_back(passage_lengths, token_index, batch_rows)
    results = []
    for section in range(N_SEGMENT):
        if section < N_SEGMENT - 1:
            cotangent = segment_cotangents[section]
        else:
            cotangent = pooled
        results.append(layer_grads(segment_inputs[section], cotangent, norm_gain[section], gate_weight[section], up_weight[section], down_weight[section]))
    input_grads = jnp.stack([item[0] for item in results])
    gate_grads = jnp.stack([item[1] for item in results])
    up_grads = jnp.stack([item[2] for item in results])
    down_grads = jnp.stack([item[3] for item in results])
    gain_grads = jnp.stack([item[4] for item in results])
    return (query_grads, passage_grads, input_grads, gate_grads, up_grads, down_grads, gain_grads)
```

```python
import jax
import jax.numpy as jnp
from jax import lax
from jax.experimental import pallas as pl
from jax.experimental.pallas import tpu as pltpu
from jax.sharding import PartitionSpec as P

HN_BLOCK = 128
TAU = 0.02
HN_WEIGHT = 64.0
EPS_NORM = 1e-06
EPS_RMS = 1e-05

F32 = jnp.float32
BF16 = jnp.bfloat16
MIB = 2**20
NT = (((1,), (1,)), ((), ()))
TN = (((0,), (0,)), ((), ()))


def vmem():
    return pl.BlockSpec(memory_space=pltpu.VMEM)


def smem():
    return pl.BlockSpec(memory_space=pltpu.SMEM)


def anywhere():
    return pl.BlockSpec(memory_space=pl.ANY)


def params(mib):
    return pltpu.CompilerParams(vmem_limit_bytes=mib * MIB)


def iota(shape, axis):
    return lax.broadcasted_iota(jnp.int32, shape, axis)


def split3(value):
    high = value.astype(BF16).astype(F32)
    rest = value - high
    middle = rest.astype(BF16).astype(F32)
    return high, middle, (rest - middle).astype(BF16).astype(F32)


def to_row(column, width):
    n = column.shape[0]
    pick = iota((n, width), 0) == iota((n, width), 1)
    return jnp.sum(jnp.where(pick, column, 0.0), axis=0, keepdims=True)


def to_columns(rows, n):
    shape = rows.shape[:-2] + (n, rows.shape[-1])
    pick = iota(shape, len(shape) - 2) == iota(shape, len(shape) - 1)
    return jnp.sum(jnp.where(pick, rows, 0.0), axis=-1, keepdims=True)


def row_inverse(ref, rows, mean, eps):
    total = jnp.zeros((rows, 1), F32)
    width = ref.shape[1]
    step = min(width, 1024)
    for at in range(0, width, step):
        part = ref[:, at : at + step].astype(F32)
        total += jnp.sum(part * part, axis=1, keepdims=True)
    if mean:
        total = total / width
    return lax.rsqrt(total + eps)


def pack_rows(query_ref, passage_ref, out_ref):
    count, block, cols = out_ref.shape
    rows = query_ref.shape[0]
    inverse = jnp.concatenate(
        [
            row_inverse(query_ref, rows, False, EPS_NORM),
            row_inverse(passage_ref, rows, False, EPS_NORM),
        ],
        axis=0,
    )
    terms = [to_row(term, cols) for term in split3(inverse)]
    extra = jnp.concatenate(
        terms + [jnp.zeros((block - 2 * rows - 3, cols), F32)], axis=0
    )
    for peer in range(count):
        cut = slice(peer * cols, (peer + 1) * cols)
        both = jnp.concatenate(
            [
                query_ref[:, cut].astype(F32),
                passage_ref[:, cut].astype(F32),
                extra,
            ],
            axis=0,
        )
        out_ref[peer] = both.astype(BF16)


def partial_scores(rows_ref, out_ref, unit_ref, inverse_ref):
    count, block, cols = rows_ref.shape
    rows = out_ref.shape[1]
    pairs = count * rows
    values = rows_ref[...].astype(F32)
    lines = values[:, 2 * rows : 2 * rows + 1]
    lines = lines + values[:, 2 * rows + 1 : 2 * rows + 2]
    lines = lines + values[:, 2 * rows + 2 : 2 * rows + 3]
    inverse = to_columns(lines, 2 * rows)
    unit = values[:, : 2 * rows] * inverse
    query_unit = unit[:, :rows].reshape(pairs, cols)
    passage_unit = unit[:, rows:].reshape(pairs, cols)
    unit_ref[0] = query_unit
    unit_ref[1] = passage_unit
    inverse_ref[0] = inverse[:, :rows].reshape(pairs, 1)
    inverse_ref[1] = inverse[:, rows:].reshape(pairs, 1)
    scores = lax.dot_general(
        query_unit.astype(BF16), passage_unit.astype(BF16), NT, preferred_element_type=F32
    )
    out_ref[...] = scores.reshape(out_ref.shape)


def softmax_rows(first_ref, parts_ref, offsets_ref, out_ref):
    count, block, pairs = out_ref.shape
    rows = parts_ref.shape[1]
    scores = jnp.sum(parts_ref[...], axis=0) / TAU
    row = first_ref[0] + iota((rows, pairs), 0)
    column = iota((rows, pairs), 1)
    base = row // HN_BLOCK * HN_BLOCK
    tallies = jnp.zeros((rows, pairs), F32)
    for k in range(offsets_ref.shape[1]):
        tallies += (base + offsets_ref[:, k : k + 1] == column).astype(F32)
    weighted = (1.0 + HN_WEIGHT * tallies) * jnp.exp(scores)
    totals = jnp.sum(weighted, axis=1, keepdims=True)
    dscore = weighted / totals - (row == column).astype(F32)
    dscore = dscore.astype(BF16).astype(F32)
    product = dscore * scores
    lines = list(split3(jnp.sum(product, axis=0, keepdims=True)))
    lines += [
        to_row(term, pairs) for term in split3(jnp.sum(product, axis=1, keepdims=True))
    ]
    lines.append(jnp.zeros((block - rows - 6, pairs), F32))
    message = jnp.concatenate([dscore] + lines, axis=0).astype(BF16)
    for peer in range(count):
        out_ref[peer] = message


def pair_grads(first, take, rows_ref, unit_ref, inverse_ref, out_ref):
    count, block, pairs = rows_ref.shape
    rows = pairs // count
    cols = unit_ref.shape[2]
    values = rows_ref[...].astype(F32)
    dscore = values[:, :rows].reshape(pairs, pairs).astype(BF16)
    column_line = jnp.sum(
        values[:, rows] + values[:, rows + 1] + values[:, rows + 2], axis=0, keepdims=True
    )
    column_dots = to_columns(column_line, pairs)
    row_lines = (
        values[:, rows + 3 : rows + 4]
        + values[:, rows + 4 : rows + 5]
        + values[:, rows + 5 : rows + 6]
    )
    row_dots = to_columns(row_lines, rows).reshape(pairs, 1)
    query_unit, passage_unit = unit_ref[0], unit_ref[1]
    query_dir = (
        jnp.dot(dscore, passage_unit.astype(BF16), preferred_element_type=F32) / TAU
    )
    passage_dir = (
        lax.dot_general(dscore, query_unit.astype(BF16), TN, preferred_element_type=F32) / TAU
    )
    query_grad = inverse_ref[0] * (query_dir - query_unit * row_dots)
    passage_grad = inverse_ref[1] * (passage_dir - passage_unit * column_dots)
    pieces = [
        query_grad.reshape(count, rows, cols),
        passage_grad.reshape(count, rows, cols),
    ]
    picked = passage_grad[first : first + take]
    spare = out_ref.shape[1] - 2 * rows - take
    if spare:
        picked = jnp.concatenate([picked, jnp.zeros((spare, cols), F32)], axis=0)
    pieces.append(jnp.broadcast_to(picked[None], (count,) + picked.shape))
    out_ref[...] = jnp.concatenate(pieces, axis=1).astype(BF16)


def layer(
    cuts,
    deep_cuts,
    place_ref,
    lengths_ref,
    back_ref,
    x_ref,
    given_ref,
    gain_ref,
    gate_hbm,
    up_hbm,
    down_hbm,
    query_out,
    passage_out,
    delta_out,
    hidden_out,
    d_up_out,
    d_gate_out,
    normed_out,
    cot_out,
    gate_w,
    up_w,
    down_w,
    gate_s,
    up_s,
    inverse_s,
    gain_s,
    gate_sem,
    up_sem,
    down_sem,
):
    tokens, width = x_ref.shape
    units = gate_s.shape[1]
    owners, own, _ = delta_out.shape
    step = width // cuts
    copies = []
    for c in range(cuts):
        part = pl.ds(c * step, step)
        a = pltpu.make_async_copy(gate_hbm.at[part], gate_w.at[part], gate_sem.at[c])
        b = pltpu.make_async_copy(up_hbm.at[part], up_w.at[part], up_sem.at[c])
        a.start()
        b.start()
        copies.append((a, b))
    deep = units // deep_cuts
    deep_copies = []
    for c in range(deep_cuts):
        part = pl.ds(c * deep, deep)
        a = pltpu.make_async_copy(down_hbm.at[part], down_w.at[part], down_sem.at[c])
        a.start()
        deep_copies.append(a)

    inverse = row_inverse(x_ref, tokens, True, EPS_RMS)
    inverse_s[...] = inverse
    for c in range(cuts):
        cut = slice(c * step, (c + 1) * step)
        normed_out[:, cut] = (
            x_ref[:, cut].astype(F32) * inverse * gain_ref[:, cut]
        ).astype(BF16)

    count, block, cols = back_ref.shape
    rows = query_out.shape[0]
    passages = block - 2 * rows
    token = iota((tokens, 1), 0)
    lane = iota((tokens, passages), 1)
    start = jnp.int32(0)
    member = jnp.zeros((tokens, passages), F32)
    scale = jnp.zeros((tokens, 1), F32)
    for m in range(lengths_ref.shape[0]):
        length = lengths_ref[m]
        inside = jnp.logical_and(token >= start, token < start + length)
        member = jnp.where(jnp.logical_and(inside, lane == m), 1.0, member)
        scale = jnp.where(inside, 1.0 / (jnp.zeros((tokens, 1), F32) + length.astype(F32)), scale)
        start = start + length
    member = member.astype(BF16)
    last = place_ref[0] == 1
    for peer in range(count):
        cut = slice(peer * cols, (peer + 1) * cols)
        piece = back_ref[peer].astype(F32)
        query_out[:, cut] = piece[:rows].astype(BF16)
        passage_out[:, cut] = piece[rows : 2 * rows].astype(BF16)
        spread = jnp.dot(member, piece[2 * rows :].astype(BF16), preferred_element_type=F32)
        pooled = (spread * scale).astype(BF16)
        cot_out[:, cut] = jnp.where(last, pooled, given_ref[:, cut])

    for c in range(cuts):
        cut = slice(c * step, (c + 1) * step)
        copies[c][0].wait()
        copies[c][1].wait()
        gate = jnp.dot(normed_out[:, cut], gate_w[cut, :], preferred_element_type=F32)
        up = jnp.dot(normed_out[:, cut], up_w[cut, :], preferred_element_type=F32)
        if c == 0:
            gate_s[...] = gate
            up_s[...] = up
        else:
            gate_s[...] += gate
            up_s[...] += up
    for c in range(deep_cuts):
        cut = slice(c * deep, (c + 1) * deep)
        deep_copies[c].wait()
        d_hidden = lax.dot_general(cot_out[...], down_w[cut, :], NT, preferred_element_type=F32)
        gate, up = gate_s[:, cut], up_s[:, cut]
        sigmoid = jax.nn.sigmoid(gate)
        active = gate * sigmoid
        hidden_out[:, cut] = (active * up).astype(BF16)
        d_up_out[:, cut] = (d_hidden * active).astype(BF16)
        d_gate_out[:, cut] = (
            d_hidden * up * sigmoid * (1.0 + gate * (1.0 - sigmoid))
        ).astype(BF16)
    inverse = inverse_s[...]
    for c in range(cuts):
        cut = slice(c * step, (c + 1) * step)
        delta = lax.dot_general(
            d_gate_out[...], gate_w[cut, :], NT, preferred_element_type=F32
        ) + lax.dot_general(d_up_out[...], up_w[cut, :], NT, preferred_element_type=F32)
        delta_out[:, :, cut] = delta.astype(BF16).reshape(owners, own, step)
        gain_s[:, cut] = jnp.sum(
            delta * (x_ref[:, cut].astype(F32) * inverse), axis=0, keepdims=True
        )
    fold = width // own
    gain = jnp.concatenate(
        [gain_s[:, r * fold : (r + 1) * fold] for r in range(own)], axis=0
    )
    high, low, _ = split3(gain)
    tail = jnp.concatenate([high, low], axis=1).astype(BF16)
    for owner in range(owners):
        delta_out[owner, :, width:] = tail


def weight_grads(
    normed_ref, d_gate_ref, d_up_ref, hidden_ref, cot_ref, gate_out, up_out, down_out, hidden_t
):
    @pl.when(pl.program_id(0) == 0)
    def _():
        hidden_t[...] = hidden_ref[...].T

    gate_out[...] = lax.dot_general(
        normed_ref[...], d_gate_ref[...], TN, preferred_element_type=F32
    ).astype(BF16)
    up_out[...] = lax.dot_general(
        normed_ref[...], d_up_ref[...], TN, preferred_element_type=F32
    ).astype(BF16)
    down_out[...] = jnp.dot(
        hidden_t[...], cot_ref[...], preferred_element_type=F32
    ).astype(BF16)


def finish(parts_ref, x_ref, cot_ref, gain_ref, input_out, gain_out):
    owners, own, total = parts_ref.shape
    width = x_ref.shape[1]
    fold = width // own
    gain = jnp.zeros((own, fold), F32)
    for p in range(owners):
        gain += parts_ref[p, :, width : width + fold].astype(F32)
        gain += parts_ref[p, :, width + fold : width + 2 * fold].astype(F32)
    for r in range(own):
        gain_out[:, r * fold : (r + 1) * fold] = gain[r : r + 1]
    delta = parts_ref[0, :, :width].astype(F32)
    for p in range(1, owners):
        delta += parts_ref[p, :, :width].astype(F32)
    inverse = row_inverse(x_ref, own, True, EPS_RMS)
    unit = x_ref[...].astype(F32) * inverse
    scaled = delta * gain_ref[...]
    mean = jnp.sum(scaled * unit, axis=1, keepdims=True) / width
    input_out[...] = (
        cot_ref[...].astype(F32) + inverse * (scaled - unit * mean)
    ).astype(BF16)


def shape(dims, dtype):
    return jax.ShapeDtypeStruct(dims, dtype)


def local(
    query_cache,
    passage_cache,
    hard_offsets,
    passage_lengths,
    segment_inputs,
    segment_cotangents,
    norm_gain,
    gate_weight,
    up_weight,
    down_weight,
):
    everyone = ("dp", "segment")
    count = lax.axis_size(everyone)
    owners = lax.axis_size("dp")
    sections = lax.axis_size("segment")
    rows, width = query_cache.shape
    pairs = rows * count
    cols = width // count
    passages = passage_lengths.shape[0]
    own = segment_inputs.shape[1]
    tokens = own * owners
    units = gate_weight.shape[2]
    section = lax.axis_index("segment")
    dp = lax.axis_index("dp")
    first_row = (lax.axis_index(everyone) * rows).astype(jnp.int32).reshape(1)
    is_last = (section == sections - 1).astype(jnp.int32).reshape(1)

    x_own, cot_own, gain = segment_inputs[0], segment_cotangents[0], norm_gain
    x_all = lax.all_gather(x_own, "dp", axis=0, tiled=True)
    cot_all = lax.all_gather(cot_own, "dp", axis=0, tiled=True)

    block1 = 4 * rows
    message = pl.pallas_call(
        pack_rows,
        out_shape=shape((count, block1, cols), BF16),
        in_specs=[vmem(), vmem()],
        out_specs=vmem(),
        compiler_params=params(16),
        name="pack_rows",
    )(query_cache, passage_cache)
    message = lax.all_to_all(message, everyone, 0, 0, tiled=True)
    parts, unit, inverse = pl.pallas_call(
        partial_scores,
        out_shape=(
            shape((count, rows, pairs), F32),
            shape((2, pairs, cols), F32),
            shape((2, pairs, 1), F32),
        ),
        in_specs=[vmem()],
        out_specs=(vmem(), vmem(), vmem()),
        compiler_params=params(32),
        name="partial_scores",
    )(message)
    parts = lax.all_to_all(parts, everyone, 0, 0, tiled=True)
    message = pl.pallas_call(
        softmax_rows,
        out_shape=shape((count, 2 * rows, pairs), BF16),
        in_specs=[smem(), vmem(), vmem()],
        out_specs=vmem(),
        compiler_params=params(32),
        name="softmax_rows",
    )(first_row, parts, hard_offsets)
    message = lax.all_to_all(message, everyone, 0, 0, tiled=True)
    back = -(-(2 * rows + passages) // 16) * 16
    message = pl.pallas_call(
        lambda *refs: pair_grads((sections - 1) * rows, passages, *refs),
        out_shape=shape((count, back, cols), BF16),
        in_specs=[vmem(), vmem(), vmem()],
        out_specs=vmem(),
        compiler_params=params(48),
        name="pair_grads",
    )(message, unit, inverse)
    message = lax.all_to_all(message, everyone, 0, 0, tiled=True)

    cuts = 8
    deep_cuts = units // 256 if units % 256 == 0 else 1
    fold = width // own
    outs = pl.pallas_call(
        lambda *refs: layer(cuts, deep_cuts, *refs),
        out_shape=(
            shape((rows, width), BF16),
            shape((rows, width), BF16),
            shape((owners, own, width + 2 * fold), BF16),
            shape((tokens, units), BF16),
            shape((tokens, units), BF16),
            shape((tokens, units), BF16),
            shape((tokens, width), BF16),
            shape((tokens, width), BF16),
        ),
        in_specs=[smem(), smem()] + [vmem()] * 4 + [anywhere()] * 3,
        out_specs=tuple(vmem() for _ in range(8)),
        scratch_shapes=[
            pltpu.VMEM((width, units), BF16),
            pltpu.VMEM((width, units), BF16),
            pltpu.VMEM((units, width), BF16),
            pltpu.VMEM((tokens, units), F32),
            pltpu.VMEM((tokens, units), F32),
            pltpu.VMEM((tokens, 1), F32),
            pltpu.VMEM((1, width), F32),
            pltpu.SemaphoreType.DMA((cuts,)),
            pltpu.SemaphoreType.DMA((cuts,)),
            pltpu.SemaphoreType.DMA((deep_cuts,)),
        ],
        compiler_params=params(60),
        cost_estimate=pl.CostEstimate(
            flops=10 * tokens * width * units,
            bytes_accessed=6 * width * units,
            transcendentals=tokens * units,
        ),
        name="layer",
    )(
        is_last,
        passage_lengths,
        message,
        x_all,
        cot_all,
        gain,
        gate_weight[0],
        up_weight[0],
        down_weight[0],
    )
    query_grads, passage_grads, delta, hidden, d_up, d_gate, normed, cot = outs
    delta = lax.all_to_all(delta, "dp", 0, 0, tiled=True)

    step = 256
    whole = lambda shape_: pl.BlockSpec(shape_, lambda i: (0, 0))
    gate_grads, up_grads, down_grads = pl.pallas_call(
        weight_grads,
        grid=(width // step,),
        out_shape=(
            shape((width, units), BF16),
            shape((width, units), BF16),
            shape((units, width), BF16),
        ),
        in_specs=[
            pl.BlockSpec((tokens, step), lambda i: (0, i)),
            whole((tokens, units)),
            whole((tokens, units)),
            whole((tokens, units)),
            pl.BlockSpec((tokens, step), lambda i: (0, i)),
        ],
        out_specs=(
            pl.BlockSpec((step, units), lambda i: (i, 0)),
            pl.BlockSpec((step, units), lambda i: (i, 0)),
            pl.BlockSpec((units, step), lambda i: (0, i)),
        ),
        scratch_shapes=[pltpu.VMEM((units, tokens), BF16)],
        compiler_params=params(40),
        cost_estimate=pl.CostEstimate(
            flops=6 * tokens * width * units,
            bytes_accessed=6 * width * units,
            transcendentals=0,
        ),
        name="weight_grads",
    )(normed, d_gate, d_up, hidden, cot)

    cot_rows = lax.dynamic_slice_in_dim(cot, dp * own, own, axis=0)
    input_grads, gain_grads = pl.pallas_call(
        finish,
        out_shape=(shape((own, width), BF16), shape((1, width), F32)),
        in_specs=[vmem()] * 4,
        out_specs=(vmem(), vmem()),
        compiler_params=params(32),
        name="finish",
    )(delta, x_own, cot_rows, gain)
    return (
        query_grads,
        passage_grads,
        input_grads[None],
        gate_grads[None],
        up_grads[None],
        down_grads[None],
        gain_grads,
    )


def solution(mesh):
    pair = P(("dp", "segment"), None)
    token = P("segment", "dp", None)
    wide = P("segment", None, "dp")
    return jax.shard_map(
        local,
        mesh=mesh,
        in_specs=(pair, pair, pair, P(), token, token, P("segment", None), wide, wide, token),
        out_specs=(pair, pair, token, wide, wide, token, P("segment", None)),
        check_vma=False,
    )
```

```python
import jax
import jax.numpy as jnp
from jax import lax
from jax.experimental import pallas as pl
from jax.experimental.pallas import tpu as pltpu
from jax.sharding import PartitionSpec as P

HN_BLOCK = 128
TAU = 0.02
HN_WEIGHT = 64.0
EPS_NORM = 1e-06
EPS_RMS = 1e-05

F32 = jnp.float32
BF16 = jnp.bfloat16
MIB = 2**20
WINDOW = 3
BIG = 62
NT = (((1,), (1,)), ((), ()))
TN = (((0,), (0,)), ((), ()))


def vmem():
    return pl.BlockSpec(memory_space=pltpu.VMEM)


def smem():
    return pl.BlockSpec(memory_space=pltpu.SMEM)


def anywhere():
    return pl.BlockSpec(memory_space=pl.ANY)


def params(mib):
    return pltpu.CompilerParams(vmem_limit_bytes=mib * MIB)


def iota(shape, axis):
    return lax.broadcasted_iota(jnp.int32, shape, axis)


def split3(value):
    high = value.astype(BF16).astype(F32)
    rest = value - high
    middle = rest.astype(BF16).astype(F32)
    return high, middle, (rest - middle).astype(BF16).astype(F32)


def to_row(column, width):
    n = column.shape[0]
    pick = iota((n, width), 0) == iota((n, width), 1)
    return jnp.sum(jnp.where(pick, column, 0.0), axis=0, keepdims=True)


def to_columns(rows, n):
    shape = rows.shape[:-2] + (n, rows.shape[-1])
    pick = iota(shape, len(shape) - 2) == iota(shape, len(shape) - 1)
    return jnp.sum(jnp.where(pick, rows, 0.0), axis=-1, keepdims=True)


def row_inverse(ref, rows, mean, eps):
    total = jnp.zeros((rows, 1), F32)
    width = ref.shape[1]
    step = min(width, 1024)
    for at in range(0, width, step):
        part = ref[:, at : at + step].astype(F32)
        total += jnp.sum(part * part, axis=1, keepdims=True)
    if mean:
        total = total / width
    return lax.rsqrt(total + eps)


def pack_rows(query_ref, passage_ref, out_ref):
    count, block, cols = out_ref.shape
    rows = query_ref.shape[0]
    inverse = jnp.concatenate(
        [
            row_inverse(query_ref, rows, False, EPS_NORM),
            row_inverse(passage_ref, rows, False, EPS_NORM),
        ],
        axis=0,
    )
    terms = [to_row(term, cols) for term in split3(inverse)]
    extra = jnp.concatenate(
        terms + [jnp.zeros((block - 2 * rows - 3, cols), F32)], axis=0
    )
    for peer in range(count):
        cut = slice(peer * cols, (peer + 1) * cols)
        both = jnp.concatenate(
            [
                query_ref[:, cut].astype(F32),
                passage_ref[:, cut].astype(F32),
                extra,
            ],
            axis=0,
        )
        out_ref[peer] = both.astype(BF16)


def partial_scores(rows_ref, out_ref, unit_ref, inverse_ref):
    count, block, cols = rows_ref.shape
    rows = out_ref.shape[1]
    pairs = count * rows
    values = rows_ref[...].astype(F32)
    lines = values[:, 2 * rows : 2 * rows + 1]
    lines = lines + values[:, 2 * rows + 1 : 2 * rows + 2]
    lines = lines + values[:, 2 * rows + 2 : 2 * rows + 3]
    inverse = to_columns(lines, 2 * rows)
    unit = values[:, : 2 * rows] * inverse
    query_unit = unit[:, :rows].reshape(pairs, cols)
    passage_unit = unit[:, rows:].reshape(pairs, cols)
    unit_ref[0] = query_unit
    unit_ref[1] = passage_unit
    inverse_ref[0] = inverse[:, :rows].reshape(pairs, 1)
    inverse_ref[1] = inverse[:, rows:].reshape(pairs, 1)
    scores = lax.dot_general(
        query_unit.astype(BF16), passage_unit.astype(BF16), NT, preferred_element_type=F32
    )
    out_ref[...] = scores.reshape(out_ref.shape)


def softmax_rows(first_ref, parts_ref, offsets_ref, out_ref):
    count, block, pairs = out_ref.shape
    rows = parts_ref.shape[1]
    scores = jnp.sum(parts_ref[...], axis=0) / TAU
    row = first_ref[0] + iota((rows, pairs), 0)
    column = iota((rows, pairs), 1)
    base = row // HN_BLOCK * HN_BLOCK
    tallies = jnp.zeros((rows, pairs), F32)
    for k in range(offsets_ref.shape[1]):
        tallies += (base + offsets_ref[:, k : k + 1] == column).astype(F32)
    weighted = (1.0 + HN_WEIGHT * tallies) * jnp.exp(scores)
    totals = jnp.sum(weighted, axis=1, keepdims=True)
    dscore = weighted / totals - (row == column).astype(F32)
    dscore = dscore.astype(BF16).astype(F32)
    product = dscore * scores
    lines = list(split3(jnp.sum(product, axis=0, keepdims=True)))
    lines += [
        to_row(term, pairs) for term in split3(jnp.sum(product, axis=1, keepdims=True))
    ]
    lines.append(jnp.zeros((block - rows - 6, pairs), F32))
    message = jnp.concatenate([dscore] + lines, axis=0).astype(BF16)
    for peer in range(count):
        out_ref[peer] = message


def pair_grads(first, take, rows_ref, unit_ref, inverse_ref, out_ref):
    count, block, pairs = rows_ref.shape
    rows = pairs // count
    cols = unit_ref.shape[2]
    values = rows_ref[...].astype(F32)
    dscore = values[:, :rows].reshape(pairs, pairs).astype(BF16)
    column_line = jnp.sum(
        values[:, rows] + values[:, rows + 1] + values[:, rows + 2], axis=0, keepdims=True
    )
    column_dots = to_columns(column_line, pairs)
    row_lines = (
        values[:, rows + 3 : rows + 4]
        + values[:, rows + 4 : rows + 5]
        + values[:, rows + 5 : rows + 6]
    )
    row_dots = to_columns(row_lines, rows).reshape(pairs, 1)
    query_unit, passage_unit = unit_ref[0], unit_ref[1]
    query_dir = (
        jnp.dot(dscore, passage_unit.astype(BF16), preferred_element_type=F32) / TAU
    )
    passage_dir = (
        lax.dot_general(dscore, query_unit.astype(BF16), TN, preferred_element_type=F32) / TAU
    )
    query_grad = inverse_ref[0] * (query_dir - query_unit * row_dots)
    passage_grad = inverse_ref[1] * (passage_dir - passage_unit * column_dots)
    pieces = [
        query_grad.reshape(count, rows, cols),
        passage_grad.reshape(count, rows, cols),
    ]
    picked = passage_grad[first : first + take]
    spare = out_ref.shape[1] - 2 * rows - take
    if spare:
        picked = jnp.concatenate([picked, jnp.zeros((spare, cols), F32)], axis=0)
    pieces.append(jnp.broadcast_to(picked[None], (count,) + picked.shape))
    out_ref[...] = jnp.concatenate(pieces, axis=1).astype(BF16)


def forward(tokens_ref, gain_ref, gate_ref, up_ref, normed_out, gate_out, up_out):
    @pl.when(pl.program_id(0) == 0)
    def _():
        tokens, width = normed_out.shape
        x = tokens_ref[...].reshape(tokens, width).astype(F32)
        inverse = lax.rsqrt(jnp.sum(x * x, axis=1, keepdims=True) / width + EPS_RMS)
        normed_out[...] = (x * inverse * gain_ref[...]).astype(BF16)

    gate_out[...] = jnp.dot(normed_out[...], gate_ref[...], preferred_element_type=F32)
    up_out[...] = jnp.dot(normed_out[...], up_ref[...], preferred_element_type=F32)


def backward(
    cuts,
    deep_cuts,
    place_ref,
    lengths_ref,
    back_ref,
    both_ref,
    gate_ref,
    up_ref,
    gate_hbm,
    up_hbm,
    down_hbm,
    query_out,
    passage_out,
    delta_out,
    hidden_out,
    d_up_out,
    d_gate_out,
    cot_out,
    gate_w,
    up_w,
    down_w,
    gain_s,
    x_s,
    inverse_s,
    d_gate_t,
    d_up_t,
    gate_sem,
    up_sem,
    down_sem,
):
    tokens, width = cot_out.shape
    units = gate_ref.shape[1]
    owners, own, _ = delta_out.shape
    deep = units // deep_cuts
    step = width // cuts

    def down_copy(c):
        slot = lax.rem(c, WINDOW)
        return pltpu.make_async_copy(
            down_hbm.at[pl.ds(c * deep, deep)], down_w.at[slot], down_sem.at[slot]
        )

    def wide_copies(c):
        slot = lax.rem(c, WINDOW)
        part = pl.ds(c * step, step)
        return (
            pltpu.make_async_copy(gate_hbm.at[part], gate_w.at[slot], gate_sem.at[slot]),
            pltpu.make_async_copy(up_hbm.at[part], up_w.at[slot], up_sem.at[slot]),
        )

    def start_wide(c):
        for copy in wide_copies(c):
            copy.start()

    for c in range(min(WINDOW, deep_cuts)):
        down_copy(c).start()
    for c in range(WINDOW - deep_cuts):
        start_wide(c)

    count, block, cols = back_ref.shape
    rows = query_out.shape[0]
    passages = block - 2 * rows
    token = iota((tokens, 1), 0)
    lane = iota((tokens, passages), 1)
    start = jnp.int32(0)
    member = jnp.zeros((tokens, passages), F32)
    scale = jnp.zeros((tokens, 1), F32)
    for m in range(lengths_ref.shape[0]):
        length = lengths_ref[m]
        inside = jnp.logical_and(token >= start, token < start + length)
        member = jnp.where(jnp.logical_and(inside, lane == m), 1.0, member)
        scale = jnp.where(inside, 1.0 / (jnp.zeros((tokens, 1), F32) + length.astype(F32)), scale)
        start = start + length
    member = member.astype(BF16)
    last = place_ref[0] == 1
    for peer in range(count):
        cut = slice(peer * cols, (peer + 1) * cols)
        piece = back_ref[peer].astype(F32)
        query_out[:, cut] = piece[:rows].astype(BF16)
        passage_out[:, cut] = piece[rows : 2 * rows].astype(BF16)
        spread = jnp.dot(member, piece[2 * rows :].astype(BF16), preferred_element_type=F32)
        pooled = (spread * scale).astype(BF16)
        given = both_ref[:, 1, :, cut].reshape(tokens, cols)
        cot_out[:, cut] = jnp.where(last, pooled, given)

    def down_step(c, carry):
        down_copy(c).wait()
        cut = pl.ds(pl.multiple_of(c * deep, deep), deep)
        d_hidden = lax.dot_general(cot_out[...], down_w[lax.rem(c, WINDOW)], NT, preferred_element_type=F32)
        gate, up = gate_ref[:, cut], up_ref[:, cut]
        sigmoid = jax.nn.sigmoid(gate)
        active = gate * sigmoid
        hidden_out[:, cut] = (active * up).astype(BF16)
        d_up_out[:, cut] = (d_hidden * active).astype(BF16)
        d_gate_out[:, cut] = (
            d_hidden * up * sigmoid * (1.0 + gate * (1.0 - sigmoid))
        ).astype(BF16)
        ahead = c + WINDOW

        @pl.when(ahead < deep_cuts)
        def _():
            down_copy(ahead).start()

        @pl.when(jnp.logical_and(ahead >= deep_cuts, ahead - deep_cuts < cuts))
        def _():
            start_wide(ahead - deep_cuts)

        return carry

    lax.fori_loop(0, deep_cuts, down_step, 0)

    x = both_ref[:, 0].reshape(tokens, width).astype(F32)
    x_s[...] = x
    inverse_s[...] = lax.rsqrt(jnp.sum(x * x, axis=1, keepdims=True) / width + EPS_RMS)
    d_gate_t[...] = d_gate_out[...].T
    d_up_t[...] = d_up_out[...].T

    def wide_step(c, carry):
        for copy in wide_copies(c):
            copy.wait()
        cut = pl.ds(pl.multiple_of(c * step, step), step)
        delta = (
            jnp.dot(gate_w[lax.rem(c, WINDOW)], d_gate_t[...], preferred_element_type=F32)
            + jnp.dot(up_w[lax.rem(c, WINDOW)], d_up_t[...], preferred_element_type=F32)
        ).T
        delta_out[:, :, cut] = delta.astype(BF16).reshape(owners, own, step)
        gain_s[:, cut] = jnp.sum(
            delta * (x_s[:, cut] * inverse_s[...]), axis=0, keepdims=True
        )

        @pl.when(c + WINDOW < cuts)
        def _():
            start_wide(c + WINDOW)

        return carry

    lax.fori_loop(0, cuts, wide_step, 0)

    fold = width // own
    gain = jnp.concatenate(
        [gain_s[:, r * fold : (r + 1) * fold] for r in range(own)], axis=0
    )
    high, low, _ = split3(gain)
    tail = jnp.concatenate([high, low], axis=1).astype(BF16)
    for owner in range(owners):
        delta_out[owner, :, width:] = tail


def weight_grads(
    normed_ref, d_gate_ref, d_up_ref, hidden_ref, cot_ref, gate_out, up_out, down_out, hidden_t
):
    @pl.when(pl.program_id(0) == 0)
    def _():
        hidden_t[...] = hidden_ref[...].T

    gate_out[...] = lax.dot_general(
        normed_ref[...], d_gate_ref[...], TN, preferred_element_type=F32
    ).astype(BF16)
    up_out[...] = lax.dot_general(
        normed_ref[...], d_up_ref[...], TN, preferred_element_type=F32
    ).astype(BF16)
    down_out[...] = jnp.dot(
        hidden_t[...], cot_ref[...], preferred_element_type=F32
    ).astype(BF16)


def finish(parts_ref, x_ref, cot_ref, gain_ref, input_out, gain_out):
    owners, own, total = parts_ref.shape
    width = x_ref.shape[1]
    fold = width // own
    gain = jnp.zeros((own, fold), F32)
    for p in range(owners):
        gain += parts_ref[p, :, width : width + fold].astype(F32)
        gain += parts_ref[p, :, width + fold : width + 2 * fold].astype(F32)
    for r in range(own):
        gain_out[:, r * fold : (r + 1) * fold] = gain[r : r + 1]
    delta = parts_ref[0, :, :width].astype(F32)
    for p in range(1, owners):
        delta += parts_ref[p, :, :width].astype(F32)
    inverse = row_inverse(x_ref, own, True, EPS_RMS)
    unit = x_ref[...].astype(F32) * inverse
    scaled = delta * gain_ref[...]
    mean = jnp.sum(scaled * unit, axis=1, keepdims=True) / width
    input_out[...] = (
        cot_ref[...].astype(F32) + inverse * (scaled - unit * mean)
    ).astype(BF16)


def shape(dims, dtype):
    return jax.ShapeDtypeStruct(dims, dtype)


def local(
    query_cache,
    passage_cache,
    hard_offsets,
    passage_lengths,
    segment_inputs,
    segment_cotangents,
    norm_gain,
    gate_weight,
    up_weight,
    down_weight,
):
    everyone = ("dp", "segment")
    count = lax.axis_size(everyone)
    owners = lax.axis_size("dp")
    sections = lax.axis_size("segment")
    rows, width = query_cache.shape
    pairs = rows * count
    cols = width // count
    passages = passage_lengths.shape[0]
    own = segment_inputs.shape[1]
    tokens = own * owners
    units = gate_weight.shape[2]
    section = lax.axis_index("segment")
    dp = lax.axis_index("dp")
    first_row = (lax.axis_index(everyone) * rows).astype(jnp.int32).reshape(1)
    is_last = (section == sections - 1).astype(jnp.int32).reshape(1)

    x_own, cot_own, gain = segment_inputs[0], segment_cotangents[0], norm_gain
    both = lax.all_gather(jnp.stack([x_own, cot_own]), "dp", axis=0, tiled=False)

    block1 = 4 * rows
    message = pl.pallas_call(
        pack_rows,
        out_shape=shape((count, block1, cols), BF16),
        in_specs=[vmem(), vmem()],
        out_specs=vmem(),
        compiler_params=params(16),
        name="pack_rows",
    )(query_cache, passage_cache)
    message = lax.all_to_all(message, everyone, 0, 0, tiled=True)
    parts, unit, inverse = pl.pallas_call(
        partial_scores,
        out_shape=(
            shape((count, rows, pairs), F32),
            shape((2, pairs, cols), F32),
            shape((2, pairs, 1), F32),
        ),
        in_specs=[vmem()],
        out_specs=(vmem(), vmem(), vmem()),
        compiler_params=params(32),
        name="partial_scores",
    )(message)
    parts = lax.all_to_all(parts, everyone, 0, 0, tiled=True)
    message = pl.pallas_call(
        softmax_rows,
        out_shape=shape((count, 2 * rows, pairs), BF16),
        in_specs=[smem(), vmem(), vmem()],
        out_specs=vmem(),
        compiler_params=params(32),
        name="softmax_rows",
    )(first_row, parts, hard_offsets)
    message = lax.all_to_all(message, everyone, 0, 0, tiled=True)
    back = -(-(2 * rows + passages) // 16) * 16
    message = pl.pallas_call(
        lambda *refs: pair_grads((sections - 1) * rows, passages, *refs),
        out_shape=shape((count, back, cols), BF16),
        in_specs=[vmem(), vmem(), vmem()],
        out_specs=vmem(),
        compiler_params=params(48),
        name="pair_grads",
    )(message, unit, inverse)
    message = lax.all_to_all(message, everyone, 0, 0, tiled=True)

    whole = lambda dims: pl.BlockSpec(dims, lambda i: (0,) * len(dims))
    step = 256 if units % 256 == 0 else units
    weight = pl.BlockSpec((width, step), lambda i: (0, i))
    part = pl.BlockSpec((tokens, step), lambda i: (0, i))
    normed, gate, up = pl.pallas_call(
        forward,
        grid=(units // step,),
        out_shape=(
            shape((tokens, width), BF16),
            shape((tokens, units), F32),
            shape((tokens, units), F32),
        ),
        in_specs=[
            pl.BlockSpec((owners, None, own, width), lambda i: (0, 0, 0, 0)),
            whole((1, width)),
            weight,
            weight,
        ],
        out_specs=(whole((tokens, width)), part, part),
        compiler_params=params(BIG),
        cost_estimate=pl.CostEstimate(
            flops=4 * tokens * width * units,
            bytes_accessed=4 * width * units,
            transcendentals=0,
        ),
        name="forward",
    )(both, gain, gate_weight[0], up_weight[0])

    cuts = 8
    deep_cuts = units // 256 if units % 256 == 0 else 1
    fold = width // own
    outs = pl.pallas_call(
        lambda *refs: backward(cuts, deep_cuts, *refs),
        out_shape=(
            shape((rows, width), BF16),
            shape((rows, width), BF16),
            shape((owners, own, width + 2 * fold), BF16),
            shape((tokens, units), BF16),
            shape((tokens, units), BF16),
            shape((tokens, units), BF16),
            shape((tokens, width), BF16),
        ),
        in_specs=[smem(), smem()] + [vmem()] * 4 + [anywhere()] * 3,
        out_specs=tuple(vmem() for _ in range(7)),
        scratch_shapes=[
            pltpu.VMEM((WINDOW, width // cuts, units), BF16),
            pltpu.VMEM((WINDOW, width // cuts, units), BF16),
            pltpu.VMEM((WINDOW, units // deep_cuts, width), BF16),
            pltpu.VMEM((1, width), F32),
            pltpu.VMEM((tokens, width), F32),
            pltpu.VMEM((tokens, 1), F32),
            pltpu.VMEM((units, tokens), BF16),
            pltpu.VMEM((units, tokens), BF16),
            pltpu.SemaphoreType.DMA((WINDOW,)),
            pltpu.SemaphoreType.DMA((WINDOW,)),
            pltpu.SemaphoreType.DMA((WINDOW,)),
        ],
        compiler_params=params(BIG),
        cost_estimate=pl.CostEstimate(
            flops=6 * tokens * width * units,
            bytes_accessed=6 * width * units,
            transcendentals=tokens * units,
        ),
        name="backward",
    )(
        is_last,
        passage_lengths,
        message,
        both,
        gate,
        up,
        gate_weight[0],
        up_weight[0],
        down_weight[0],
    )
    query_grads, passage_grads, delta, hidden, d_up, d_gate, cot = outs
    delta = lax.all_to_all(delta, "dp", 0, 0, tiled=True)

    step = min(512, width)
    gate_grads, up_grads, down_grads = pl.pallas_call(
        weight_grads,
        grid=(width // step,),
        out_shape=(
            shape((width, units), BF16),
            shape((width, units), BF16),
            shape((units, width), BF16),
        ),
        in_specs=[
            pl.BlockSpec((tokens, step), lambda i: (0, i)),
            whole((tokens, units)),
            whole((tokens, units)),
            whole((tokens, units)),
            pl.BlockSpec((tokens, step), lambda i: (0, i)),
        ],
        out_specs=(
            pl.BlockSpec((step, units), lambda i: (i, 0)),
            pl.BlockSpec((step, units), lambda i: (i, 0)),
            pl.BlockSpec((units, step), lambda i: (0, i)),
        ),
        scratch_shapes=[pltpu.VMEM((units, tokens), BF16)],
        compiler_params=params(BIG),
        cost_estimate=pl.CostEstimate(
            flops=6 * tokens * width * units,
            bytes_accessed=6 * width * units,
            transcendentals=0,
        ),
        name="weight_grads",
    )(normed, d_gate, d_up, hidden, cot)

    cot_rows = lax.dynamic_slice_in_dim(cot, dp * own, own, axis=0)
    input_grads, gain_grads = pl.pallas_call(
        finish,
        out_shape=(shape((own, width), BF16), shape((1, width), F32)),
        in_specs=[vmem()] * 4,
        out_specs=(vmem(), vmem()),
        compiler_params=params(32),
        name="finish",
    )(delta, x_own, cot_rows, gain)
    return (
        query_grads,
        passage_grads,
        input_grads[None],
        gate_grads[None],
        up_grads[None],
        down_grads[None],
        gain_grads,
    )


def solution(mesh):
    pair = P(("dp", "segment"), None)
    token = P("segment", "dp", None)
    wide = P("segment", None, "dp")
    return jax.shard_map(
        local,
        mesh=mesh,
        in_specs=(pair, pair, pair, P(), token, token, P("segment", None), wide, wide, token),
        out_specs=(pair, pair, token, wide, wide, token, P("segment", None)),
        check_vma=False,
    )
```

```python
import jax
import jax.numpy as jnp
from jax import lax
from jax.experimental import pallas as pl
from jax.experimental.pallas import tpu as pltpu
from jax.sharding import PartitionSpec as P

HN_BLOCK = 128
TAU = 0.02
HN_WEIGHT = 64.0
EPS_NORM = 1e-06
EPS_RMS = 1e-05

F32 = jnp.float32
BF16 = jnp.bfloat16
MIB = 2**20
WINDOW = 3
BIG = 62
NT = (((1,), (1,)), ((), ()))
TN = (((0,), (0,)), ((), ()))


def vmem():
    return pl.BlockSpec(memory_space=pltpu.VMEM)


def smem():
    return pl.BlockSpec(memory_space=pltpu.SMEM)


def anywhere():
    return pl.BlockSpec(memory_space=pl.ANY)


def params(mib):
    return pltpu.CompilerParams(vmem_limit_bytes=mib * MIB)


def iota(shape, axis):
    return lax.broadcasted_iota(jnp.int32, shape, axis)


def split3(value):
    high = value.astype(BF16).astype(F32)
    rest = value - high
    middle = rest.astype(BF16).astype(F32)
    return high, middle, (rest - middle).astype(BF16).astype(F32)


def to_row(column, width):
    n = column.shape[0]
    pick = iota((n, width), 0) == iota((n, width), 1)
    return jnp.sum(jnp.where(pick, column, 0.0), axis=0, keepdims=True)


def to_columns(rows, n):
    shape = rows.shape[:-2] + (n, rows.shape[-1])
    pick = iota(shape, len(shape) - 2) == iota(shape, len(shape) - 1)
    return jnp.sum(jnp.where(pick, rows, 0.0), axis=-1, keepdims=True)


def row_inverse(ref, rows, mean, eps):
    total = jnp.zeros((rows, 1), F32)
    width = ref.shape[1]
    step = min(width, 1024)
    for at in range(0, width, step):
        part = ref[:, at : at + step].astype(F32)
        total += jnp.sum(part * part, axis=1, keepdims=True)
    if mean:
        total = total / width
    return lax.rsqrt(total + eps)


def pack_rows(
    query_hbm, passage_hbm, x_hbm, cot_hbm, out_ref, both_ref, query_ref, passage_ref, sems
):
    count, block, cols = out_ref.shape
    rows = query_ref.shape[0]
    copies = [
        pltpu.make_async_copy(query_hbm, query_ref, sems.at[0]),
        pltpu.make_async_copy(passage_hbm, passage_ref, sems.at[1]),
        pltpu.make_async_copy(x_hbm, both_ref.at[0], sems.at[2]),
        pltpu.make_async_copy(cot_hbm, both_ref.at[1], sems.at[3]),
    ]
    for copy in copies:
        copy.start()
    copies[0].wait()
    copies[1].wait()
    inverse = jnp.concatenate(
        [
            row_inverse(query_ref, rows, False, EPS_NORM),
            row_inverse(passage_ref, rows, False, EPS_NORM),
        ],
        axis=0,
    )
    terms = [to_row(term, cols) for term in split3(inverse)]
    extra = jnp.concatenate(
        terms + [jnp.zeros((block - 2 * rows - 3, cols), F32)], axis=0
    )
    for peer in range(count):
        cut = slice(peer * cols, (peer + 1) * cols)
        both = jnp.concatenate(
            [
                query_ref[:, cut].astype(F32),
                passage_ref[:, cut].astype(F32),
                extra,
            ],
            axis=0,
        )
        out_ref[peer] = both.astype(BF16)
    copies[2].wait()
    copies[3].wait()


def partial_scores(rows_ref, out_ref, unit_ref, inverse_ref):
    count, block, cols = rows_ref.shape
    rows = out_ref.shape[1]
    pairs = count * rows
    values = rows_ref[...].astype(F32)
    lines = values[:, 2 * rows : 2 * rows + 1]
    lines = lines + values[:, 2 * rows + 1 : 2 * rows + 2]
    lines = lines + values[:, 2 * rows + 2 : 2 * rows + 3]
    inverse = to_columns(lines, 2 * rows)
    unit = values[:, : 2 * rows] * inverse
    query_unit = unit[:, :rows].reshape(pairs, cols)
    passage_unit = unit[:, rows:].reshape(pairs, cols)
    unit_ref[0] = query_unit
    unit_ref[1] = passage_unit
    inverse_ref[0] = inverse[:, :rows].reshape(pairs, 1)
    inverse_ref[1] = inverse[:, rows:].reshape(pairs, 1)
    scores = lax.dot_general(
        query_unit.astype(BF16), passage_unit.astype(BF16), NT, preferred_element_type=F32
    )
    out_ref[...] = scores.reshape(out_ref.shape)


def softmax_rows(first_ref, parts_ref, offsets_ref, out_ref):
    count, block, pairs = out_ref.shape
    rows = parts_ref.shape[1]
    scores = jnp.sum(parts_ref[...], axis=0) / TAU
    row = first_ref[0] + iota((rows, pairs), 0)
    column = iota((rows, pairs), 1)
    base = row // HN_BLOCK * HN_BLOCK
    offsets = to_columns(offsets_ref[...].astype(F32)[:, None, :], rows).astype(jnp.int32)
    tallies = jnp.zeros((rows, pairs), F32)
    for k in range(offsets_ref.shape[0]):
        tallies += (base + offsets[k] == column).astype(F32)
    weighted = (1.0 + HN_WEIGHT * tallies) * jnp.exp(scores)
    totals = jnp.sum(weighted, axis=1, keepdims=True)
    dscore = weighted / totals - (row == column).astype(F32)
    dscore = dscore.astype(BF16).astype(F32)
    product = dscore * scores
    lines = list(split3(jnp.sum(product, axis=0, keepdims=True)))
    lines += [
        to_row(term, pairs) for term in split3(jnp.sum(product, axis=1, keepdims=True))
    ]
    lines.append(jnp.zeros((block - rows - 6, pairs), F32))
    message = jnp.concatenate([dscore] + lines, axis=0).astype(BF16)
    for peer in range(count):
        out_ref[peer] = message


def pair_grads(first, take, rows_ref, unit_ref, inverse_ref, out_ref):
    count, block, pairs = rows_ref.shape
    rows = pairs // count
    cols = unit_ref.shape[2]
    values = rows_ref[...].astype(F32)
    dscore = values[:, :rows].reshape(pairs, pairs).astype(BF16)
    column_line = jnp.sum(
        values[:, rows] + values[:, rows + 1] + values[:, rows + 2], axis=0, keepdims=True
    )
    column_dots = to_columns(column_line, pairs)
    row_lines = (
        values[:, rows + 3 : rows + 4]
        + values[:, rows + 4 : rows + 5]
        + values[:, rows + 5 : rows + 6]
    )
    row_dots = to_columns(row_lines, rows).reshape(pairs, 1)
    query_unit, passage_unit = unit_ref[0], unit_ref[1]
    query_dir = (
        jnp.dot(dscore, passage_unit.astype(BF16), preferred_element_type=F32) / TAU
    )
    passage_dir = (
        lax.dot_general(dscore, query_unit.astype(BF16), TN, preferred_element_type=F32) / TAU
    )
    query_grad = inverse_ref[0] * (query_dir - query_unit * row_dots)
    passage_grad = inverse_ref[1] * (passage_dir - passage_unit * column_dots)
    pieces = [
        query_grad.reshape(count, rows, cols),
        passage_grad.reshape(count, rows, cols),
    ]
    picked = passage_grad[first : first + take]
    spare = out_ref.shape[1] - 2 * rows - take
    if spare:
        picked = jnp.concatenate([picked, jnp.zeros((spare, cols), F32)], axis=0)
    pieces.append(jnp.broadcast_to(picked[None], (count,) + picked.shape))
    out_ref[...] = jnp.concatenate(pieces, axis=1).astype(BF16)


class Ring:
    def __init__(self, hbm, slots, sems, step):
        self.hbm, self.slots, self.sems, self.step = hbm, slots, sems, step

    def copy(self, c):
        slot = lax.rem(c, WINDOW)
        part = pl.ds(c * self.step, self.step)
        return pltpu.make_async_copy(self.hbm.at[part], self.slots.at[slot], self.sems.at[slot])


def forward(
    both_hbm,
    gain_ref,
    gate_hbm,
    up_hbm,
    normed_out,
    gate_out,
    up_out,
    x_s,
    gate_w,
    up_w,
    x_sem,
    gate_sem,
    up_sem,
):
    tokens, width = normed_out.shape
    step = gate_w.shape[1]
    blocks = width // step
    gate_ring = Ring(gate_hbm, gate_w, gate_sem, step)
    up_ring = Ring(up_hbm, up_w, up_sem, step)
    fetch = pltpu.make_async_copy(both_hbm.at[:, 0], x_s, x_sem.at[0])
    fetch.start()
    for c in range(min(WINDOW, blocks)):
        gate_ring.copy(c).start()
        up_ring.copy(c).start()
    fetch.wait()
    x = x_s[...].reshape(tokens, width).astype(F32)
    inverse = lax.rsqrt(jnp.sum(x * x, axis=1, keepdims=True) / width + EPS_RMS)
    normed_out[...] = (x * inverse * gain_ref[...]).astype(BF16)

    def block(c, first):
        slot = lax.rem(c, WINDOW)
        cut = pl.ds(pl.multiple_of(c * step, step), step)
        normed = normed_out[:, cut]
        gate_ring.copy(c).wait()
        gate = jnp.dot(normed, gate_w[slot], preferred_element_type=F32)
        gate_out[...] = gate if first else gate_out[...] + gate
        up_ring.copy(c).wait()
        up = jnp.dot(normed, up_w[slot], preferred_element_type=F32)
        up_out[...] = up if first else up_out[...] + up

        @pl.when(c + WINDOW < blocks)
        def _():
            gate_ring.copy(c + WINDOW).start()
            up_ring.copy(c + WINDOW).start()

    def more(c, carry):
        block(c, False)
        return carry

    block(jnp.int32(0), True)
    lax.fori_loop(1, blocks, more, 0)


def partner(mine, k, n):
    if n & (n - 1) == 0:
        return mine ^ k
    return (k + n - mine) % n


def delta_columns(mine, cuts, rings, started, both_ref, d_gate_t, d_up_t, outs, delta_s, gain_s, inverse_s):
    owners = len(outs)
    own, total = outs[0].shape
    width = gain_s.shape[1]
    tokens = owners * own
    gate_ring, up_ring = rings
    step = gate_ring.step
    for c in range(started, min(WINDOW, cuts)):
        gate_ring.copy(c).start()
        up_ring.copy(c).start()
    x = both_ref[:, 0].reshape(tokens, width).astype(F32)
    inverse_s[...] = lax.rsqrt(jnp.sum(x * x, axis=1, keepdims=True) / width + EPS_RMS)

    def one(c, carry):
        slot = lax.rem(c, WINDOW)
        gate_ring.copy(c).wait()
        up_ring.copy(c).wait()
        cut = pl.ds(pl.multiple_of(c * step, step), step)
        delta = (
            jnp.dot(gate_ring.slots[slot], d_gate_t[...], preferred_element_type=F32)
            + jnp.dot(up_ring.slots[slot], d_up_t[...], preferred_element_type=F32)
        ).T
        low = delta.astype(BF16)
        for owner in range(owners):
            delta_s[partner(mine, owner, owners), :, cut] = low[owner * own : (owner + 1) * own]
        unit = both_ref[:, 0, :, cut].reshape(tokens, step).astype(F32) * inverse_s[...]
        gain_s[:, cut] = jnp.sum(delta * unit, axis=0, keepdims=True)

        @pl.when(c + WINDOW < cuts)
        def _():
            gate_ring.copy(c + WINDOW).start()
            up_ring.copy(c + WINDOW).start()

        return carry

    lax.fori_loop(0, cuts, one, 0)
    fold = width // own
    gain = jnp.concatenate(
        [gain_s[:, r * fold : (r + 1) * fold] for r in range(own)], axis=0
    )
    high, low, _ = split3(gain)
    tail = jnp.concatenate([high, low], axis=1).astype(BF16)
    for k in range(owners):
        outs[k][:, :width] = delta_s[k]
        outs[k][:, width:] = tail


def backward(
    cuts,
    deep_cuts,
    last_ref,
    mine_ref,
    lengths_ref,
    back_ref,
    both_ref,
    gate_ref,
    up_ref,
    gate_hbm,
    up_hbm,
    down_hbm,
    query_out,
    passage_out,
    hidden_out,
    d_up_out,
    d_gate_out,
    cot_out,
    cot_own_out,
    *more,
):
    *delta_outs, gate_w, up_w, down_w, d_up_t, d_gate_t, delta_s, gain_s, inverse_s = more[:-3]
    gate_sem, up_sem, down_sem = more[-3:]
    tokens, width = cot_out.shape
    units = gate_ref.shape[1]
    own = delta_outs[0].shape[0]
    deep = units // deep_cuts
    step = gain_s.shape[1] // cuts
    down_ring = Ring(down_hbm, down_w, down_sem, deep)
    gate_ring = Ring(gate_hbm, gate_w, gate_sem, step)
    up_ring = Ring(up_hbm, up_w, up_sem, step)
    early = min(WINDOW, deep_cuts, cuts)
    for c in range(min(WINDOW, deep_cuts)):
        down_ring.copy(c).start()

    count, block, cols = back_ref.shape
    rows = query_out.shape[0]
    passages = block - 2 * rows
    token = iota((tokens, 1), 0)
    lane = iota((tokens, passages), 1)
    start = jnp.int32(0)
    member = jnp.zeros((tokens, passages), F32)
    scale = jnp.zeros((tokens, 1), F32)
    for m in range(lengths_ref.shape[0]):
        length = lengths_ref[m]
        inside = jnp.logical_and(token >= start, token < start + length)
        member = jnp.where(jnp.logical_and(inside, lane == m), 1.0, member)
        scale = jnp.where(inside, 1.0 / (jnp.zeros((tokens, 1), F32) + length.astype(F32)), scale)
        start = start + length
    member = member.astype(BF16)
    last = last_ref[0] == 1
    for peer in range(count):
        cut = slice(peer * cols, (peer + 1) * cols)
        piece = back_ref[peer].astype(F32)
        query_out[:, cut] = piece[:rows].astype(BF16)
        passage_out[:, cut] = piece[rows : 2 * rows].astype(BF16)
        spread = jnp.dot(member, piece[2 * rows :].astype(BF16), preferred_element_type=F32)
        pooled = (spread * scale).astype(BF16)
        given = both_ref[:, 1, :, cut].reshape(tokens, cols)
        cot_out[:, cut] = jnp.where(last, pooled, given)

    cot_own_out[...] = cot_out[pl.ds(pl.multiple_of(mine_ref[0] * own, own), own), :]

    def down_step(c, carry):
        slot = lax.rem(c, WINDOW)
        down_ring.copy(c).wait()
        cut = pl.ds(pl.multiple_of(c * deep, deep), deep)
        d_hidden = lax.dot_general(cot_out[...], down_w[slot], NT, preferred_element_type=F32)
        gate, up = gate_ref[:, cut], up_ref[:, cut]
        sigmoid = jax.nn.sigmoid(gate)
        active = gate * sigmoid
        hidden_out[:, cut] = (active * up).astype(BF16)
        d_up = (d_hidden * active).astype(BF16)
        d_gate = (d_hidden * up * sigmoid * (1.0 + gate * (1.0 - sigmoid))).astype(BF16)
        d_up_out[:, cut] = d_up
        d_gate_out[:, cut] = d_gate
        d_up_t[cut, :] = d_up.T
        d_gate_t[cut, :] = d_gate.T
        ahead = c + WINDOW

        @pl.when(ahead < deep_cuts)
        def _():
            down_ring.copy(ahead).start()

        @pl.when(jnp.logical_and(ahead >= deep_cuts, ahead - deep_cuts < early))
        def _():
            gate_ring.copy(ahead - deep_cuts).start()
            up_ring.copy(ahead - deep_cuts).start()

        return carry

    lax.fori_loop(0, deep_cuts, down_step, 0)
    delta_columns(
        mine_ref[0],
        cuts,
        (gate_ring, up_ring),
        early,
        both_ref,
        d_gate_t,
        d_up_t,
        delta_outs,
        delta_s,
        gain_s,
        inverse_s,
    )


def weight_grads(
    normed_ref, d_gate_ref, d_up_ref, hidden_ref, cot_ref, gate_out, up_out, down_out, hidden_t
):
    @pl.when(pl.program_id(0) == 0)
    def _():
        hidden_t[...] = hidden_ref[...].T

    gate_out[...] = lax.dot_general(
        normed_ref[...], d_gate_ref[...], TN, preferred_element_type=F32
    ).astype(BF16)
    up_out[...] = lax.dot_general(
        normed_ref[...], d_up_ref[...], TN, preferred_element_type=F32
    ).astype(BF16)
    down_out[...] = jnp.dot(
        hidden_t[...], cot_ref[...], preferred_element_type=F32
    ).astype(BF16)


def finish(mine_ref, *refs):
    *part_refs, x_ref, cot_ref, gain_ref, input_out, gain_out, tail_s = refs
    owners = len(part_refs)
    own, width = x_ref.shape
    fold = width // own
    for k in range(owners):
        tail = part_refs[k][:, width:].astype(F32)
        tail_s[partner(mine_ref[0], k, owners)] = tail[:, :fold] + tail[:, fold:]
    gain = tail_s[0]
    for p in range(1, owners):
        gain += tail_s[p]
    for r in range(own):
        gain_out[:, r * fold : (r + 1) * fold] = gain[r : r + 1]
    delta = part_refs[0][:, :width].astype(F32)
    for k in range(1, owners):
        delta += part_refs[k][:, :width].astype(F32)
    inverse = row_inverse(x_ref, own, True, EPS_RMS)
    unit = x_ref[...].astype(F32) * inverse
    scaled = delta * gain_ref[...]
    mean = jnp.sum(scaled * unit, axis=1, keepdims=True) / width
    input_out[...] = (
        cot_ref[...].astype(F32) + inverse * (scaled - unit * mean)
    ).astype(BF16)


def shape(dims, dtype):
    return jax.ShapeDtypeStruct(dims, dtype)


def local(
    query_cache,
    passage_cache,
    hard_offsets,
    passage_lengths,
    segment_inputs,
    segment_cotangents,
    norm_gain,
    gate_weight,
    up_weight,
    down_weight,
):
    everyone = ("dp", "segment")
    count = lax.axis_size(everyone)
    owners = lax.axis_size("dp")
    sections = lax.axis_size("segment")
    rows, width = query_cache.shape
    pairs = rows * count
    cols = width // count
    passages = passage_lengths.shape[0]
    own = segment_inputs.shape[1]
    tokens = own * owners
    units = gate_weight.shape[2]
    section = lax.axis_index("segment")
    dp = lax.axis_index("dp")
    first_row = (lax.axis_index(everyone) * rows).astype(jnp.int32).reshape(1)
    is_last = (section == sections - 1).astype(jnp.int32).reshape(1)
    mine = dp.astype(jnp.int32).reshape(1)

    x_own, cot_own, gain = segment_inputs[0], segment_cotangents[0], norm_gain
    block1 = 4 * rows
    message, both = pl.pallas_call(
        pack_rows,
        out_shape=(shape((count, block1, cols), BF16), shape((2, own, width), BF16)),
        in_specs=[anywhere()] * 4,
        out_specs=(vmem(), vmem()),
        scratch_shapes=[
            pltpu.VMEM((rows, width), BF16),
            pltpu.VMEM((rows, width), BF16),
            pltpu.SemaphoreType.DMA((4,)),
        ],
        compiler_params=params(BIG),
        name="pack_rows",
    )(query_cache, passage_cache, x_own, cot_own)
    both = lax.all_gather(both, "dp", axis=0, tiled=False)
    message = lax.all_to_all(message, everyone, 0, 0, tiled=True)
    parts, unit, inverse = pl.pallas_call(
        partial_scores,
        out_shape=(
            shape((count, rows, pairs), F32),
            shape((2, pairs, cols), F32),
            shape((2, pairs, 1), F32),
        ),
        in_specs=[vmem()],
        out_specs=(vmem(), vmem(), vmem()),
        compiler_params=params(32),
        name="partial_scores",
    )(message)
    parts = lax.all_to_all(parts, everyone, 0, 0, tiled=True)
    message = pl.pallas_call(
        softmax_rows,
        out_shape=shape((count, 2 * rows, pairs), BF16),
        in_specs=[smem(), vmem(), vmem()],
        out_specs=vmem(),
        compiler_params=params(32),
        name="softmax_rows",
    )(first_row, parts, hard_offsets.T)
    message = lax.all_to_all(message, everyone, 0, 0, tiled=True)
    back = -(-(2 * rows + passages) // 16) * 16
    message = pl.pallas_call(
        lambda *refs: pair_grads((sections - 1) * rows, passages, *refs),
        out_shape=shape((count, back, cols), BF16),
        in_specs=[vmem(), vmem(), vmem()],
        out_specs=vmem(),
        compiler_params=params(48),
        name="pair_grads",
    )(message, unit, inverse)
    message = lax.all_to_all(message, everyone, 0, 0, tiled=True)

    whole = lambda dims: pl.BlockSpec(dims, lambda i: (0,) * len(dims))
    ring = pltpu.SemaphoreType.DMA((WINDOW,))
    step = min(512, width)
    normed, gate, up = pl.pallas_call(
        forward,
        out_shape=(
            shape((tokens, width), BF16),
            shape((tokens, units), F32),
            shape((tokens, units), F32),
        ),
        in_specs=[anywhere(), vmem(), anywhere(), anywhere()],
        out_specs=(vmem(), vmem(), vmem()),
        scratch_shapes=[
            pltpu.VMEM((owners, own, width), BF16),
            pltpu.VMEM((WINDOW, step, units), BF16),
            pltpu.VMEM((WINDOW, step, units), BF16),
            pltpu.SemaphoreType.DMA((1,)),
            ring,
            ring,
        ],
        compiler_params=params(BIG),
        cost_estimate=pl.CostEstimate(
            flops=4 * tokens * width * units,
            bytes_accessed=4 * width * units,
            transcendentals=0,
        ),
        name="forward",
    )(both, gain, gate_weight[0], up_weight[0])

    cuts = max(1, width // 512)
    deep_cuts = units // 256 if units % 256 == 0 else 1
    part_shape = shape((own, width + 2 * (width // own)), BF16)
    block = (WINDOW, width // cuts, units)
    outs = pl.pallas_call(
        lambda *refs: backward(cuts, deep_cuts, *refs),
        out_shape=(
            shape((rows, width), BF16),
            shape((rows, width), BF16),
            shape((tokens, units), BF16),
            shape((tokens, units), BF16),
            shape((tokens, units), BF16),
            shape((tokens, width), BF16),
            shape((own, width), BF16),
        )
        + (part_shape,) * owners,
        in_specs=[smem(), smem(), smem()] + [vmem()] * 4 + [anywhere()] * 3,
        out_specs=tuple(vmem() for _ in range(7 + owners)),
        scratch_shapes=[
            pltpu.VMEM(block, BF16),
            pltpu.VMEM(block, BF16),
            pltpu.VMEM((WINDOW, units // deep_cuts, width), BF16),
            pltpu.VMEM((units, tokens), BF16),
            pltpu.VMEM((units, tokens), BF16),
            pltpu.VMEM((owners, own, width), BF16),
            pltpu.VMEM((1, width), F32),
            pltpu.VMEM((tokens, 1), F32),
            ring,
            ring,
            ring,
        ],
        compiler_params=params(BIG),
        cost_estimate=pl.CostEstimate(
            flops=6 * tokens * width * units,
            bytes_accessed=6 * width * units,
            transcendentals=tokens * units,
        ),
        name="backward",
    )(
        is_last,
        mine,
        passage_lengths,
        message,
        both,
        gate,
        up,
        gate_weight[0],
        up_weight[0],
        down_weight[0],
    )
    query_grads, passage_grads, hidden, d_up, d_gate, cot, cot_rows = outs[:7]
    deltas = [outs[7]]
    for k in range(1, owners):
        pairs_ = [(partner(i, k, owners), i) for i in range(owners)]
        deltas.append(lax.ppermute(outs[7 + k], "dp", pairs_))

    step = min(512, width)
    gate_grads, up_grads, down_grads = pl.pallas_call(
        weight_grads,
        grid=(width // step,),
        out_shape=(
            shape((width, units), BF16),
            shape((width, units), BF16),
            shape((units, width), BF16),
        ),
        in_specs=[
            pl.BlockSpec((tokens, step), lambda i: (0, i)),
            whole((tokens, units)),
            whole((tokens, units)),
            whole((tokens, units)),
            pl.BlockSpec((tokens, step), lambda i: (0, i)),
        ],
        out_specs=(
            pl.BlockSpec((step, units), lambda i: (i, 0)),
            pl.BlockSpec((step, units), lambda i: (i, 0)),
            pl.BlockSpec((units, step), lambda i: (0, i)),
        ),
        scratch_shapes=[pltpu.VMEM((units, tokens), BF16)],
        compiler_params=params(BIG),
        cost_estimate=pl.CostEstimate(
            flops=6 * tokens * width * units,
            bytes_accessed=6 * width * units,
            transcendentals=0,
        ),
        name="weight_grads",
    )(normed, d_gate, d_up, hidden, cot)

    input_grads, gain_grads = pl.pallas_call(
        finish,
        out_shape=(shape((own, width), BF16), shape((1, width), F32)),
        in_specs=[smem()] + [vmem()] * (owners + 3),
        out_specs=(vmem(), vmem()),
        scratch_shapes=[pltpu.VMEM((owners, own, width // own), F32)],
        compiler_params=params(32),
        name="finish",
    )(mine, *deltas, x_own, cot_rows, gain)
    return (
        query_grads,
        passage_grads,
        input_grads[None],
        gate_grads[None],
        up_grads[None],
        down_grads[None],
        gain_grads,
    )


def solution(mesh):
    pair = P(("dp", "segment"), None)
    token = P("segment", "dp", None)
    wide = P("segment", None, "dp")
    return jax.shard_map(
        local,
        mesh=mesh,
        in_specs=(pair, pair, pair, P(), token, token, P("segment", None), wide, wide, token),
        out_specs=(pair, pair, token, wide, wide, token, P("segment", None)),
        check_vma=False,
    )
```

```python
import jax
import jax.numpy as jnp
from jax import lax
from jax.experimental import pallas as pl
from jax.experimental.pallas import tpu as pltpu
from jax.sharding import PartitionSpec as P

HN_BLOCK = 128
TAU = 0.02
HN_WEIGHT = 64.0
EPS_NORM = 1e-06
EPS_RMS = 1e-05

F32 = jnp.float32
BF16 = jnp.bfloat16
MIB = 2**20
WINDOW = 3
BIG = 62
NT = (((1,), (1,)), ((), ()))
TN = (((0,), (0,)), ((), ()))


def vmem():
    return pl.BlockSpec(memory_space=pltpu.VMEM)


def smem():
    return pl.BlockSpec(memory_space=pltpu.SMEM)


def anywhere():
    return pl.BlockSpec(memory_space=pl.ANY)


def params(mib):
    return pltpu.CompilerParams(vmem_limit_bytes=mib * MIB)


def iota(shape, axis):
    return lax.broadcasted_iota(jnp.int32, shape, axis)


def split3(value):
    high = value.astype(BF16).astype(F32)
    rest = value - high
    middle = rest.astype(BF16).astype(F32)
    return high, middle, (rest - middle).astype(BF16).astype(F32)


def to_row(column, width):
    n = column.shape[0]
    pick = iota((n, width), 0) == iota((n, width), 1)
    return jnp.sum(jnp.where(pick, column, 0.0), axis=0, keepdims=True)


def to_columns(rows, n):
    shape = rows.shape[:-2] + (n, rows.shape[-1])
    pick = iota(shape, len(shape) - 2) == iota(shape, len(shape) - 1)
    return jnp.sum(jnp.where(pick, rows, 0.0), axis=-1, keepdims=True)


def row_inverse(ref, rows, mean, eps):
    total = jnp.zeros((rows, 1), F32)
    width = ref.shape[1]
    step = min(width, 1024)
    for at in range(0, width, step):
        part = ref[:, at : at + step].astype(F32)
        total += jnp.sum(part * part, axis=1, keepdims=True)
    if mean:
        total = total / width
    return lax.rsqrt(total + eps)


def pack_rows(query_hbm, passage_hbm, out_ref, query_ref, passage_ref, sems):
    count, block, cols = out_ref.shape
    rows = query_ref.shape[0]
    copies = [
        pltpu.make_async_copy(query_hbm, query_ref, sems.at[0]),
        pltpu.make_async_copy(passage_hbm, passage_ref, sems.at[1]),
    ]
    for copy in copies:
        copy.start()
    copies[0].wait()
    copies[1].wait()
    inverse = jnp.concatenate(
        [
            row_inverse(query_ref, rows, False, EPS_NORM),
            row_inverse(passage_ref, rows, False, EPS_NORM),
        ],
        axis=0,
    )
    terms = [to_row(term, cols) for term in split3(inverse)]
    extra = jnp.concatenate(
        terms + [jnp.zeros((block - 2 * rows - 3, cols), F32)], axis=0
    )
    for peer in range(count):
        cut = slice(peer * cols, (peer + 1) * cols)
        both = jnp.concatenate(
            [
                query_ref[:, cut].astype(F32),
                passage_ref[:, cut].astype(F32),
                extra,
            ],
            axis=0,
        )
        out_ref[peer] = both.astype(BF16)


def partial_scores(rows_ref, out_ref, unit_ref, inverse_ref):
    count, block, cols = rows_ref.shape
    rows = out_ref.shape[1]
    pairs = count * rows
    values = rows_ref[...].astype(F32)
    lines = values[:, 2 * rows : 2 * rows + 1]
    lines = lines + values[:, 2 * rows + 1 : 2 * rows + 2]
    lines = lines + values[:, 2 * rows + 2 : 2 * rows + 3]
    inverse = to_columns(lines, 2 * rows)
    unit = values[:, : 2 * rows] * inverse
    query_unit = unit[:, :rows].reshape(pairs, cols)
    passage_unit = unit[:, rows:].reshape(pairs, cols)
    unit_ref[0] = query_unit
    unit_ref[1] = passage_unit
    inverse_ref[0] = inverse[:, :rows].reshape(pairs, 1)
    inverse_ref[1] = inverse[:, rows:].reshape(pairs, 1)
    scores = lax.dot_general(
        query_unit.astype(BF16), passage_unit.astype(BF16), NT, preferred_element_type=F32
    )
    out_ref[...] = scores.reshape(out_ref.shape)


def softmax_rows(first_ref, parts_ref, offsets_ref, out_ref):
    count, block, pairs = out_ref.shape
    rows = parts_ref.shape[1]
    scores = jnp.sum(parts_ref[...], axis=0) / TAU
    row = first_ref[0] + iota((rows, pairs), 0)
    column = iota((rows, pairs), 1)
    base = row // HN_BLOCK * HN_BLOCK
    offsets = to_columns(offsets_ref[...].astype(F32)[:, None, :], rows).astype(jnp.int32)
    tallies = jnp.zeros((rows, pairs), F32)
    for k in range(offsets_ref.shape[0]):
        tallies += (base + offsets[k] == column).astype(F32)
    weighted = (1.0 + HN_WEIGHT * tallies) * jnp.exp(scores)
    totals = jnp.sum(weighted, axis=1, keepdims=True)
    dscore = weighted / totals - (row == column).astype(F32)
    dscore = dscore.astype(BF16).astype(F32)
    product = dscore * scores
    lines = list(split3(jnp.sum(product, axis=0, keepdims=True)))
    lines += [
        to_row(term, pairs) for term in split3(jnp.sum(product, axis=1, keepdims=True))
    ]
    lines.append(jnp.zeros((block - rows - 6, pairs), F32))
    message = jnp.concatenate([dscore] + lines, axis=0).astype(BF16)
    for peer in range(count):
        out_ref[peer] = message


def pair_grads(first, take, rows_ref, unit_ref, inverse_ref, out_ref):
    count, block, pairs = rows_ref.shape
    rows = pairs // count
    cols = unit_ref.shape[2]
    values = rows_ref[...].astype(F32)
    dscore = values[:, :rows].reshape(pairs, pairs).astype(BF16)
    column_line = jnp.sum(
        values[:, rows] + values[:, rows + 1] + values[:, rows + 2], axis=0, keepdims=True
    )
    column_dots = to_columns(column_line, pairs)
    row_lines = (
        values[:, rows + 3 : rows + 4]
        + values[:, rows + 4 : rows + 5]
        + values[:, rows + 5 : rows + 6]
    )
    row_dots = to_columns(row_lines, rows).reshape(pairs, 1)
    query_unit, passage_unit = unit_ref[0], unit_ref[1]
    query_dir = (
        jnp.dot(dscore, passage_unit.astype(BF16), preferred_element_type=F32) / TAU
    )
    passage_dir = (
        lax.dot_general(dscore, query_unit.astype(BF16), TN, preferred_element_type=F32) / TAU
    )
    query_grad = inverse_ref[0] * (query_dir - query_unit * row_dots)
    passage_grad = inverse_ref[1] * (passage_dir - passage_unit * column_dots)
    pieces = [
        query_grad.reshape(count, rows, cols),
        passage_grad.reshape(count, rows, cols),
    ]
    picked = passage_grad[first : first + take]
    spare = out_ref.shape[1] - 2 * rows - take
    if spare:
        picked = jnp.concatenate([picked, jnp.zeros((spare, cols), F32)], axis=0)
    pieces.append(jnp.broadcast_to(picked[None], (count,) + picked.shape))
    out_ref[...] = jnp.concatenate(pieces, axis=1).astype(BF16)


class Ring:
    def __init__(self, hbm, slots, sems, step):
        self.hbm, self.slots, self.sems, self.step = hbm, slots, sems, step

    def copy(self, c):
        slot = lax.rem(c, WINDOW)
        part = pl.ds(c * self.step, self.step)
        return pltpu.make_async_copy(self.hbm.at[part], self.slots.at[slot], self.sems.at[slot])


def forward(
    near_hbm,
    far_hbm,
    gain_ref,
    gate_hbm,
    up_hbm,
    normed_out,
    gate_out,
    up_out,
    x_s,
    gate_w,
    up_w,
    x_sem,
    gate_sem,
    up_sem,
):
    tokens, width = normed_out.shape
    step = gate_w.shape[1]
    blocks = width // step
    gate_ring = Ring(gate_hbm, gate_w, gate_sem, step)
    up_ring = Ring(up_hbm, up_w, up_sem, step)
    half = tokens // 2
    fetches = [
        pltpu.make_async_copy(near_hbm, x_s.at[pl.ds(0, half)], x_sem.at[0]),
        pltpu.make_async_copy(far_hbm, x_s.at[pl.ds(half, half)], x_sem.at[1]),
    ]
    for fetch in fetches:
        fetch.start()
    for c in range(min(WINDOW, blocks)):
        gate_ring.copy(c).start()
        up_ring.copy(c).start()
    for fetch in fetches:
        fetch.wait()
    x = x_s[...].astype(F32)
    inverse = lax.rsqrt(jnp.sum(x * x, axis=1, keepdims=True) / width + EPS_RMS)
    normed_out[...] = (x * inverse * gain_ref[...]).astype(BF16)

    def block(c, first):
        slot = lax.rem(c, WINDOW)
        cut = pl.ds(pl.multiple_of(c * step, step), step)
        normed = normed_out[:, cut]
        gate_ring.copy(c).wait()
        gate = jnp.dot(normed, gate_w[slot], preferred_element_type=F32)
        gate_out[...] = gate if first else gate_out[...] + gate
        up_ring.copy(c).wait()
        up = jnp.dot(normed, up_w[slot], preferred_element_type=F32)
        up_out[...] = up if first else up_out[...] + up

        @pl.when(c + WINDOW < blocks)
        def _():
            gate_ring.copy(c + WINDOW).start()
            up_ring.copy(c + WINDOW).start()

    def more(c, carry):
        block(c, False)
        return carry

    block(jnp.int32(0), True)
    lax.fori_loop(1, blocks, more, 0)


def delta_columns(cuts, rings, started, x_s, d_gate_t, d_up_t, outs, gain_s, inverse_s):
    owners = len(outs)
    own, total = outs[0].shape
    width = gain_s.shape[1]
    tokens = owners * own
    gate_ring, up_ring = rings
    step = gate_ring.step
    for c in range(started, min(WINDOW, cuts)):
        gate_ring.copy(c).start()
        up_ring.copy(c).start()
    x = x_s[...].astype(F32)
    inverse_s[...] = lax.rsqrt(jnp.sum(x * x, axis=1, keepdims=True) / width + EPS_RMS)

    def one(c, carry):
        slot = lax.rem(c, WINDOW)
        gate_ring.copy(c).wait()
        up_ring.copy(c).wait()
        cut = pl.ds(pl.multiple_of(c * step, step), step)
        delta = (
            jnp.dot(gate_ring.slots[slot], d_gate_t[...], preferred_element_type=F32)
            + jnp.dot(up_ring.slots[slot], d_up_t[...], preferred_element_type=F32)
        ).T
        low = delta.astype(BF16)
        for owner in range(owners):
            outs[owner][:, cut] = low[owner * own : (owner + 1) * own]
        unit = x_s[:, cut].astype(F32) * inverse_s[...]
        gain_s[:, cut] = jnp.sum(delta * unit, axis=0, keepdims=True)

        @pl.when(c + WINDOW < cuts)
        def _():
            gate_ring.copy(c + WINDOW).start()
            up_ring.copy(c + WINDOW).start()

        return carry

    lax.fori_loop(0, cuts, one, 0)
    fold = width // own
    gain = jnp.concatenate(
        [gain_s[:, r * fold : (r + 1) * fold] for r in range(own)], axis=0
    )
    high, low, _ = split3(gain)
    tail = jnp.concatenate([high, low], axis=1).astype(BF16)
    for k in range(owners):
        outs[k][:, width:] = tail


def backward(
    order,
    cuts,
    deep_cuts,
    last_ref,
    mine_ref,
    lengths_ref,
    back_ref,
    x_near,
    x_far,
    cot_near,
    cot_far,
    gate_ref,
    up_ref,
    gate_hbm,
    up_hbm,
    down_hbm,
    query_out,
    passage_out,
    hidden_out,
    d_up_out,
    d_gate_out,
    cot_out,
    *more,
):
    *delta_outs, gate_w, up_w, down_w, d_up_t, d_gate_t, x_s, gain_s, inverse_s = more[:-3]
    gate_sem, up_sem, down_sem = more[-3:]
    tokens, width = cot_out.shape
    units = gate_ref.shape[1]
    own = delta_outs[0].shape[0]
    deep = units // deep_cuts
    step = gain_s.shape[1] // cuts
    down_ring = Ring(down_hbm, down_w, down_sem, deep)
    gate_ring = Ring(gate_hbm, gate_w, gate_sem, step)
    up_ring = Ring(up_hbm, up_w, up_sem, step)
    early = min(WINDOW, deep_cuts, cuts)
    for c in range(min(WINDOW, deep_cuts)):
        down_ring.copy(c).start()

    count, block, cols = back_ref.shape
    rows = query_out.shape[0]
    passages = block - 2 * rows
    token = jnp.concatenate(
        [iota((own, 1), 0) + (mine_ref[0] ^ mask) * own for mask in order], axis=0
    )
    half = tokens // 2
    x_s[:half, :] = x_near[...]
    x_s[half:, :] = x_far[...]
    lane = iota((tokens, passages), 1)
    start = jnp.int32(0)
    member = jnp.zeros((tokens, passages), F32)
    scale = jnp.zeros((tokens, 1), F32)
    for m in range(lengths_ref.shape[0]):
        length = lengths_ref[m]
        inside = jnp.logical_and(token >= start, token < start + length)
        member = jnp.where(jnp.logical_and(inside, lane == m), 1.0, member)
        scale = jnp.where(inside, 1.0 / (jnp.zeros((tokens, 1), F32) + length.astype(F32)), scale)
        start = start + length
    member = member.astype(BF16)
    last = last_ref[0] == 1
    for peer in range(count):
        cut = slice(peer * cols, (peer + 1) * cols)
        piece = back_ref[peer].astype(F32)
        query_out[:, cut] = piece[:rows].astype(BF16)
        passage_out[:, cut] = piece[rows : 2 * rows].astype(BF16)
        spread = jnp.dot(member, piece[2 * rows :].astype(BF16), preferred_element_type=F32)
        pooled = (spread * scale).astype(BF16)
        given = jnp.concatenate([cot_near[:, cut], cot_far[:, cut]], axis=0)
        cot_out[:, cut] = jnp.where(last, pooled, given)

    def down_step(c, carry):
        slot = lax.rem(c, WINDOW)
        down_ring.copy(c).wait()
        cut = pl.ds(pl.multiple_of(c * deep, deep), deep)
        d_hidden = lax.dot_general(cot_out[...], down_w[slot], NT, preferred_element_type=F32)
        gate, up = gate_ref[:, cut], up_ref[:, cut]
        sigmoid = jax.nn.sigmoid(gate)
        active = gate * sigmoid
        hidden_out[:, cut] = (active * up).astype(BF16)
        d_up = (d_hidden * active).astype(BF16)
        d_gate = (d_hidden * up * sigmoid * (1.0 + gate * (1.0 - sigmoid))).astype(BF16)
        d_up_out[:, cut] = d_up
        d_gate_out[:, cut] = d_gate
        d_up_t[cut, :] = d_up.T
        d_gate_t[cut, :] = d_gate.T
        ahead = c + WINDOW

        @pl.when(ahead < deep_cuts)
        def _():
            down_ring.copy(ahead).start()

        @pl.when(jnp.logical_and(ahead >= deep_cuts, ahead - deep_cuts < early))
        def _():
            gate_ring.copy(ahead - deep_cuts).start()
            up_ring.copy(ahead - deep_cuts).start()

        return carry

    lax.fori_loop(0, deep_cuts, down_step, 0)
    delta_columns(
        cuts,
        (gate_ring, up_ring),
        early,
        x_s,
        d_gate_t,
        d_up_t,
        delta_outs,
        gain_s,
        inverse_s,
    )


def weight_grads(
    normed_ref, d_gate_ref, d_up_ref, hidden_ref, cot_ref, gate_out, up_out, down_out, hidden_t
):
    @pl.when(pl.program_id(0) == 0)
    def _():
        hidden_t[...] = hidden_ref[...].T

    gate_out[...] = lax.dot_general(
        normed_ref[...], d_gate_ref[...], TN, preferred_element_type=F32
    ).astype(BF16)
    up_out[...] = lax.dot_general(
        normed_ref[...], d_up_ref[...], TN, preferred_element_type=F32
    ).astype(BF16)
    down_out[...] = jnp.dot(
        hidden_t[...], cot_ref[...], preferred_element_type=F32
    ).astype(BF16)


def finish(order, mine_ref, *refs):
    *part_refs, x_ref, cot_ref, gain_ref, input_out, gain_out, tail_s = refs
    owners = len(part_refs)
    own, width = x_ref.shape
    fold = width // own
    for k in range(owners):
        tail = part_refs[k][:, width:].astype(F32)
        tail_s[mine_ref[0] ^ order[k]] = tail[:, :fold] + tail[:, fold:]
    gain = tail_s[0]
    for p in range(1, owners):
        gain += tail_s[p]
    for r in range(own):
        gain_out[:, r * fold : (r + 1) * fold] = gain[r : r + 1]
    delta = part_refs[0][:, :width].astype(F32)
    for k in range(1, owners):
        delta += part_refs[k][:, :width].astype(F32)
    inverse = row_inverse(x_ref, own, True, EPS_RMS)
    unit = x_ref[...].astype(F32) * inverse
    scaled = delta * gain_ref[...]
    mean = jnp.sum(scaled * unit, axis=1, keepdims=True) / width
    input_out[...] = (
        cot_ref[...].astype(F32) + inverse * (scaled - unit * mean)
    ).astype(BF16)


def shape(dims, dtype):
    return jax.ShapeDtypeStruct(dims, dtype)


def local(
    query_cache,
    passage_cache,
    hard_offsets,
    passage_lengths,
    segment_inputs,
    segment_cotangents,
    norm_gain,
    gate_weight,
    up_weight,
    down_weight,
):
    everyone = ("dp", "segment")
    count = lax.axis_size(everyone)
    owners = lax.axis_size("dp")
    sections = lax.axis_size("segment")
    rows, width = query_cache.shape
    pairs = rows * count
    cols = width // count
    passages = passage_lengths.shape[0]
    own = segment_inputs.shape[1]
    tokens = own * owners
    units = gate_weight.shape[2]
    section = lax.axis_index("segment")
    dp = lax.axis_index("dp")
    first_row = (lax.axis_index(everyone) * rows).astype(jnp.int32).reshape(1)
    is_last = (section == sections - 1).astype(jnp.int32).reshape(1)
    mine = dp.astype(jnp.int32).reshape(1)

    assert owners & (owners - 1) == 0 and owners > 1
    x_own, cot_own, gain = segment_inputs[0], segment_cotangents[0], norm_gain
    block1 = 4 * rows
    message = pl.pallas_call(
        pack_rows,
        out_shape=shape((count, block1, cols), BF16),
        in_specs=[anywhere()] * 2,
        out_specs=vmem(),
        scratch_shapes=[
            pltpu.VMEM((rows, width), BF16),
            pltpu.VMEM((rows, width), BF16),
            pltpu.SemaphoreType.DMA((2,)),
        ],
        compiler_params=params(BIG),
        name="pack_rows",
    )(query_cache, passage_cache)
    order = [0]
    x_half, cot_half = x_own, cot_own
    moved = []

    def double(values):
        nonlocal x_half, cot_half
        if len(order) == owners:
            return values
        if moved:
            x_half = jnp.concatenate([x_half, moved[0]], axis=0)
            cot_half = jnp.concatenate([cot_half, moved[1]], axis=0)
        mask = owners // 2 // len(order)
        swap = [(i, i ^ mask) for i in range(owners)]
        moved[:] = [lax.ppermute(x_half, "dp", swap), lax.ppermute(cot_half, "dp", swap)]
        order.extend([o ^ mask for o in order])
        return values

    message = double(message)
    message = lax.all_to_all(message, everyone, 0, 0, tiled=True)
    message = double(message)
    parts, unit, inverse = pl.pallas_call(
        partial_scores,
        out_shape=(
            shape((count, rows, pairs), F32),
            shape((2, pairs, cols), F32),
            shape((2, pairs, 1), F32),
        ),
        in_specs=[vmem()],
        out_specs=(vmem(), vmem(), vmem()),
        compiler_params=params(32),
        name="partial_scores",
    )(message)
    parts = lax.all_to_all(parts, everyone, 0, 0, tiled=True)
    parts = double(parts)
    message = pl.pallas_call(
        softmax_rows,
        out_shape=shape((count, 2 * rows, pairs), BF16),
        in_specs=[smem(), vmem(), vmem()],
        out_specs=vmem(),
        compiler_params=params(32),
        name="softmax_rows",
    )(first_row, parts, hard_offsets.T)
    message = lax.all_to_all(message, everyone, 0, 0, tiled=True)
    back = -(-(2 * rows + passages) // 16) * 16
    message = pl.pallas_call(
        lambda *refs: pair_grads((sections - 1) * rows, passages, *refs),
        out_shape=shape((count, back, cols), BF16),
        in_specs=[vmem(), vmem(), vmem()],
        out_specs=vmem(),
        compiler_params=params(48),
        name="pair_grads",
    )(message, unit, inverse)
    message = lax.all_to_all(message, everyone, 0, 0, tiled=True)

    while len(order) < owners:
        message = double(message)
    halves = (x_half, moved[0], cot_half, moved[1])
    whole = lambda dims: pl.BlockSpec(dims, lambda i: (0,) * len(dims))
    ring = pltpu.SemaphoreType.DMA((WINDOW,))
    step = min(512, width)
    normed, gate, up = pl.pallas_call(
        forward,
        out_shape=(
            shape((tokens, width), BF16),
            shape((tokens, units), F32),
            shape((tokens, units), F32),
        ),
        in_specs=[anywhere(), anywhere(), vmem(), anywhere(), anywhere()],
        out_specs=(vmem(), vmem(), vmem()),
        scratch_shapes=[
            pltpu.VMEM((tokens, width), BF16),
            pltpu.VMEM((WINDOW, step, units), BF16),
            pltpu.VMEM((WINDOW, step, units), BF16),
            pltpu.SemaphoreType.DMA((2,)),
            ring,
            ring,
        ],
        compiler_params=params(BIG),
        cost_estimate=pl.CostEstimate(
            flops=4 * tokens * width * units,
            bytes_accessed=4 * width * units,
            transcendentals=0,
        ),
        name="forward",
    )(*halves[:2], gain, gate_weight[0], up_weight[0])

    cuts = max(1, width // 512)
    deep_cuts = units // 256 if units % 256 == 0 else 1
    part_shape = shape((own, width + 2 * (width // own)), BF16)
    block = (WINDOW, width // cuts, units)
    outs = pl.pallas_call(
        lambda *refs: backward(order, cuts, deep_cuts, *refs),
        out_shape=(
            shape((rows, width), BF16),
            shape((rows, width), BF16),
            shape((tokens, units), BF16),
            shape((tokens, units), BF16),
            shape((tokens, units), BF16),
            shape((tokens, width), BF16),
        )
        + (part_shape,) * owners,
        in_specs=[smem(), smem(), smem()] + [vmem()] * 7 + [anywhere()] * 3,
        out_specs=tuple(vmem() for _ in range(6 + owners)),
        scratch_shapes=[
            pltpu.VMEM(block, BF16),
            pltpu.VMEM(block, BF16),
            pltpu.VMEM((WINDOW, units // deep_cuts, width), BF16),
            pltpu.VMEM((units, tokens), BF16),
            pltpu.VMEM((units, tokens), BF16),
            pltpu.VMEM((tokens, width), BF16),
            pltpu.VMEM((1, width), F32),
            pltpu.VMEM((tokens, 1), F32),
            ring,
            ring,
            ring,
        ],
        compiler_params=params(BIG),
        cost_estimate=pl.CostEstimate(
            flops=6 * tokens * width * units,
            bytes_accessed=6 * width * units,
            transcendentals=tokens * units,
        ),
        name="backward",
    )(
        is_last,
        mine,
        passage_lengths,
        message,
        *halves,
        gate,
        up,
        gate_weight[0],
        up_weight[0],
        down_weight[0],
    )
    query_grads, passage_grads, hidden, d_up, d_gate, cot = outs[:6]
    deltas = [outs[6]]
    for mask, part in zip(order[1:], outs[7:]):
        deltas.append(lax.ppermute(part, "dp", [(i, i ^ mask) for i in range(owners)]))

    step = min(512, width)
    gate_grads, up_grads, down_grads = pl.pallas_call(
        weight_grads,
        grid=(width // step,),
        out_shape=(
            shape((width, units), BF16),
            shape((width, units), BF16),
            shape((units, width), BF16),
        ),
        in_specs=[
            pl.BlockSpec((tokens, step), lambda i: (0, i)),
            whole((tokens, units)),
            whole((tokens, units)),
            whole((tokens, units)),
            pl.BlockSpec((tokens, step), lambda i: (0, i)),
        ],
        out_specs=(
            pl.BlockSpec((step, units), lambda i: (i, 0)),
            pl.BlockSpec((step, units), lambda i: (i, 0)),
            pl.BlockSpec((units, step), lambda i: (0, i)),
        ),
        scratch_shapes=[pltpu.VMEM((units, tokens), BF16)],
        compiler_params=params(BIG),
        cost_estimate=pl.CostEstimate(
            flops=6 * tokens * width * units,
            bytes_accessed=6 * width * units,
            transcendentals=0,
        ),
        name="weight_grads",
    )(normed, d_gate, d_up, hidden, cot)

    input_grads, gain_grads = pl.pallas_call(
        lambda *refs: finish(order, *refs),
        out_shape=(shape((own, width), BF16), shape((1, width), F32)),
        in_specs=[smem()] + [vmem()] * (owners + 3),
        out_specs=(vmem(), vmem()),
        scratch_shapes=[pltpu.VMEM((owners, own, width // own), F32)],
        compiler_params=params(32),
        name="finish",
    )(mine, *deltas, x_own, cot[:own], gain)
    return (
        query_grads,
        passage_grads,
        input_grads[None],
        gate_grads[None],
        up_grads[None],
        down_grads[None],
        gain_grads,
    )


def solution(mesh):
    pair = P(("dp", "segment"), None)
    token = P("segment", "dp", None)
    wide = P("segment", None, "dp")
    return jax.shard_map(
        local,
        mesh=mesh,
        in_specs=(pair, pair, pair, P(), token, token, P("segment", None), wide, wide, token),
        out_specs=(pair, pair, token, wide, wide, token, P("segment", None)),
        check_vma=False,
    )
```

```python
import jax
import jax.numpy as jnp
from jax import lax
from jax.experimental import pallas as pl
from jax.experimental.pallas import tpu as pltpu
from jax.sharding import PartitionSpec as P

HN_BLOCK = 128
TAU = 0.02
HN_WEIGHT = 64.0
EPS_NORM = 1e-06
EPS_RMS = 1e-05

F32 = jnp.float32
BF16 = jnp.bfloat16
MIB = 2**20
WINDOW = 3
BIG = 62
NT = (((1,), (1,)), ((), ()))
TN = (((0,), (0,)), ((), ()))


def vmem():
    return pl.BlockSpec(memory_space=pltpu.VMEM)


def smem():
    return pl.BlockSpec(memory_space=pltpu.SMEM)


def anywhere():
    return pl.BlockSpec(memory_space=pl.ANY)


def params(mib):
    return pltpu.CompilerParams(vmem_limit_bytes=mib * MIB)


def iota(shape, axis):
    return lax.broadcasted_iota(jnp.int32, shape, axis)


def split3(value):
    high = value.astype(BF16).astype(F32)
    rest = value - high
    middle = rest.astype(BF16).astype(F32)
    return high, middle, (rest - middle).astype(BF16).astype(F32)


def to_row(column, width):
    n = column.shape[0]
    pick = iota((n, width), 0) == iota((n, width), 1)
    return jnp.sum(jnp.where(pick, column, 0.0), axis=0, keepdims=True)


def to_columns(rows, n):
    shape = rows.shape[:-2] + (n, rows.shape[-1])
    pick = iota(shape, len(shape) - 2) == iota(shape, len(shape) - 1)
    return jnp.sum(jnp.where(pick, rows, 0.0), axis=-1, keepdims=True)


def row_inverse(ref, rows, mean, eps):
    total = jnp.zeros((rows, 1), F32)
    width = ref.shape[1]
    step = min(width, 1024)
    for at in range(0, width, step):
        part = ref[:, at : at + step].astype(F32)
        total += jnp.sum(part * part, axis=1, keepdims=True)
    if mean:
        total = total / width
    return lax.rsqrt(total + eps)


def pack_rows(query_hbm, passage_hbm, out_ref, query_ref, passage_ref, sems):
    count, block, cols = out_ref.shape
    rows = query_ref.shape[0]
    copies = [
        pltpu.make_async_copy(query_hbm, query_ref, sems.at[0]),
        pltpu.make_async_copy(passage_hbm, passage_ref, sems.at[1]),
    ]
    for copy in copies:
        copy.start()
    copies[0].wait()
    copies[1].wait()
    inverse = jnp.concatenate(
        [
            row_inverse(query_ref, rows, False, EPS_NORM),
            row_inverse(passage_ref, rows, False, EPS_NORM),
        ],
        axis=0,
    )
    terms = [to_row(term, cols) for term in split3(inverse)]
    extra = jnp.concatenate(
        terms + [jnp.zeros((block - 2 * rows - 3, cols), F32)], axis=0
    )
    for peer in range(count):
        cut = slice(peer * cols, (peer + 1) * cols)
        both = jnp.concatenate(
            [
                query_ref[:, cut].astype(F32),
                passage_ref[:, cut].astype(F32),
                extra,
            ],
            axis=0,
        )
        out_ref[peer] = both.astype(BF16)


def partial_scores(rows_ref, out_ref, unit_ref, inverse_ref):
    count, block, cols = rows_ref.shape
    rows = out_ref.shape[1]
    pairs = count * rows
    values = rows_ref[...].astype(F32)
    lines = values[:, 2 * rows : 2 * rows + 1]
    lines = lines + values[:, 2 * rows + 1 : 2 * rows + 2]
    lines = lines + values[:, 2 * rows + 2 : 2 * rows + 3]
    inverse = to_columns(lines, 2 * rows)
    unit = values[:, : 2 * rows] * inverse
    query_unit = unit[:, :rows].reshape(pairs, cols)
    passage_unit = unit[:, rows:].reshape(pairs, cols)
    unit_ref[0] = query_unit
    unit_ref[1] = passage_unit
    inverse_ref[0] = inverse[:, :rows].reshape(pairs, 1)
    inverse_ref[1] = inverse[:, rows:].reshape(pairs, 1)
    scores = lax.dot_general(
        query_unit.astype(BF16), passage_unit.astype(BF16), NT, preferred_element_type=F32
    )
    out_ref[...] = scores.reshape(out_ref.shape)


def softmax_rows(first_ref, parts_ref, offsets_ref, out_ref):
    count, block, pairs = out_ref.shape
    rows = parts_ref.shape[1]
    scores = jnp.sum(parts_ref[...], axis=0) / TAU
    row = first_ref[0] + iota((rows, pairs), 0)
    column = iota((rows, pairs), 1)
    base = row // HN_BLOCK * HN_BLOCK
    offsets = to_columns(offsets_ref[...].astype(F32)[:, None, :], rows).astype(jnp.int32)
    tallies = jnp.zeros((rows, pairs), F32)
    for k in range(offsets_ref.shape[0]):
        tallies += (base + offsets[k] == column).astype(F32)
    weighted = (1.0 + HN_WEIGHT * tallies) * jnp.exp(scores)
    totals = jnp.sum(weighted, axis=1, keepdims=True)
    dscore = weighted / totals - (row == column).astype(F32)
    dscore = dscore.astype(BF16).astype(F32)
    product = dscore * scores
    lines = list(split3(jnp.sum(product, axis=0, keepdims=True)))
    lines += [
        to_row(term, pairs) for term in split3(jnp.sum(product, axis=1, keepdims=True))
    ]
    lines.append(jnp.zeros((block - rows - 6, pairs), F32))
    message = jnp.concatenate([dscore] + lines, axis=0).astype(BF16)
    for peer in range(count):
        out_ref[peer] = message


def pair_grads(first, take, rows_ref, unit_ref, inverse_ref, out_ref):
    count, block, pairs = rows_ref.shape
    rows = pairs // count
    cols = unit_ref.shape[2]
    values = rows_ref[...].astype(F32)
    dscore = values[:, :rows].reshape(pairs, pairs).astype(BF16)
    column_line = jnp.sum(
        values[:, rows] + values[:, rows + 1] + values[:, rows + 2], axis=0, keepdims=True
    )
    column_dots = to_columns(column_line, pairs)
    row_lines = (
        values[:, rows + 3 : rows + 4]
        + values[:, rows + 4 : rows + 5]
        + values[:, rows + 5 : rows + 6]
    )
    row_dots = to_columns(row_lines, rows).reshape(pairs, 1)
    query_unit, passage_unit = unit_ref[0], unit_ref[1]
    query_dir = (
        jnp.dot(dscore, passage_unit.astype(BF16), preferred_element_type=F32) / TAU
    )
    passage_dir = (
        lax.dot_general(dscore, query_unit.astype(BF16), TN, preferred_element_type=F32) / TAU
    )
    query_grad = inverse_ref[0] * (query_dir - query_unit * row_dots)
    passage_grad = inverse_ref[1] * (passage_dir - passage_unit * column_dots)
    pieces = [
        query_grad.reshape(count, rows, cols),
        passage_grad.reshape(count, rows, cols),
    ]
    picked = passage_grad[first : first + take]
    spare = out_ref.shape[1] - 2 * rows - take
    if spare:
        picked = jnp.concatenate([picked, jnp.zeros((spare, cols), F32)], axis=0)
    pieces.append(jnp.broadcast_to(picked[None], (count,) + picked.shape))
    out_ref[...] = jnp.concatenate(pieces, axis=1).astype(BF16)


class Ring:
    def __init__(self, hbm, slots, sems, step):
        self.hbm, self.slots, self.sems, self.step = hbm, slots, sems, step

    def copy(self, c):
        slot = lax.rem(c, WINDOW)
        part = pl.ds(c * self.step, self.step)
        return pltpu.make_async_copy(self.hbm.at[part], self.slots.at[slot], self.sems.at[slot])


def forward(
    near_hbm,
    far_hbm,
    gain_ref,
    gate_hbm,
    up_hbm,
    normed_out,
    gate_out,
    up_out,
    x_s,
    gate_w,
    up_w,
    x_sem,
    gate_sem,
    up_sem,
):
    tokens, width = normed_out.shape
    step = gate_w.shape[1]
    blocks = width // step
    gate_ring = Ring(gate_hbm, gate_w, gate_sem, step)
    up_ring = Ring(up_hbm, up_w, up_sem, step)
    half = tokens // 2
    fetches = [
        pltpu.make_async_copy(near_hbm, x_s.at[pl.ds(0, half)], x_sem.at[0]),
        pltpu.make_async_copy(far_hbm, x_s.at[pl.ds(half, half)], x_sem.at[1]),
    ]
    for fetch in fetches:
        fetch.start()
    for c in range(min(WINDOW, blocks)):
        gate_ring.copy(c).start()
        up_ring.copy(c).start()
    for fetch in fetches:
        fetch.wait()
    x = x_s[...].astype(F32)
    inverse = lax.rsqrt(jnp.sum(x * x, axis=1, keepdims=True) / width + EPS_RMS)
    normed_out[...] = (x * inverse * gain_ref[...]).astype(BF16)

    def block(c, first):
        slot = lax.rem(c, WINDOW)
        cut = pl.ds(pl.multiple_of(c * step, step), step)
        normed = normed_out[:, cut]
        gate_ring.copy(c).wait()
        gate = jnp.dot(normed, gate_w[slot], preferred_element_type=F32)
        gate_out[...] = gate if first else gate_out[...] + gate
        up_ring.copy(c).wait()
        up = jnp.dot(normed, up_w[slot], preferred_element_type=F32)
        up_out[...] = up if first else up_out[...] + up

        @pl.when(c + WINDOW < blocks)
        def _():
            gate_ring.copy(c + WINDOW).start()
            up_ring.copy(c + WINDOW).start()

    def more(c, carry):
        block(c, False)
        return carry

    block(jnp.int32(0), True)
    lax.fori_loop(1, blocks, more, 0)


def delta_columns(cuts, rings, started, x_s, d_gate_t, d_up_t, outs, gain_s, inverse_s):
    owners = len(outs)
    own, total = outs[0].shape
    width = gain_s.shape[1]
    tokens = owners * own
    gate_ring, up_ring = rings
    step = gate_ring.step
    for c in range(started, min(WINDOW, cuts)):
        gate_ring.copy(c).start()
        up_ring.copy(c).start()
    x = x_s[...].astype(F32)
    inverse_s[...] = lax.rsqrt(jnp.sum(x * x, axis=1, keepdims=True) / width + EPS_RMS)

    def one(c, carry):
        slot = lax.rem(c, WINDOW)
        gate_ring.copy(c).wait()
        up_ring.copy(c).wait()
        cut = pl.ds(pl.multiple_of(c * step, step), step)
        delta = (
            jnp.dot(gate_ring.slots[slot], d_gate_t[...], preferred_element_type=F32)
            + jnp.dot(up_ring.slots[slot], d_up_t[...], preferred_element_type=F32)
        ).T
        low = delta.astype(BF16)
        for owner in range(owners):
            outs[owner][:, cut] = low[owner * own : (owner + 1) * own]
        unit = x_s[:, cut].astype(F32) * inverse_s[...]
        gain_s[:, cut] = jnp.sum(delta * unit, axis=0, keepdims=True)

        @pl.when(c + WINDOW < cuts)
        def _():
            gate_ring.copy(c + WINDOW).start()
            up_ring.copy(c + WINDOW).start()

        return carry

    lax.fori_loop(0, cuts, one, 0)
    fold = width // own
    gain = jnp.concatenate(
        [gain_s[:, r * fold : (r + 1) * fold] for r in range(own)], axis=0
    )
    high, low, _ = split3(gain)
    tail = jnp.concatenate([high, low], axis=1).astype(BF16)
    for k in range(owners):
        outs[k][:, width:] = tail


def backward(
    order,
    cuts,
    deep_cuts,
    last_ref,
    mine_ref,
    lengths_ref,
    back_ref,
    x_near,
    x_far,
    cot_near,
    cot_far,
    gate_ref,
    up_ref,
    gate_hbm,
    up_hbm,
    down_hbm,
    query_out,
    passage_out,
    hidden_out,
    d_up_out,
    d_gate_out,
    cot_out,
    cot_own_out,
    *more,
):
    *delta_outs, gate_w, up_w, down_w, d_up_t, d_gate_t, x_s, gain_s, inverse_s = more[:-3]
    gate_sem, up_sem, down_sem = more[-3:]
    tokens, width = cot_out.shape
    units = gate_ref.shape[1]
    own = delta_outs[0].shape[0]
    deep = units // deep_cuts
    step = gain_s.shape[1] // cuts
    down_ring = Ring(down_hbm, down_w, down_sem, deep)
    gate_ring = Ring(gate_hbm, gate_w, gate_sem, step)
    up_ring = Ring(up_hbm, up_w, up_sem, step)
    early = min(WINDOW, deep_cuts, cuts)
    for c in range(min(WINDOW, deep_cuts)):
        down_ring.copy(c).start()

    count, block, cols = back_ref.shape
    rows = query_out.shape[0]
    passages = block - 2 * rows
    token = jnp.concatenate(
        [iota((own, 1), 0) + (mine_ref[0] ^ mask) * own for mask in order], axis=0
    )
    half = tokens // 2
    x_s[:half, :] = x_near[...]
    x_s[half:, :] = x_far[...]
    lane = iota((tokens, passages), 1)
    start = jnp.int32(0)
    member = jnp.zeros((tokens, passages), F32)
    scale = jnp.zeros((tokens, 1), F32)
    for m in range(lengths_ref.shape[0]):
        length = lengths_ref[m]
        inside = jnp.logical_and(token >= start, token < start + length)
        member = jnp.where(jnp.logical_and(inside, lane == m), 1.0, member)
        scale = jnp.where(inside, 1.0 / (jnp.zeros((tokens, 1), F32) + length.astype(F32)), scale)
        start = start + length
    member = member.astype(BF16)
    last = last_ref[0] == 1
    for peer in range(count):
        cut = slice(peer * cols, (peer + 1) * cols)
        piece = back_ref[peer].astype(F32)
        query_out[:, cut] = piece[:rows].astype(BF16)
        passage_out[:, cut] = piece[rows : 2 * rows].astype(BF16)
        spread = jnp.dot(member, piece[2 * rows :].astype(BF16), preferred_element_type=F32)
        pooled = (spread * scale).astype(BF16)
        given = jnp.concatenate([cot_near[:, cut], cot_far[:, cut]], axis=0)
        cot_out[:, cut] = jnp.where(last, pooled, given)

    cot_own_out[...] = cot_out[:own, :]

    def down_step(c, carry):
        slot = lax.rem(c, WINDOW)
        down_ring.copy(c).wait()
        cut = pl.ds(pl.multiple_of(c * deep, deep), deep)
        d_hidden = lax.dot_general(cot_out[...], down_w[slot], NT, preferred_element_type=F32)
        gate, up = gate_ref[:, cut], up_ref[:, cut]
        sigmoid = jax.nn.sigmoid(gate)
        active = gate * sigmoid
        hidden_out[:, cut] = (active * up).astype(BF16)
        d_up = (d_hidden * active).astype(BF16)
        d_gate = (d_hidden * up * sigmoid * (1.0 + gate * (1.0 - sigmoid))).astype(BF16)
        d_up_out[:, cut] = d_up
        d_gate_out[:, cut] = d_gate
        d_up_t[cut, :] = d_up.T
        d_gate_t[cut, :] = d_gate.T
        ahead = c + WINDOW

        @pl.when(ahead < deep_cuts)
        def _():
            down_ring.copy(ahead).start()

        @pl.when(jnp.logical_and(ahead >= deep_cuts, ahead - deep_cuts < early))
        def _():
            gate_ring.copy(ahead - deep_cuts).start()
            up_ring.copy(ahead - deep_cuts).start()

        return carry

    lax.fori_loop(0, deep_cuts, down_step, 0)
    delta_columns(
        cuts,
        (gate_ring, up_ring),
        early,
        x_s,
        d_gate_t,
        d_up_t,
        delta_outs,
        gain_s,
        inverse_s,
    )


def weight_grads(
    normed_ref, d_gate_ref, d_up_ref, hidden_ref, cot_ref, gate_out, up_out, down_out, hidden_t
):
    @pl.when(pl.program_id(0) == 0)
    def _():
        hidden_t[...] = hidden_ref[...].T

    gate_out[...] = lax.dot_general(
        normed_ref[...], d_gate_ref[...], TN, preferred_element_type=F32
    ).astype(BF16)
    up_out[...] = lax.dot_general(
        normed_ref[...], d_up_ref[...], TN, preferred_element_type=F32
    ).astype(BF16)
    down_out[...] = jnp.dot(
        hidden_t[...], cot_ref[...], preferred_element_type=F32
    ).astype(BF16)


def finish(order, mine_ref, *refs):
    *part_refs, x_ref, cot_ref, gain_ref, input_out, gain_out, tail_s = refs
    owners = len(part_refs)
    own, width = x_ref.shape
    fold = width // own
    for k in range(owners):
        tail = part_refs[k][:, width:].astype(F32)
        tail_s[mine_ref[0] ^ order[k]] = tail[:, :fold] + tail[:, fold:]
    gain = tail_s[0]
    for p in range(1, owners):
        gain += tail_s[p]
    for r in range(own):
        gain_out[:, r * fold : (r + 1) * fold] = gain[r : r + 1]
    delta = part_refs[0][:, :width].astype(F32)
    for k in range(1, owners):
        delta += part_refs[k][:, :width].astype(F32)
    inverse = row_inverse(x_ref, own, True, EPS_RMS)
    unit = x_ref[...].astype(F32) * inverse
    scaled = delta * gain_ref[...]
    mean = jnp.sum(scaled * unit, axis=1, keepdims=True) / width
    input_out[...] = (
        cot_ref[...].astype(F32) + inverse * (scaled - unit * mean)
    ).astype(BF16)


def shape(dims, dtype):
    return jax.ShapeDtypeStruct(dims, dtype)


def local(
    query_cache,
    passage_cache,
    hard_offsets,
    passage_lengths,
    segment_inputs,
    segment_cotangents,
    norm_gain,
    gate_weight,
    up_weight,
    down_weight,
):
    everyone = ("dp", "segment")
    count = lax.axis_size(everyone)
    owners = lax.axis_size("dp")
    sections = lax.axis_size("segment")
    rows, width = query_cache.shape
    pairs = rows * count
    cols = width // count
    passages = passage_lengths.shape[0]
    own = segment_inputs.shape[1]
    tokens = own * owners
    units = gate_weight.shape[2]
    section = lax.axis_index("segment")
    dp = lax.axis_index("dp")
    first_row = (lax.axis_index(everyone) * rows).astype(jnp.int32).reshape(1)
    is_last = (section == sections - 1).astype(jnp.int32).reshape(1)
    mine = dp.astype(jnp.int32).reshape(1)

    assert owners & (owners - 1) == 0 and owners > 1
    x_own, cot_own, gain = segment_inputs[0], segment_cotangents[0], norm_gain
    block1 = 4 * rows
    message = pl.pallas_call(
        pack_rows,
        out_shape=shape((count, block1, cols), BF16),
        in_specs=[anywhere()] * 2,
        out_specs=vmem(),
        scratch_shapes=[
            pltpu.VMEM((rows, width), BF16),
            pltpu.VMEM((rows, width), BF16),
            pltpu.SemaphoreType.DMA((2,)),
        ],
        compiler_params=params(BIG),
        name="pack_rows",
    )(query_cache, passage_cache)
    order = [0]
    x_half, cot_half = x_own, cot_own
    moved = []

    def double(values):
        nonlocal x_half, cot_half
        if len(order) == owners:
            return values
        if moved:
            x_half = jnp.concatenate([x_half, moved[0]], axis=0)
            cot_half = jnp.concatenate([cot_half, moved[1]], axis=0)
        mask = owners // 2 // len(order)
        swap = [(i, i ^ mask) for i in range(owners)]
        x_far = lax.ppermute(x_half, "dp", swap)
        if mask == 1:
            x_far, cot_half = lax.optimization_barrier((x_far, cot_half))
        moved[:] = [x_far, lax.ppermute(cot_half, "dp", swap)]
        order.extend([o ^ mask for o in order])
        return values

    message = double(message)
    message = lax.all_to_all(message, everyone, 0, 0, tiled=True)
    message = double(message)
    parts, unit, inverse = pl.pallas_call(
        partial_scores,
        out_shape=(
            shape((count, rows, pairs), F32),
            shape((2, pairs, cols), F32),
            shape((2, pairs, 1), F32),
        ),
        in_specs=[vmem()],
        out_specs=(vmem(), vmem(), vmem()),
        compiler_params=params(32),
        name="partial_scores",
    )(message)
    parts = lax.all_to_all(parts, everyone, 0, 0, tiled=True)
    parts = double(parts)
    message = pl.pallas_call(
        softmax_rows,
        out_shape=shape((count, 2 * rows, pairs), BF16),
        in_specs=[smem(), vmem(), vmem()],
        out_specs=vmem(),
        compiler_params=params(32),
        name="softmax_rows",
    )(first_row, parts, hard_offsets.T)
    message = lax.all_to_all(message, everyone, 0, 0, tiled=True)
    back = -(-(2 * rows + passages) // 16) * 16
    message = pl.pallas_call(
        lambda *refs: pair_grads((sections - 1) * rows, passages, *refs),
        out_shape=shape((count, back, cols), BF16),
        in_specs=[vmem(), vmem(), vmem()],
        out_specs=vmem(),
        compiler_params=params(48),
        name="pair_grads",
    )(message, unit, inverse)
    message = lax.all_to_all(message, everyone, 0, 0, tiled=True)

    while len(order) < owners:
        message = double(message)
    halves = (x_half, moved[0], cot_half, moved[1])
    whole = lambda dims: pl.BlockSpec(dims, lambda i: (0,) * len(dims))
    ring = pltpu.SemaphoreType.DMA((WINDOW,))
    step = min(512, width)
    normed, gate, up = pl.pallas_call(
        forward,
        out_shape=(
            shape((tokens, width), BF16),
            shape((tokens, units), F32),
            shape((tokens, units), F32),
        ),
        in_specs=[anywhere(), anywhere(), vmem(), anywhere(), anywhere()],
        out_specs=(vmem(), vmem(), vmem()),
        scratch_shapes=[
            pltpu.VMEM((tokens, width), BF16),
            pltpu.VMEM((WINDOW, step, units), BF16),
            pltpu.VMEM((WINDOW, step, units), BF16),
            pltpu.SemaphoreType.DMA((2,)),
            ring,
            ring,
        ],
        compiler_params=params(BIG),
        cost_estimate=pl.CostEstimate(
            flops=4 * tokens * width * units,
            bytes_accessed=4 * width * units,
            transcendentals=0,
        ),
        name="forward",
    )(*halves[:2], gain, gate_weight[0], up_weight[0])

    cuts = max(1, width // 512)
    deep_cuts = units // 256 if units % 256 == 0 else 1
    part_shape = shape((own, width + 2 * (width // own)), BF16)
    block = (WINDOW, width // cuts, units)
    outs = pl.pallas_call(
        lambda *refs: backward(order, cuts, deep_cuts, *refs),
        out_shape=(
            shape((rows, width), BF16),
            shape((rows, width), BF16),
            shape((tokens, units), BF16),
            shape((tokens, units), BF16),
            shape((tokens, units), BF16),
            shape((tokens, width), BF16),
            shape((own, width), BF16),
        )
        + (part_shape,) * owners,
        in_specs=[smem(), smem(), smem()] + [vmem()] * 7 + [anywhere()] * 3,
        out_specs=tuple(vmem() for _ in range(7 + owners)),
        scratch_shapes=[
            pltpu.VMEM(block, BF16),
            pltpu.VMEM(block, BF16),
            pltpu.VMEM((WINDOW, units // deep_cuts, width), BF16),
            pltpu.VMEM((units, tokens), BF16),
            pltpu.VMEM((units, tokens), BF16),
            pltpu.VMEM((tokens, width), BF16),
            pltpu.VMEM((1, width), F32),
            pltpu.VMEM((tokens, 1), F32),
            ring,
            ring,
            ring,
        ],
        compiler_params=params(BIG),
        cost_estimate=pl.CostEstimate(
            flops=6 * tokens * width * units,
            bytes_accessed=6 * width * units,
            transcendentals=tokens * units,
        ),
        name="backward",
    )(
        is_last,
        mine,
        passage_lengths,
        message,
        *halves,
        gate,
        up,
        gate_weight[0],
        up_weight[0],
        down_weight[0],
    )
    query_grads, passage_grads, hidden, d_up, d_gate, cot, cot_rows = outs[:7]
    deltas = list(outs[7:])
    for mask in range(1, owners):
        j = order.index(mask)
        deltas[j] = lax.ppermute(deltas[j], "dp", [(i, i ^ mask) for i in range(owners)])

    step = min(512, width)
    gate_grads, up_grads, down_grads = pl.pallas_call(
        weight_grads,
        grid=(width // step,),
        out_shape=(
            shape((width, units), BF16),
            shape((width, units), BF16),
            shape((units, width), BF16),
        ),
        in_specs=[
            pl.BlockSpec((tokens, step), lambda i: (0, i)),
            whole((tokens, units)),
            whole((tokens, units)),
            whole((tokens, units)),
            pl.BlockSpec((tokens, step), lambda i: (0, i)),
        ],
        out_specs=(
            pl.BlockSpec((step, units), lambda i: (i, 0)),
            pl.BlockSpec((step, units), lambda i: (i, 0)),
            pl.BlockSpec((units, step), lambda i: (0, i)),
        ),
        scratch_shapes=[pltpu.VMEM((units, tokens), BF16)],
        compiler_params=params(BIG),
        cost_estimate=pl.CostEstimate(
            flops=6 * tokens * width * units,
            bytes_accessed=6 * width * units,
            transcendentals=0,
        ),
        name="weight_grads",
    )(normed, d_gate, d_up, hidden, cot)

    input_grads, gain_grads = pl.pallas_call(
        lambda *refs: finish(order, *refs),
        out_shape=(shape((own, width), BF16), shape((1, width), F32)),
        in_specs=[smem()] + [vmem()] * (owners + 3),
        out_specs=(vmem(), vmem()),
        scratch_shapes=[pltpu.VMEM((owners, own, width // own), F32)],
        compiler_params=params(32),
        name="finish",
    )(mine, *deltas, x_own, cot_rows, gain)
    return (
        query_grads,
        passage_grads,
        input_grads[None],
        gate_grads[None],
        up_grads[None],
        down_grads[None],
        gain_grads,
    )


def solution(mesh):
    pair = P(("dp", "segment"), None)
    token = P("segment", "dp", None)
    wide = P("segment", None, "dp")
    return jax.shard_map(
        local,
        mesh=mesh,
        in_specs=(pair, pair, pair, P(), token, token, P("segment", None), wide, wide, token),
        out_specs=(pair, pair, token, wide, wide, token, P("segment", None)),
        check_vma=False,
    )
```

```python
import jax
import jax.numpy as jnp
from jax import lax
from jax.experimental import pallas as pl
from jax.experimental.pallas import tpu as pltpu
from jax.sharding import PartitionSpec as P

HN_BLOCK = 128
TAU = 0.02
HN_WEIGHT = 64.0
EPS_NORM = 1e-06
EPS_RMS = 1e-05

F32 = jnp.float32
BF16 = jnp.bfloat16
MIB = 2**20
WINDOW = 3
BIG = 62
NT = (((1,), (1,)), ((), ()))
TN = (((0,), (0,)), ((), ()))


def vmem():
    return pl.BlockSpec(memory_space=pltpu.VMEM)


def smem():
    return pl.BlockSpec(memory_space=pltpu.SMEM)


def anywhere():
    return pl.BlockSpec(memory_space=pl.ANY)


def params(mib):
    return pltpu.CompilerParams(vmem_limit_bytes=mib * MIB)


def iota(shape, axis):
    return lax.broadcasted_iota(jnp.int32, shape, axis)


def split3(value):
    high = value.astype(BF16).astype(F32)
    rest = value - high
    middle = rest.astype(BF16).astype(F32)
    return high, middle, (rest - middle).astype(BF16).astype(F32)


def to_row(column, width):
    n = column.shape[0]
    pick = iota((n, width), 0) == iota((n, width), 1)
    return jnp.sum(jnp.where(pick, column, 0.0), axis=0, keepdims=True)


def to_columns(rows, n):
    shape = rows.shape[:-2] + (n, rows.shape[-1])
    pick = iota(shape, len(shape) - 2) == iota(shape, len(shape) - 1)
    return jnp.sum(jnp.where(pick, rows, 0.0), axis=-1, keepdims=True)


def row_inverse(ref, rows, mean, eps):
    total = jnp.zeros((rows, 1), F32)
    width = ref.shape[1]
    step = min(width, 1024)
    for at in range(0, width, step):
        part = ref[:, at : at + step].astype(F32)
        total += jnp.sum(part * part, axis=1, keepdims=True)
    if mean:
        total = total / width
    return lax.rsqrt(total + eps)


def pack_rows(query_hbm, passage_hbm, out_ref, query_ref, passage_ref, sems):
    count, block, cols = out_ref.shape
    rows = query_ref.shape[0]
    copies = [
        pltpu.make_async_copy(query_hbm, query_ref, sems.at[0]),
        pltpu.make_async_copy(passage_hbm, passage_ref, sems.at[1]),
    ]
    for copy in copies:
        copy.start()
    copies[0].wait()
    copies[1].wait()
    inverse = jnp.concatenate(
        [
            row_inverse(query_ref, rows, False, EPS_NORM),
            row_inverse(passage_ref, rows, False, EPS_NORM),
        ],
        axis=0,
    )
    terms = [to_row(term, cols) for term in split3(inverse)]
    extra = jnp.concatenate(
        terms + [jnp.zeros((block - 2 * rows - 3, cols), F32)], axis=0
    )
    for peer in range(count):
        cut = slice(peer * cols, (peer + 1) * cols)
        both = jnp.concatenate(
            [
                query_ref[:, cut].astype(F32),
                passage_ref[:, cut].astype(F32),
                extra,
            ],
            axis=0,
        )
        out_ref[peer] = both.astype(BF16)


def partial_scores(rows_ref, out_ref, unit_ref, inverse_ref):
    count, block, cols = rows_ref.shape
    rows = out_ref.shape[1]
    pairs = count * rows
    values = rows_ref[...].astype(F32)
    lines = values[:, 2 * rows : 2 * rows + 1]
    lines = lines + values[:, 2 * rows + 1 : 2 * rows + 2]
    lines = lines + values[:, 2 * rows + 2 : 2 * rows + 3]
    inverse = to_columns(lines, 2 * rows)
    unit = values[:, : 2 * rows] * inverse
    query_unit = unit[:, :rows].reshape(pairs, cols)
    passage_unit = unit[:, rows:].reshape(pairs, cols)
    unit_ref[0] = query_unit
    unit_ref[1] = passage_unit
    inverse_ref[0] = inverse[:, :rows].reshape(pairs, 1)
    inverse_ref[1] = inverse[:, rows:].reshape(pairs, 1)
    scores = lax.dot_general(
        query_unit.astype(BF16), passage_unit.astype(BF16), NT, preferred_element_type=F32
    )
    out_ref[...] = scores.reshape(out_ref.shape)


def softmax_rows(first_ref, parts_ref, offsets_ref, out_ref):
    count, block, pairs = out_ref.shape
    rows = parts_ref.shape[1]
    scores = jnp.sum(parts_ref[...], axis=0) / TAU
    row = first_ref[0] + iota((rows, pairs), 0)
    column = iota((rows, pairs), 1)
    base = row // HN_BLOCK * HN_BLOCK
    offsets = to_columns(offsets_ref[...].astype(F32)[:, None, :], rows).astype(jnp.int32)
    tallies = jnp.zeros((rows, pairs), F32)
    for k in range(offsets_ref.shape[0]):
        tallies += (base + offsets[k] == column).astype(F32)
    weighted = (1.0 + HN_WEIGHT * tallies) * jnp.exp(scores)
    totals = jnp.sum(weighted, axis=1, keepdims=True)
    dscore = weighted / totals - (row == column).astype(F32)
    dscore = dscore.astype(BF16).astype(F32)
    product = dscore * scores
    lines = list(split3(jnp.sum(product, axis=0, keepdims=True)))
    lines += [
        to_row(term, pairs) for term in split3(jnp.sum(product, axis=1, keepdims=True))
    ]
    lines.append(jnp.zeros((block - rows - 6, pairs), F32))
    message = jnp.concatenate([dscore] + lines, axis=0).astype(BF16)
    for peer in range(count):
        out_ref[peer] = message


def pair_grads(first, take, rows_ref, unit_ref, inverse_ref, out_ref):
    count, block, pairs = rows_ref.shape
    rows = pairs // count
    cols = unit_ref.shape[2]
    values = rows_ref[...].astype(F32)
    dscore = values[:, :rows].reshape(pairs, pairs).astype(BF16)
    column_line = jnp.sum(
        values[:, rows] + values[:, rows + 1] + values[:, rows + 2], axis=0, keepdims=True
    )
    column_dots = to_columns(column_line, pairs)
    row_lines = (
        values[:, rows + 3 : rows + 4]
        + values[:, rows + 4 : rows + 5]
        + values[:, rows + 5 : rows + 6]
    )
    row_dots = to_columns(row_lines, rows).reshape(pairs, 1)
    query_unit, passage_unit = unit_ref[0], unit_ref[1]
    query_dir = (
        jnp.dot(dscore, passage_unit.astype(BF16), preferred_element_type=F32) / TAU
    )
    passage_dir = (
        lax.dot_general(dscore, query_unit.astype(BF16), TN, preferred_element_type=F32) / TAU
    )
    query_grad = inverse_ref[0] * (query_dir - query_unit * row_dots)
    passage_grad = inverse_ref[1] * (passage_dir - passage_unit * column_dots)
    pieces = [
        query_grad.reshape(count, rows, cols),
        passage_grad.reshape(count, rows, cols),
    ]
    picked = passage_grad[first : first + take]
    spare = out_ref.shape[1] - 2 * rows - take
    if spare:
        picked = jnp.concatenate([picked, jnp.zeros((spare, cols), F32)], axis=0)
    pieces.append(jnp.broadcast_to(picked[None], (count,) + picked.shape))
    out_ref[...] = jnp.concatenate(pieces, axis=1).astype(BF16)


class Ring:
    def __init__(self, hbm, slots, sems, step):
        self.hbm, self.slots, self.sems, self.step = hbm, slots, sems, step

    def copy(self, c):
        slot = lax.rem(c, WINDOW)
        part = pl.ds(c * self.step, self.step)
        return pltpu.make_async_copy(self.hbm.at[part], self.slots.at[slot], self.sems.at[slot])


def forward(
    near_hbm,
    far_hbm,
    gain_ref,
    gate_hbm,
    up_hbm,
    normed_out,
    gate_out,
    up_out,
    x_s,
    gate_w,
    up_w,
    x_sem,
    gate_sem,
    up_sem,
):
    tokens, width = normed_out.shape
    step = gate_w.shape[1]
    blocks = width // step
    gate_ring = Ring(gate_hbm, gate_w, gate_sem, step)
    up_ring = Ring(up_hbm, up_w, up_sem, step)
    half = tokens // 2
    fetches = [
        pltpu.make_async_copy(near_hbm, x_s.at[pl.ds(0, half)], x_sem.at[0]),
        pltpu.make_async_copy(far_hbm, x_s.at[pl.ds(half, half)], x_sem.at[1]),
    ]
    for fetch in fetches:
        fetch.start()
    for c in range(min(WINDOW, blocks)):
        gate_ring.copy(c).start()
        up_ring.copy(c).start()
    for fetch in fetches:
        fetch.wait()
    x = x_s[...].astype(F32)
    inverse = lax.rsqrt(jnp.sum(x * x, axis=1, keepdims=True) / width + EPS_RMS)
    normed_out[...] = (x * inverse * gain_ref[...]).astype(BF16)

    def block(c, first):
        slot = lax.rem(c, WINDOW)
        cut = pl.ds(pl.multiple_of(c * step, step), step)
        normed = normed_out[:, cut]
        gate_ring.copy(c).wait()
        gate = jnp.dot(normed, gate_w[slot], preferred_element_type=F32)
        gate_out[...] = gate if first else gate_out[...] + gate
        up_ring.copy(c).wait()
        up = jnp.dot(normed, up_w[slot], preferred_element_type=F32)
        up_out[...] = up if first else up_out[...] + up

        @pl.when(c + WINDOW < blocks)
        def _():
            gate_ring.copy(c + WINDOW).start()
            up_ring.copy(c + WINDOW).start()

    def more(c, carry):
        block(c, False)
        return carry

    block(jnp.int32(0), True)
    lax.fori_loop(1, blocks, more, 0)


def delta_columns(cuts, rings, started, x_s, d_gate_t, d_up_t, outs, gain_s, inverse_s):
    owners = len(outs)
    own, total = outs[0].shape
    width = gain_s.shape[1]
    tokens = owners * own
    gate_ring, up_ring = rings
    step = gate_ring.step
    for c in range(started, min(WINDOW, cuts)):
        gate_ring.copy(c).start()
        up_ring.copy(c).start()
    x = x_s[...].astype(F32)
    inverse_s[...] = lax.rsqrt(jnp.sum(x * x, axis=1, keepdims=True) / width + EPS_RMS)

    def one(c, carry):
        slot = lax.rem(c, WINDOW)
        gate_ring.copy(c).wait()
        up_ring.copy(c).wait()
        cut = pl.ds(pl.multiple_of(c * step, step), step)
        delta = (
            jnp.dot(gate_ring.slots[slot], d_gate_t[...], preferred_element_type=F32)
            + jnp.dot(up_ring.slots[slot], d_up_t[...], preferred_element_type=F32)
        ).T
        low = delta.astype(BF16)
        for owner in range(owners):
            outs[owner][:, cut] = low[owner * own : (owner + 1) * own]
        unit = x_s[:, cut].astype(F32) * inverse_s[...]
        gain_s[:, cut] = jnp.sum(delta * unit, axis=0, keepdims=True)

        @pl.when(c + WINDOW < cuts)
        def _():
            gate_ring.copy(c + WINDOW).start()
            up_ring.copy(c + WINDOW).start()

        return carry

    lax.fori_loop(0, cuts, one, 0)
    fold = width // own
    gain = jnp.concatenate(
        [gain_s[:, r * fold : (r + 1) * fold] for r in range(own)], axis=0
    )
    high, low, _ = split3(gain)
    tail = jnp.concatenate([high, low], axis=1).astype(BF16)
    for k in range(owners):
        outs[k][:, width:] = tail


def backward(
    order,
    cuts,
    deep_cuts,
    last_ref,
    mine_ref,
    lengths_ref,
    back_ref,
    x_near,
    x_far,
    cot_near,
    cot_far,
    gate_ref,
    up_ref,
    gate_hbm,
    up_hbm,
    down_hbm,
    query_out,
    passage_out,
    hidden_out,
    d_up_out,
    d_gate_out,
    cot_out,
    cot_own_out,
    *more,
):
    *by_mask, gate_w, up_w, down_w, d_up_t, d_gate_t, x_s, gain_s, inverse_s = more[:-3]
    delta_outs = [by_mask[mask] for mask in order]
    gate_sem, up_sem, down_sem = more[-3:]
    tokens, width = cot_out.shape
    units = gate_ref.shape[1]
    own = delta_outs[0].shape[0]
    deep = units // deep_cuts
    step = gain_s.shape[1] // cuts
    down_ring = Ring(down_hbm, down_w, down_sem, deep)
    gate_ring = Ring(gate_hbm, gate_w, gate_sem, step)
    up_ring = Ring(up_hbm, up_w, up_sem, step)
    early = min(WINDOW, deep_cuts, cuts)
    for c in range(min(WINDOW, deep_cuts)):
        down_ring.copy(c).start()

    count, block, cols = back_ref.shape
    rows = query_out.shape[0]
    passages = block - 2 * rows
    token = jnp.concatenate(
        [iota((own, 1), 0) + (mine_ref[0] ^ mask) * own for mask in order], axis=0
    )
    half = tokens // 2
    x_s[:half, :] = x_near[...]
    x_s[half:, :] = x_far[...]
    lane = iota((tokens, passages), 1)
    start = jnp.int32(0)
    member = jnp.zeros((tokens, passages), F32)
    scale = jnp.zeros((tokens, 1), F32)
    for m in range(lengths_ref.shape[0]):
        length = lengths_ref[m]
        inside = jnp.logical_and(token >= start, token < start + length)
        member = jnp.where(jnp.logical_and(inside, lane == m), 1.0, member)
        scale = jnp.where(inside, 1.0 / (jnp.zeros((tokens, 1), F32) + length.astype(F32)), scale)
        start = start + length
    member = member.astype(BF16)
    last = last_ref[0] == 1
    for peer in range(count):
        cut = slice(peer * cols, (peer + 1) * cols)
        piece = back_ref[peer].astype(F32)
        query_out[:, cut] = piece[:rows].astype(BF16)
        passage_out[:, cut] = piece[rows : 2 * rows].astype(BF16)
        spread = jnp.dot(member, piece[2 * rows :].astype(BF16), preferred_element_type=F32)
        pooled = (spread * scale).astype(BF16)
        given = jnp.concatenate([cot_near[:, cut], cot_far[:, cut]], axis=0)
        cot_out[:, cut] = jnp.where(last, pooled, given)

    cot_own_out[...] = cot_out[:own, :]

    def down_step(c, carry):
        slot = lax.rem(c, WINDOW)
        down_ring.copy(c).wait()
        cut = pl.ds(pl.multiple_of(c * deep, deep), deep)
        d_hidden = lax.dot_general(cot_out[...], down_w[slot], NT, preferred_element_type=F32)
        gate, up = gate_ref[:, cut], up_ref[:, cut]
        sigmoid = jax.nn.sigmoid(gate)
        active = gate * sigmoid
        hidden_out[:, cut] = (active * up).astype(BF16)
        d_up = (d_hidden * active).astype(BF16)
        d_gate = (d_hidden * up * sigmoid * (1.0 + gate * (1.0 - sigmoid))).astype(BF16)
        d_up_out[:, cut] = d_up
        d_gate_out[:, cut] = d_gate
        d_up_t[cut, :] = d_up.T
        d_gate_t[cut, :] = d_gate.T
        ahead = c + WINDOW

        @pl.when(ahead < deep_cuts)
        def _():
            down_ring.copy(ahead).start()

        late = c - (deep_cuts - early)

        @pl.when(late >= 0)
        def _():
            gate_ring.copy(late).start()
            up_ring.copy(late).start()

        return carry

    lax.fori_loop(0, deep_cuts, down_step, 0)
    delta_columns(
        cuts,
        (gate_ring, up_ring),
        early,
        x_s,
        d_gate_t,
        d_up_t,
        delta_outs,
        gain_s,
        inverse_s,
    )


def weight_grads(
    normed_ref, d_gate_ref, d_up_ref, hidden_ref, cot_ref, gate_out, up_out, down_out, hidden_t
):
    @pl.when(pl.program_id(0) == 0)
    def _():
        hidden_t[...] = hidden_ref[...].T

    gate_out[...] = lax.dot_general(
        normed_ref[...], d_gate_ref[...], TN, preferred_element_type=F32
    ).astype(BF16)
    up_out[...] = lax.dot_general(
        normed_ref[...], d_up_ref[...], TN, preferred_element_type=F32
    ).astype(BF16)
    down_out[...] = jnp.dot(
        hidden_t[...], cot_ref[...], preferred_element_type=F32
    ).astype(BF16)


def finish(mine_ref, *refs):
    *part_refs, x_ref, cot_ref, gain_ref, input_out, gain_out, tail_s = refs
    owners = len(part_refs)
    own, width = x_ref.shape
    fold = width // own
    for k in range(owners):
        tail = part_refs[k][:, width:].astype(F32)
        tail_s[mine_ref[0] ^ k] = tail[:, :fold] + tail[:, fold:]
    gain = tail_s[0]
    for p in range(1, owners):
        gain += tail_s[p]
    for r in range(own):
        gain_out[:, r * fold : (r + 1) * fold] = gain[r : r + 1]
    delta = part_refs[0][:, :width].astype(F32)
    for k in range(1, owners):
        delta += part_refs[k][:, :width].astype(F32)
    inverse = row_inverse(x_ref, own, True, EPS_RMS)
    unit = x_ref[...].astype(F32) * inverse
    scaled = delta * gain_ref[...]
    mean = jnp.sum(scaled * unit, axis=1, keepdims=True) / width
    input_out[...] = (
        cot_ref[...].astype(F32) + inverse * (scaled - unit * mean)
    ).astype(BF16)


def shape(dims, dtype):
    return jax.ShapeDtypeStruct(dims, dtype)


def local(
    query_cache,
    passage_cache,
    hard_offsets,
    passage_lengths,
    segment_inputs,
    segment_cotangents,
    norm_gain,
    gate_weight,
    up_weight,
    down_weight,
):
    everyone = ("dp", "segment")
    count = lax.axis_size(everyone)
    owners = lax.axis_size("dp")
    sections = lax.axis_size("segment")
    rows, width = query_cache.shape
    pairs = rows * count
    cols = width // count
    passages = passage_lengths.shape[0]
    own = segment_inputs.shape[1]
    tokens = own * owners
    units = gate_weight.shape[2]
    room = min(BIG, 45 + tokens // 16)
    section = lax.axis_index("segment")
    dp = lax.axis_index("dp")
    first_row = (lax.axis_index(everyone) * rows).astype(jnp.int32).reshape(1)
    is_last = (section == sections - 1).astype(jnp.int32).reshape(1)
    mine = dp.astype(jnp.int32).reshape(1)

    assert owners & (owners - 1) == 0 and owners > 1
    x_own, cot_own, gain = segment_inputs[0], segment_cotangents[0], norm_gain
    block1 = 4 * rows
    message = pl.pallas_call(
        pack_rows,
        out_shape=shape((count, block1, cols), BF16),
        in_specs=[anywhere()] * 2,
        out_specs=vmem(),
        scratch_shapes=[
            pltpu.VMEM((rows, width), BF16),
            pltpu.VMEM((rows, width), BF16),
            pltpu.SemaphoreType.DMA((2,)),
        ],
        compiler_params=params(BIG),
        name="pack_rows",
    )(query_cache, passage_cache)
    order = [0]
    x_half, cot_half = x_own, cot_own
    moved = []

    def double(values):
        nonlocal x_half, cot_half
        if len(order) == owners:
            return values
        if moved:
            x_half = jnp.concatenate([x_half, moved[0]], axis=0)
            cot_half = jnp.concatenate([cot_half, moved[1]], axis=0)
        mask = owners // 2 // len(order)
        swap = [(i, i ^ mask) for i in range(owners)]
        x_far = lax.ppermute(x_half, "dp", swap)
        if mask == 1:
            x_far, cot_half = lax.optimization_barrier((x_far, cot_half))
        moved[:] = [x_far, lax.ppermute(cot_half, "dp", swap)]
        order.extend([o ^ mask for o in order])
        return values

    message = double(message)
    message = lax.all_to_all(message, everyone, 0, 0, tiled=True)
    message = double(message)
    parts, unit, inverse = pl.pallas_call(
        partial_scores,
        out_shape=(
            shape((count, rows, pairs), F32),
            shape((2, pairs, cols), F32),
            shape((2, pairs, 1), F32),
        ),
        in_specs=[vmem()],
        out_specs=(vmem(), vmem(), vmem()),
        compiler_params=params(32),
        name="partial_scores",
    )(message)
    parts = lax.all_to_all(parts, everyone, 0, 0, tiled=True)
    parts = double(parts)
    message = pl.pallas_call(
        softmax_rows,
        out_shape=shape((count, 2 * rows, pairs), BF16),
        in_specs=[smem(), vmem(), vmem()],
        out_specs=vmem(),
        compiler_params=params(32),
        name="softmax_rows",
    )(first_row, parts, hard_offsets.T)
    message = lax.all_to_all(message, everyone, 0, 0, tiled=True)
    back = -(-(2 * rows + passages) // 16) * 16
    message = pl.pallas_call(
        lambda *refs: pair_grads((sections - 1) * rows, passages, *refs),
        out_shape=shape((count, back, cols), BF16),
        in_specs=[vmem(), vmem(), vmem()],
        out_specs=vmem(),
        compiler_params=params(48),
        name="pair_grads",
    )(message, unit, inverse)
    message = lax.all_to_all(message, everyone, 0, 0, tiled=True)

    while len(order) < owners:
        message = double(message)
    halves = (x_half, moved[0], cot_half, moved[1])
    whole = lambda dims: pl.BlockSpec(dims, lambda i: (0,) * len(dims))
    ring = pltpu.SemaphoreType.DMA((WINDOW,))
    step = min(512, width)
    normed, gate, up = pl.pallas_call(
        forward,
        out_shape=(
            shape((tokens, width), BF16),
            shape((tokens, units), F32),
            shape((tokens, units), F32),
        ),
        in_specs=[anywhere(), anywhere(), vmem(), anywhere(), anywhere()],
        out_specs=(vmem(), vmem(), vmem()),
        scratch_shapes=[
            pltpu.VMEM((tokens, width), BF16),
            pltpu.VMEM((WINDOW, step, units), BF16),
            pltpu.VMEM((WINDOW, step, units), BF16),
            pltpu.SemaphoreType.DMA((2,)),
            ring,
            ring,
        ],
        compiler_params=params(room),
        cost_estimate=pl.CostEstimate(
            flops=4 * tokens * width * units,
            bytes_accessed=4 * width * units,
            transcendentals=0,
        ),
        name="forward",
    )(*halves[:2], gain, gate_weight[0], up_weight[0])

    cuts = max(1, width // 512)
    deep_cuts = units // 256 if units % 256 == 0 else 1
    part_shape = shape((own, width + 2 * (width // own)), BF16)
    block = (WINDOW, width // cuts, units)
    outs = pl.pallas_call(
        lambda *refs: backward(order, cuts, deep_cuts, *refs),
        out_shape=(
            shape((rows, width), BF16),
            shape((rows, width), BF16),
            shape((tokens, units), BF16),
            shape((tokens, units), BF16),
            shape((tokens, units), BF16),
            shape((tokens, width), BF16),
            shape((own, width), BF16),
        )
        + (part_shape,) * owners,
        in_specs=[smem(), smem(), smem()] + [vmem()] * 7 + [anywhere()] * 3,
        out_specs=tuple(vmem() for _ in range(7 + owners)),
        scratch_shapes=[
            pltpu.VMEM(block, BF16),
            pltpu.VMEM(block, BF16),
            pltpu.VMEM((WINDOW, units // deep_cuts, width), BF16),
            pltpu.VMEM((units, tokens), BF16),
            pltpu.VMEM((units, tokens), BF16),
            pltpu.VMEM((tokens, width), BF16),
            pltpu.VMEM((1, width), F32),
            pltpu.VMEM((tokens, 1), F32),
            ring,
            ring,
            ring,
        ],
        compiler_params=params(room),
        cost_estimate=pl.CostEstimate(
            flops=6 * tokens * width * units,
            bytes_accessed=6 * width * units,
            transcendentals=tokens * units,
        ),
        name="backward",
    )(
        is_last,
        mine,
        passage_lengths,
        message,
        *halves,
        gate,
        up,
        gate_weight[0],
        up_weight[0],
        down_weight[0],
    )
    query_grads, passage_grads, hidden, d_up, d_gate, cot, cot_rows = outs[:7]
    by_mask = list(outs[7:])
    for mask in range(1, owners):
        by_mask[mask] = lax.ppermute(
            by_mask[mask], "dp", [(i, i ^ mask) for i in range(owners)]
        )

    step = min(512, width)
    gate_grads, up_grads, down_grads = pl.pallas_call(
        weight_grads,
        grid=(width // step,),
        out_shape=(
            shape((width, units), BF16),
            shape((width, units), BF16),
            shape((units, width), BF16),
        ),
        in_specs=[
            pl.BlockSpec((tokens, step), lambda i: (0, i)),
            whole((tokens, units)),
            whole((tokens, units)),
            whole((tokens, units)),
            pl.BlockSpec((tokens, step), lambda i: (0, i)),
        ],
        out_specs=(
            pl.BlockSpec((step, units), lambda i: (i, 0)),
            pl.BlockSpec((step, units), lambda i: (i, 0)),
            pl.BlockSpec((units, step), lambda i: (0, i)),
        ),
        scratch_shapes=[pltpu.VMEM((units, tokens), BF16)],
        compiler_params=params(BIG),
        cost_estimate=pl.CostEstimate(
            flops=6 * tokens * width * units,
            bytes_accessed=6 * width * units,
            transcendentals=0,
        ),
        name="weight_grads",
    )(normed, d_gate, d_up, hidden, cot)

    input_grads, gain_grads = pl.pallas_call(
        finish,
        out_shape=(shape((own, width), BF16), shape((1, width), F32)),
        in_specs=[smem()] + [vmem()] * (owners + 3),
        out_specs=(vmem(), vmem()),
        scratch_shapes=[pltpu.VMEM((owners, own, width // own), F32)],
        compiler_params=params(32),
        name="finish",
    )(mine, *by_mask, x_own, cot_rows, gain)
    return (
        query_grads,
        passage_grads,
        input_grads[None],
        gate_grads[None],
        up_grads[None],
        down_grads[None],
        gain_grads,
    )


def solution(mesh):
    pair = P(("dp", "segment"), None)
    token = P("segment", "dp", None)
    wide = P("segment", None, "dp")
    return jax.shard_map(
        local,
        mesh=mesh,
        in_specs=(pair, pair, pair, P(), token, token, P("segment", None), wide, wide, token),
        out_specs=(pair, pair, token, wide, wide, token, P("segment", None)),
        check_vma=False,
    )
```

```python
import jax
import jax.numpy as jnp
from jax import lax
from jax.experimental import pallas as pl
from jax.experimental.pallas import tpu as pltpu
from jax.sharding import PartitionSpec as P

HN_BLOCK = 128
TAU = 0.02
HN_WEIGHT = 64.0
EPS_NORM = 1e-06
EPS_RMS = 1e-05

F32 = jnp.float32
BF16 = jnp.bfloat16
MIB = 2**20
WINDOW = 3
BIG = 62
NT = (((1,), (1,)), ((), ()))
TN = (((0,), (0,)), ((), ()))


def vmem():
    return pl.BlockSpec(memory_space=pltpu.VMEM)


def smem():
    return pl.BlockSpec(memory_space=pltpu.SMEM)


def anywhere():
    return pl.BlockSpec(memory_space=pl.ANY)


def params(mib):
    return pltpu.CompilerParams(vmem_limit_bytes=mib * MIB)


def iota(shape, axis):
    return lax.broadcasted_iota(jnp.int32, shape, axis)


def split3(value):
    high = value.astype(BF16).astype(F32)
    rest = value - high
    middle = rest.astype(BF16).astype(F32)
    return high, middle, (rest - middle).astype(BF16).astype(F32)


def to_row(column, width):
    n = column.shape[0]
    pick = iota((n, width), 0) == iota((n, width), 1)
    return jnp.sum(jnp.where(pick, column, 0.0), axis=0, keepdims=True)


def to_columns(rows, n):
    shape = rows.shape[:-2] + (n, rows.shape[-1])
    pick = iota(shape, len(shape) - 2) == iota(shape, len(shape) - 1)
    return jnp.sum(jnp.where(pick, rows, 0.0), axis=-1, keepdims=True)


def row_inverse(ref, rows, mean, eps):
    total = jnp.zeros((rows, 1), F32)
    width = ref.shape[1]
    step = min(width, 1024)
    for at in range(0, width, step):
        part = ref[:, at : at + step].astype(F32)
        total += jnp.sum(part * part, axis=1, keepdims=True)
    if mean:
        total = total / width
    return lax.rsqrt(total + eps)


def pack_rows(query_hbm, passage_hbm, out_ref, query_ref, passage_ref, sems):
    count, block, cols = out_ref.shape
    rows = query_ref.shape[0]
    copies = [
        pltpu.make_async_copy(query_hbm, query_ref, sems.at[0]),
        pltpu.make_async_copy(passage_hbm, passage_ref, sems.at[1]),
    ]
    for copy in copies:
        copy.start()
    copies[0].wait()
    copies[1].wait()
    inverse = jnp.concatenate(
        [
            row_inverse(query_ref, rows, False, EPS_NORM),
            row_inverse(passage_ref, rows, False, EPS_NORM),
        ],
        axis=0,
    )
    terms = [to_row(term, cols) for term in split3(inverse)]
    extra = jnp.concatenate(
        terms + [jnp.zeros((block - 2 * rows - 3, cols), F32)], axis=0
    )
    for peer in range(count):
        cut = slice(peer * cols, (peer + 1) * cols)
        both = jnp.concatenate(
            [
                query_ref[:, cut].astype(F32),
                passage_ref[:, cut].astype(F32),
                extra,
            ],
            axis=0,
        )
        out_ref[peer] = both.astype(BF16)


def partial_scores(rows_ref, out_ref, unit_ref, inverse_ref):
    count, block, cols = rows_ref.shape
    rows = out_ref.shape[1]
    pairs = count * rows
    values = rows_ref[...].astype(F32)
    lines = values[:, 2 * rows : 2 * rows + 1]
    lines = lines + values[:, 2 * rows + 1 : 2 * rows + 2]
    lines = lines + values[:, 2 * rows + 2 : 2 * rows + 3]
    inverse = to_columns(lines, 2 * rows)
    unit = values[:, : 2 * rows] * inverse
    query_unit = unit[:, :rows].reshape(pairs, cols)
    passage_unit = unit[:, rows:].reshape(pairs, cols)
    unit_ref[0] = query_unit
    unit_ref[1] = passage_unit
    inverse_ref[0] = inverse[:, :rows].reshape(pairs, 1)
    inverse_ref[1] = inverse[:, rows:].reshape(pairs, 1)
    scores = lax.dot_general(
        query_unit.astype(BF16), passage_unit.astype(BF16), NT, preferred_element_type=F32
    )
    out_ref[...] = scores.reshape(out_ref.shape)


def softmax_rows(first_ref, parts_ref, offsets_ref, out_ref):
    count, block, pairs = out_ref.shape
    rows = parts_ref.shape[1]
    scores = jnp.sum(parts_ref[...], axis=0) / TAU
    row = first_ref[0] + iota((rows, pairs), 0)
    column = iota((rows, pairs), 1)
    base = row // HN_BLOCK * HN_BLOCK
    offsets = to_columns(offsets_ref[...].astype(F32)[:, None, :], rows).astype(jnp.int32)
    tallies = jnp.zeros((rows, pairs), F32)
    for k in range(offsets_ref.shape[0]):
        tallies += (base + offsets[k] == column).astype(F32)
    weighted = (1.0 + HN_WEIGHT * tallies) * jnp.exp(scores)
    totals = jnp.sum(weighted, axis=1, keepdims=True)
    dscore = weighted / totals - (row == column).astype(F32)
    dscore = dscore.astype(BF16).astype(F32)
    product = dscore * scores
    lines = list(split3(jnp.sum(product, axis=0, keepdims=True)))
    lines += [
        to_row(term, pairs) for term in split3(jnp.sum(product, axis=1, keepdims=True))
    ]
    lines.append(jnp.zeros((block - rows - 6, pairs), F32))
    message = jnp.concatenate([dscore] + lines, axis=0).astype(BF16)
    for peer in range(count):
        out_ref[peer] = message


def pair_grads(first, take, rows_ref, unit_ref, inverse_ref, out_ref):
    count, block, pairs = rows_ref.shape
    rows = pairs // count
    cols = unit_ref.shape[2]
    values = rows_ref[...].astype(F32)
    dscore = values[:, :rows].reshape(pairs, pairs).astype(BF16)
    column_line = jnp.sum(
        values[:, rows] + values[:, rows + 1] + values[:, rows + 2], axis=0, keepdims=True
    )
    column_dots = to_columns(column_line, pairs)
    row_lines = (
        values[:, rows + 3 : rows + 4]
        + values[:, rows + 4 : rows + 5]
        + values[:, rows + 5 : rows + 6]
    )
    row_dots = to_columns(row_lines, rows).reshape(pairs, 1)
    query_unit, passage_unit = unit_ref[0], unit_ref[1]
    query_dir = (
        jnp.dot(dscore, passage_unit.astype(BF16), preferred_element_type=F32) / TAU
    )
    passage_dir = (
        lax.dot_general(dscore, query_unit.astype(BF16), TN, preferred_element_type=F32) / TAU
    )
    query_grad = inverse_ref[0] * (query_dir - query_unit * row_dots)
    passage_grad = inverse_ref[1] * (passage_dir - passage_unit * column_dots)
    pieces = [
        query_grad.reshape(count, rows, cols),
        passage_grad.reshape(count, rows, cols),
    ]
    picked = passage_grad[first : first + take]
    spare = out_ref.shape[1] - 2 * rows - take
    if spare:
        picked = jnp.concatenate([picked, jnp.zeros((spare, cols), F32)], axis=0)
    pieces.append(jnp.broadcast_to(picked[None], (count,) + picked.shape))
    out_ref[...] = jnp.concatenate(pieces, axis=1).astype(BF16)


class Ring:
    def __init__(self, hbm, slots, sems, step):
        self.hbm, self.slots, self.sems, self.step = hbm, slots, sems, step

    def copy(self, c):
        slot = lax.rem(c, WINDOW)
        part = pl.ds(c * self.step, self.step)
        return pltpu.make_async_copy(self.hbm.at[part], self.slots.at[slot], self.sems.at[slot])


def forward(
    near_hbm,
    far_hbm,
    gain_ref,
    gate_hbm,
    up_hbm,
    normed_out,
    gate_out,
    up_out,
    x_s,
    gate_w,
    up_w,
    x_sem,
    gate_sem,
    up_sem,
):
    tokens, width = normed_out.shape
    step = gate_w.shape[1]
    blocks = width // step
    gate_ring = Ring(gate_hbm, gate_w, gate_sem, step)
    up_ring = Ring(up_hbm, up_w, up_sem, step)
    half = tokens // 2
    fetches = [
        pltpu.make_async_copy(near_hbm, x_s.at[pl.ds(0, half)], x_sem.at[0]),
        pltpu.make_async_copy(far_hbm, x_s.at[pl.ds(half, half)], x_sem.at[1]),
    ]
    for fetch in fetches:
        fetch.start()
    for c in range(min(WINDOW, blocks)):
        gate_ring.copy(c).start()
        up_ring.copy(c).start()
    for fetch in fetches:
        fetch.wait()
    x = x_s[...].astype(F32)
    inverse = lax.rsqrt(jnp.sum(x * x, axis=1, keepdims=True) / width + EPS_RMS)
    normed_out[...] = (x * inverse * gain_ref[...]).astype(BF16)

    def block(c, first):
        slot = lax.rem(c, WINDOW)
        cut = pl.ds(pl.multiple_of(c * step, step), step)
        normed = normed_out[:, cut]
        gate_ring.copy(c).wait()
        gate = jnp.dot(normed, gate_w[slot], preferred_element_type=F32)
        gate_out[...] = gate if first else gate_out[...] + gate
        up_ring.copy(c).wait()
        up = jnp.dot(normed, up_w[slot], preferred_element_type=F32)
        up_out[...] = up if first else up_out[...] + up

        @pl.when(c + WINDOW < blocks)
        def _():
            gate_ring.copy(c + WINDOW).start()
            up_ring.copy(c + WINDOW).start()

    def more(c, carry):
        block(c, False)
        return carry

    block(jnp.int32(0), True)
    lax.fori_loop(1, blocks, more, 0)


def delta_columns(cuts, rings, started, x_s, d_gate_t, d_up_t, outs, gain_s, inverse_s):
    owners = len(outs)
    own, total = outs[0].shape
    width = gain_s.shape[1]
    tokens = owners * own
    gate_ring, up_ring = rings
    step = gate_ring.step
    for c in range(started, min(WINDOW, cuts)):
        gate_ring.copy(c).start()
        up_ring.copy(c).start()
    x = x_s[...].astype(F32)
    inverse_s[...] = lax.rsqrt(jnp.sum(x * x, axis=1, keepdims=True) / width + EPS_RMS)

    def one(c, carry):
        slot = lax.rem(c, WINDOW)
        gate_ring.copy(c).wait()
        up_ring.copy(c).wait()
        cut = pl.ds(pl.multiple_of(c * step, step), step)
        delta = (
            jnp.dot(gate_ring.slots[slot], d_gate_t[...], preferred_element_type=F32)
            + jnp.dot(up_ring.slots[slot], d_up_t[...], preferred_element_type=F32)
        ).T
        low = delta.astype(BF16)
        for owner in range(owners):
            outs[owner][:, cut] = low[owner * own : (owner + 1) * own]
        unit = x_s[:, cut].astype(F32) * inverse_s[...]
        gain_s[:, cut] = jnp.sum(delta * unit, axis=0, keepdims=True)

        @pl.when(c + WINDOW < cuts)
        def _():
            gate_ring.copy(c + WINDOW).start()
            up_ring.copy(c + WINDOW).start()

        return carry

    lax.fori_loop(0, cuts, one, 0)
    fold = width // own
    gain = jnp.concatenate(
        [gain_s[:, r * fold : (r + 1) * fold] for r in range(own)], axis=0
    )
    for k in range(owners):
        outs[k][:, width:] = gain.astype(BF16)


def backward(
    order,
    cuts,
    deep_cuts,
    last_ref,
    mine_ref,
    lengths_ref,
    back_ref,
    x_near,
    x_far,
    cot_near,
    cot_far,
    gate_ref,
    up_ref,
    gate_hbm,
    up_hbm,
    down_hbm,
    query_out,
    passage_out,
    hidden_out,
    d_up_out,
    d_gate_out,
    cot_out,
    cot_own_out,
    *more,
):
    *by_mask, gate_w, up_w, down_w, d_up_t, d_gate_t, x_s, gain_s, inverse_s = more[:-3]
    delta_outs = [by_mask[mask] for mask in order]
    gate_sem, up_sem, down_sem = more[-3:]
    tokens, width = cot_out.shape
    units = gate_ref.shape[1]
    own = delta_outs[0].shape[0]
    deep = units // deep_cuts
    step = gain_s.shape[1] // cuts
    down_ring = Ring(down_hbm, down_w, down_sem, deep)
    gate_ring = Ring(gate_hbm, gate_w, gate_sem, step)
    up_ring = Ring(up_hbm, up_w, up_sem, step)
    early = min(WINDOW, deep_cuts, cuts)
    for c in range(min(WINDOW, deep_cuts)):
        down_ring.copy(c).start()

    count, block, cols = back_ref.shape
    rows = query_out.shape[0]
    passages = block - 2 * rows
    token = jnp.concatenate(
        [iota((own, 1), 0) + (mine_ref[0] ^ mask) * own for mask in order], axis=0
    )
    half = tokens // 2
    x_s[:half, :] = x_near[...]
    x_s[half:, :] = x_far[...]
    lane = iota((tokens, passages), 1)
    start = jnp.int32(0)
    member = jnp.zeros((tokens, passages), F32)
    scale = jnp.zeros((tokens, 1), F32)
    for m in range(lengths_ref.shape[0]):
        length = lengths_ref[m]
        inside = jnp.logical_and(token >= start, token < start + length)
        member = jnp.where(jnp.logical_and(inside, lane == m), 1.0, member)
        scale = jnp.where(inside, 1.0 / (jnp.zeros((tokens, 1), F32) + length.astype(F32)), scale)
        start = start + length
    member = member.astype(BF16)
    last = last_ref[0] == 1
    for peer in range(count):
        cut = slice(peer * cols, (peer + 1) * cols)
        piece = back_ref[peer].astype(F32)
        query_out[:, cut] = piece[:rows].astype(BF16)
        passage_out[:, cut] = piece[rows : 2 * rows].astype(BF16)
        spread = jnp.dot(member, piece[2 * rows :].astype(BF16), preferred_element_type=F32)
        pooled = (spread * scale).astype(BF16)
        given = jnp.concatenate([cot_near[:, cut], cot_far[:, cut]], axis=0)
        cot_out[:, cut] = jnp.where(last, pooled, given)

    cot_own_out[...] = cot_out[:own, :]

    def down_step(c, carry):
        slot = lax.rem(c, WINDOW)
        down_ring.copy(c).wait()
        cut = pl.ds(pl.multiple_of(c * deep, deep), deep)
        d_hidden = lax.dot_general(cot_out[...], down_w[slot], NT, preferred_element_type=F32)
        gate, up = gate_ref[:, cut], up_ref[:, cut]
        sigmoid = jax.nn.sigmoid(gate)
        active = gate * sigmoid
        hidden_out[:, cut] = (active * up).astype(BF16)
        d_up = (d_hidden * active).astype(BF16)
        d_gate = (d_hidden * up * sigmoid * (1.0 + gate * (1.0 - sigmoid))).astype(BF16)
        d_up_out[:, cut] = d_up
        d_gate_out[:, cut] = d_gate
        d_up_t[cut, :] = d_up.T
        d_gate_t[cut, :] = d_gate.T
        ahead = c + WINDOW

        @pl.when(ahead < deep_cuts)
        def _():
            down_ring.copy(ahead).start()

        late = c - (deep_cuts - early)

        @pl.when(late >= 0)
        def _():
            gate_ring.copy(late).start()
            up_ring.copy(late).start()

        return carry

    lax.fori_loop(0, deep_cuts, down_step, 0)
    delta_columns(
        cuts,
        (gate_ring, up_ring),
        early,
        x_s,
        d_gate_t,
        d_up_t,
        delta_outs,
        gain_s,
        inverse_s,
    )


def weight_grads(
    normed_ref, d_gate_ref, d_up_ref, hidden_ref, cot_ref, gate_out, up_out, down_out, hidden_t
):
    @pl.when(pl.program_id(0) == 0)
    def _():
        hidden_t[...] = hidden_ref[...].T

    gate_out[...] = lax.dot_general(
        normed_ref[...], d_gate_ref[...], TN, preferred_element_type=F32
    ).astype(BF16)
    up_out[...] = lax.dot_general(
        normed_ref[...], d_up_ref[...], TN, preferred_element_type=F32
    ).astype(BF16)
    down_out[...] = jnp.dot(
        hidden_t[...], cot_ref[...], preferred_element_type=F32
    ).astype(BF16)


def finish(mine_ref, *refs):
    *part_refs, x_ref, cot_ref, gain_ref, input_out, gain_out, tail_s = refs
    owners = len(part_refs)
    own, width = x_ref.shape
    fold = width // own
    for k in range(owners):
        tail_s[mine_ref[0] ^ k] = part_refs[k][:, width:].astype(F32)
    gain = tail_s[0]
    for p in range(1, owners):
        gain += tail_s[p]
    for r in range(own):
        gain_out[:, r * fold : (r + 1) * fold] = gain[r : r + 1]
    delta = part_refs[0][:, :width].astype(F32)
    for k in range(1, owners):
        delta += part_refs[k][:, :width].astype(F32)
    inverse = row_inverse(x_ref, own, True, EPS_RMS)
    unit = x_ref[...].astype(F32) * inverse
    scaled = delta * gain_ref[...]
    mean = jnp.sum(scaled * unit, axis=1, keepdims=True) / width
    input_out[...] = (
        cot_ref[...].astype(F32) + inverse * (scaled - unit * mean)
    ).astype(BF16)


def shape(dims, dtype):
    return jax.ShapeDtypeStruct(dims, dtype)


def local(
    query_cache,
    passage_cache,
    hard_offsets,
    passage_lengths,
    segment_inputs,
    segment_cotangents,
    norm_gain,
    gate_weight,
    up_weight,
    down_weight,
):
    everyone = ("dp", "segment")
    count = lax.axis_size(everyone)
    owners = lax.axis_size("dp")
    sections = lax.axis_size("segment")
    rows, width = query_cache.shape
    pairs = rows * count
    cols = width // count
    passages = passage_lengths.shape[0]
    own = segment_inputs.shape[1]
    tokens = own * owners
    units = gate_weight.shape[2]
    room = min(BIG, 45 + tokens // 16)
    section = lax.axis_index("segment")
    dp = lax.axis_index("dp")
    first_row = (lax.axis_index(everyone) * rows).astype(jnp.int32).reshape(1)
    is_last = (section == sections - 1).astype(jnp.int32).reshape(1)
    mine = dp.astype(jnp.int32).reshape(1)

    assert owners & (owners - 1) == 0 and owners > 1
    x_own, cot_own, gain = segment_inputs[0], segment_cotangents[0], norm_gain
    block1 = 4 * rows
    message = pl.pallas_call(
        pack_rows,
        out_shape=shape((count, block1, cols), BF16),
        in_specs=[anywhere()] * 2,
        out_specs=vmem(),
        scratch_shapes=[
            pltpu.VMEM((rows, width), BF16),
            pltpu.VMEM((rows, width), BF16),
            pltpu.SemaphoreType.DMA((2,)),
        ],
        compiler_params=params(BIG),
        name="pack_rows",
    )(query_cache, passage_cache)
    order = [0]
    x_half, cot_half = x_own, cot_own
    moved = []

    def double(values):
        nonlocal x_half, cot_half
        if len(order) == owners:
            return values
        if moved:
            x_half = jnp.concatenate([x_half, moved[0]], axis=0)
            cot_half = jnp.concatenate([cot_half, moved[1]], axis=0)
        mask = owners // 2 // len(order)
        swap = [(i, i ^ mask) for i in range(owners)]
        x_far = lax.ppermute(x_half, "dp", swap)
        if mask == 1:
            x_far, cot_half = lax.optimization_barrier((x_far, cot_half))
        moved[:] = [x_far, lax.ppermute(cot_half, "dp", swap)]
        order.extend([o ^ mask for o in order])
        return values

    message = double(message)
    message = lax.all_to_all(message, everyone, 0, 0, tiled=True)
    message = double(message)
    parts, unit, inverse = pl.pallas_call(
        partial_scores,
        out_shape=(
            shape((count, rows, pairs), F32),
            shape((2, pairs, cols), F32),
            shape((2, pairs, 1), F32),
        ),
        in_specs=[vmem()],
        out_specs=(vmem(), vmem(), vmem()),
        compiler_params=params(32),
        name="partial_scores",
    )(message)
    parts = lax.all_to_all(parts, everyone, 0, 0, tiled=True)
    parts = double(parts)
    message = pl.pallas_call(
        softmax_rows,
        out_shape=shape((count, 2 * rows, pairs), BF16),
        in_specs=[smem(), vmem(), vmem()],
        out_specs=vmem(),
        compiler_params=params(32),
        name="softmax_rows",
    )(first_row, parts, hard_offsets.T)
    message = lax.all_to_all(message, everyone, 0, 0, tiled=True)
    back = -(-(2 * rows + passages) // 16) * 16
    message = pl.pallas_call(
        lambda *refs: pair_grads((sections - 1) * rows, passages, *refs),
        out_shape=shape((count, back, cols), BF16),
        in_specs=[vmem(), vmem(), vmem()],
        out_specs=vmem(),
        compiler_params=params(48),
        name="pair_grads",
    )(message, unit, inverse)
    message = lax.all_to_all(message, everyone, 0, 0, tiled=True)

    while len(order) < owners:
        message = double(message)
    halves = (x_half, moved[0], cot_half, moved[1])
    whole = lambda dims: pl.BlockSpec(dims, lambda i: (0,) * len(dims))
    ring = pltpu.SemaphoreType.DMA((WINDOW,))
    step = min(512, width)
    normed, gate, up = pl.pallas_call(
        forward,
        out_shape=(
            shape((tokens, width), BF16),
            shape((tokens, units), F32),
            shape((tokens, units), F32),
        ),
        in_specs=[anywhere(), anywhere(), vmem(), anywhere(), anywhere()],
        out_specs=(vmem(), vmem(), vmem()),
        scratch_shapes=[
            pltpu.VMEM((tokens, width), BF16),
            pltpu.VMEM((WINDOW, step, units), BF16),
            pltpu.VMEM((WINDOW, step, units), BF16),
            pltpu.SemaphoreType.DMA((2,)),
            ring,
            ring,
        ],
        compiler_params=params(room),
        cost_estimate=pl.CostEstimate(
            flops=4 * tokens * width * units,
            bytes_accessed=4 * width * units,
            transcendentals=0,
        ),
        name="forward",
    )(*halves[:2], gain, gate_weight[0], up_weight[0])

    cuts = max(1, width // 512)
    deep_cuts = units // 256 if units % 256 == 0 else 1
    part_shape = shape((own, width + width // own), BF16)
    block = (WINDOW, width // cuts, units)
    outs = pl.pallas_call(
        lambda *refs: backward(order, cuts, deep_cuts, *refs),
        out_shape=(
            shape((rows, width), BF16),
            shape((rows, width), BF16),
            shape((tokens, units), BF16),
            shape((tokens, units), BF16),
            shape((tokens, units), BF16),
            shape((tokens, width), BF16),
            shape((own, width), BF16),
        )
        + (part_shape,) * owners,
        in_specs=[smem(), smem(), smem()] + [vmem()] * 7 + [anywhere()] * 3,
        out_specs=tuple(vmem() for _ in range(7 + owners)),
        scratch_shapes=[
            pltpu.VMEM(block, BF16),
            pltpu.VMEM(block, BF16),
            pltpu.VMEM((WINDOW, units // deep_cuts, width), BF16),
            pltpu.VMEM((units, tokens), BF16),
            pltpu.VMEM((units, tokens), BF16),
            pltpu.VMEM((tokens, width), BF16),
            pltpu.VMEM((1, width), F32),
            pltpu.VMEM((tokens, 1), F32),
            ring,
            ring,
            ring,
        ],
        compiler_params=params(room),
        cost_estimate=pl.CostEstimate(
            flops=6 * tokens * width * units,
            bytes_accessed=6 * width * units,
            transcendentals=tokens * units,
        ),
        name="backward",
    )(
        is_last,
        mine,
        passage_lengths,
        message,
        *halves,
        gate,
        up,
        gate_weight[0],
        up_weight[0],
        down_weight[0],
    )
    query_grads, passage_grads, hidden, d_up, d_gate, cot, cot_rows = outs[:7]
    by_mask = list(outs[7:])
    for mask in range(1, owners):
        by_mask[mask] = lax.ppermute(
            by_mask[mask], "dp", [(i, i ^ mask) for i in range(owners)]
        )

    step = min(512, width)
    gate_grads, up_grads, down_grads = pl.pallas_call(
        weight_grads,
        grid=(width // step,),
        out_shape=(
            shape((width, units), BF16),
            shape((width, units), BF16),
            shape((units, width), BF16),
        ),
        in_specs=[
            pl.BlockSpec((tokens, step), lambda i: (0, i)),
            whole((tokens, units)),
            whole((tokens, units)),
            whole((tokens, units)),
            pl.BlockSpec((tokens, step), lambda i: (0, i)),
        ],
        out_specs=(
            pl.BlockSpec((step, units), lambda i: (i, 0)),
            pl.BlockSpec((step, units), lambda i: (i, 0)),
            pl.BlockSpec((units, step), lambda i: (0, i)),
        ),
        scratch_shapes=[pltpu.VMEM((units, tokens), BF16)],
        compiler_params=params(BIG),
        cost_estimate=pl.CostEstimate(
            flops=6 * tokens * width * units,
            bytes_accessed=6 * width * units,
            transcendentals=0,
        ),
        name="weight_grads",
    )(normed, d_gate, d_up, hidden, cot)

    input_grads, gain_grads = pl.pallas_call(
        finish,
        out_shape=(shape((own, width), BF16), shape((1, width), F32)),
        in_specs=[smem()] + [vmem()] * (owners + 3),
        out_specs=(vmem(), vmem()),
        scratch_shapes=[pltpu.VMEM((owners, own, width // own), F32)],
        compiler_params=params(32),
        name="finish",
    )(mine, *by_mask, x_own, cot_rows, gain)
    return (
        query_grads,
        passage_grads,
        input_grads[None],
        gate_grads[None],
        up_grads[None],
        down_grads[None],
        gain_grads,
    )


def solution(mesh):
    pair = P(("dp", "segment"), None)
    token = P("segment", "dp", None)
    wide = P("segment", None, "dp")
    return jax.shard_map(
        local,
        mesh=mesh,
        in_specs=(pair, pair, pair, P(), token, token, P("segment", None), wide, wide, token),
        out_specs=(pair, pair, token, wide, wide, token, P("segment", None)),
        check_vma=False,
    )
```

```python
import jax
import jax.numpy as jnp
from jax import lax
from jax.experimental import pallas as pl
from jax.experimental.pallas import tpu as pltpu
from jax.sharding import PartitionSpec as P

HN_BLOCK = 128
TAU = 0.02
HN_WEIGHT = 64.0
EPS_NORM = 1e-06
EPS_RMS = 1e-05

F32 = jnp.float32
BF16 = jnp.bfloat16
MIB = 2**20
WINDOW = 3
BIG = 62
NT = (((1,), (1,)), ((), ()))
TN = (((0,), (0,)), ((), ()))


def vmem():
    return pl.BlockSpec(memory_space=pltpu.VMEM)


def smem():
    return pl.BlockSpec(memory_space=pltpu.SMEM)


def anywhere():
    return pl.BlockSpec(memory_space=pl.ANY)


def params(mib):
    return pltpu.CompilerParams(vmem_limit_bytes=mib * MIB)


def iota(shape, axis):
    return lax.broadcasted_iota(jnp.int32, shape, axis)


def split3(value):
    high = value.astype(BF16).astype(F32)
    rest = value - high
    middle = rest.astype(BF16).astype(F32)
    return high, middle, (rest - middle).astype(BF16).astype(F32)


def to_row(column, width):
    n = column.shape[0]
    pick = iota((n, width), 0) == iota((n, width), 1)
    return jnp.sum(jnp.where(pick, column, 0.0), axis=0, keepdims=True)


def to_columns(rows, n):
    shape = rows.shape[:-2] + (n, rows.shape[-1])
    pick = iota(shape, len(shape) - 2) == iota(shape, len(shape) - 1)
    return jnp.sum(jnp.where(pick, rows, 0.0), axis=-1, keepdims=True)


def row_inverse(ref, rows, mean, eps):
    total = jnp.zeros((rows, 1), F32)
    width = ref.shape[1]
    step = min(width, 1024)
    for at in range(0, width, step):
        part = ref[:, at : at + step].astype(F32)
        total += jnp.sum(part * part, axis=1, keepdims=True)
    if mean:
        total = total / width
    return lax.rsqrt(total + eps)


def pack_rows(query_hbm, passage_hbm, out_ref, query_ref, passage_ref, sems):
    count, block, cols = out_ref.shape
    rows = query_ref.shape[0]
    copies = [
        pltpu.make_async_copy(query_hbm, query_ref, sems.at[0]),
        pltpu.make_async_copy(passage_hbm, passage_ref, sems.at[1]),
    ]
    for copy in copies:
        copy.start()
    copies[0].wait()
    copies[1].wait()
    inverse = jnp.concatenate(
        [
            row_inverse(query_ref, rows, False, EPS_NORM),
            row_inverse(passage_ref, rows, False, EPS_NORM),
        ],
        axis=0,
    )
    terms = [to_row(term, cols) for term in split3(inverse)]
    extra = jnp.concatenate(
        terms + [jnp.zeros((block - 2 * rows - 3, cols), F32)], axis=0
    )
    for peer in range(count):
        cut = slice(peer * cols, (peer + 1) * cols)
        both = jnp.concatenate(
            [
                query_ref[:, cut].astype(F32),
                passage_ref[:, cut].astype(F32),
                extra,
            ],
            axis=0,
        )
        out_ref[peer] = both.astype(BF16)


def partial_scores(rows_ref, out_ref, unit_ref, inverse_ref):
    count, block, cols = rows_ref.shape
    rows = out_ref.shape[1]
    pairs = count * rows
    values = rows_ref[...].astype(F32)
    lines = values[:, 2 * rows : 2 * rows + 1]
    lines = lines + values[:, 2 * rows + 1 : 2 * rows + 2]
    lines = lines + values[:, 2 * rows + 2 : 2 * rows + 3]
    inverse = to_columns(lines, 2 * rows)
    unit = values[:, : 2 * rows] * inverse
    query_unit = unit[:, :rows].reshape(pairs, cols)
    passage_unit = unit[:, rows:].reshape(pairs, cols)
    unit_ref[0] = query_unit
    unit_ref[1] = passage_unit
    inverse_ref[0] = inverse[:, :rows].reshape(pairs, 1)
    inverse_ref[1] = inverse[:, rows:].reshape(pairs, 1)
    scores = lax.dot_general(
        query_unit.astype(BF16), passage_unit.astype(BF16), NT, preferred_element_type=F32
    )
    out_ref[...] = scores.reshape(out_ref.shape)


def softmax_rows(first_ref, parts_ref, offsets_ref, out_ref):
    count, block, pairs = out_ref.shape
    rows = parts_ref.shape[1]
    scores = jnp.sum(parts_ref[...], axis=0) / TAU
    row = first_ref[0] + iota((rows, pairs), 0)
    column = iota((rows, pairs), 1)
    base = row // HN_BLOCK * HN_BLOCK
    offsets = to_columns(offsets_ref[...].astype(F32)[:, None, :], rows).astype(jnp.int32)
    tallies = jnp.zeros((rows, pairs), F32)
    for k in range(offsets_ref.shape[0]):
        tallies += (base + offsets[k] == column).astype(F32)
    weighted = (1.0 + HN_WEIGHT * tallies) * jnp.exp(scores)
    totals = jnp.sum(weighted, axis=1, keepdims=True)
    dscore = weighted / totals - (row == column).astype(F32)
    dscore = dscore.astype(BF16).astype(F32)
    product = dscore * scores
    lines = list(split3(jnp.sum(product, axis=0, keepdims=True)))
    lines += [
        to_row(term, pairs) for term in split3(jnp.sum(product, axis=1, keepdims=True))
    ]
    lines.append(jnp.zeros((block - rows - 6, pairs), F32))
    message = jnp.concatenate([dscore] + lines, axis=0).astype(BF16)
    for peer in range(count):
        out_ref[peer] = message


def pair_grads(first, take, rows_ref, unit_ref, inverse_ref, out_ref):
    count, block, pairs = rows_ref.shape
    rows = pairs // count
    cols = unit_ref.shape[2]
    values = rows_ref[...].astype(F32)
    dscore = values[:, :rows].reshape(pairs, pairs).astype(BF16)
    column_line = jnp.sum(
        values[:, rows] + values[:, rows + 1] + values[:, rows + 2], axis=0, keepdims=True
    )
    column_dots = to_columns(column_line, pairs)
    row_lines = (
        values[:, rows + 3 : rows + 4]
        + values[:, rows + 4 : rows + 5]
        + values[:, rows + 5 : rows + 6]
    )
    row_dots = to_columns(row_lines, rows).reshape(pairs, 1)
    query_unit, passage_unit = unit_ref[0], unit_ref[1]
    query_dir = (
        jnp.dot(dscore, passage_unit.astype(BF16), preferred_element_type=F32) / TAU
    )
    passage_dir = (
        lax.dot_general(dscore, query_unit.astype(BF16), TN, preferred_element_type=F32) / TAU
    )
    query_grad = inverse_ref[0] * (query_dir - query_unit * row_dots)
    passage_grad = inverse_ref[1] * (passage_dir - passage_unit * column_dots)
    pieces = [
        query_grad.reshape(count, rows, cols),
        passage_grad.reshape(count, rows, cols),
    ]
    picked = passage_grad[first : first + take]
    spare = out_ref.shape[1] - 2 * rows - take
    if spare:
        picked = jnp.concatenate([picked, jnp.zeros((spare, cols), F32)], axis=0)
    pieces.append(jnp.broadcast_to(picked[None], (count,) + picked.shape))
    out_ref[...] = jnp.concatenate(pieces, axis=1).astype(BF16)


class Ring:
    def __init__(self, hbm, slots, sems, step):
        self.hbm, self.slots, self.sems, self.step = hbm, slots, sems, step

    def copy(self, c):
        slot = lax.rem(c, self.slots.shape[0])
        part = pl.ds(c * self.step, self.step)
        return pltpu.make_async_copy(self.hbm.at[part], self.slots.at[slot], self.sems.at[slot])


def forward(
    near_hbm,
    far_hbm,
    gain_ref,
    gate_hbm,
    up_hbm,
    normed_out,
    gate_out,
    up_out,
    x_s,
    gate_w,
    up_w,
    x_sem,
    gate_sem,
    up_sem,
):
    tokens, width = normed_out.shape
    step = gate_w.shape[1]
    blocks = width // step
    window = gate_w.shape[0]
    gate_ring = Ring(gate_hbm, gate_w, gate_sem, step)
    up_ring = Ring(up_hbm, up_w, up_sem, step)
    half = tokens // 2
    fetches = [
        pltpu.make_async_copy(near_hbm, x_s.at[pl.ds(0, half)], x_sem.at[0]),
        pltpu.make_async_copy(far_hbm, x_s.at[pl.ds(half, half)], x_sem.at[1]),
    ]
    for fetch in fetches:
        fetch.start()
    for c in range(min(window, blocks)):
        gate_ring.copy(c).start()
        up_ring.copy(c).start()
    for fetch in fetches:
        fetch.wait()
    x = x_s[...].astype(F32)
    inverse = lax.rsqrt(jnp.sum(x * x, axis=1, keepdims=True) / width + EPS_RMS)
    normed_out[...] = (x * inverse * gain_ref[...]).astype(BF16)

    def block(c, first):
        slot = lax.rem(c, window)
        cut = pl.ds(pl.multiple_of(c * step, step), step)
        normed = normed_out[:, cut]
        gate_ring.copy(c).wait()
        gate = jnp.dot(normed, gate_w[slot], preferred_element_type=F32)
        gate_out[...] = gate if first else gate_out[...] + gate
        up_ring.copy(c).wait()
        up = jnp.dot(normed, up_w[slot], preferred_element_type=F32)
        up_out[...] = up if first else up_out[...] + up

        @pl.when(c + window < blocks)
        def _():
            gate_ring.copy(c + window).start()
            up_ring.copy(c + window).start()

    def more(c, carry):
        block(c, False)
        return carry

    block(jnp.int32(0), True)
    lax.fori_loop(1, blocks, more, 0)


def delta_columns(cuts, rings, started, x_s, d_gate_t, d_up_t, outs, gain_s, inverse_s):
    owners = len(outs)
    own, total = outs[0].shape
    width = gain_s.shape[1]
    tokens = owners * own
    gate_ring, up_ring = rings
    step = gate_ring.step
    for c in range(started, min(WINDOW, cuts)):
        gate_ring.copy(c).start()
        up_ring.copy(c).start()
    x = x_s[...].astype(F32)
    inverse_s[...] = lax.rsqrt(jnp.sum(x * x, axis=1, keepdims=True) / width + EPS_RMS)

    def one(c, carry):
        slot = lax.rem(c, WINDOW)
        gate_ring.copy(c).wait()
        up_ring.copy(c).wait()
        cut = pl.ds(pl.multiple_of(c * step, step), step)
        delta = (
            jnp.dot(gate_ring.slots[slot], d_gate_t[...], preferred_element_type=F32)
            + jnp.dot(up_ring.slots[slot], d_up_t[...], preferred_element_type=F32)
        ).T
        low = delta.astype(BF16)
        for owner in range(owners):
            outs[owner][:, cut] = low[owner * own : (owner + 1) * own]
        unit = x_s[:, cut].astype(F32) * inverse_s[...]
        gain_s[:, cut] = jnp.sum(delta * unit, axis=0, keepdims=True)

        @pl.when(c + WINDOW < cuts)
        def _():
            gate_ring.copy(c + WINDOW).start()
            up_ring.copy(c + WINDOW).start()

        return carry

    lax.fori_loop(0, cuts, one, 0)
    fold = width // own
    gain = jnp.concatenate(
        [gain_s[:, r * fold : (r + 1) * fold] for r in range(own)], axis=0
    )
    for k in range(owners):
        outs[k][:, width:] = gain.astype(BF16)


def backward(
    order,
    cuts,
    deep_cuts,
    last_ref,
    mine_ref,
    lengths_ref,
    back_ref,
    x_near,
    x_far,
    cot_near,
    cot_far,
    gate_ref,
    up_ref,
    gate_hbm,
    up_hbm,
    down_hbm,
    query_out,
    passage_out,
    hidden_out,
    d_up_out,
    d_gate_out,
    cot_out,
    cot_own_out,
    *more,
):
    *by_mask, gate_w, up_w, down_w, d_up_t, d_gate_t, x_s, gain_s, inverse_s = more[:-3]
    delta_outs = [by_mask[mask] for mask in order]
    gate_sem, up_sem, down_sem = more[-3:]
    tokens, width = cot_out.shape
    units = gate_ref.shape[1]
    own = delta_outs[0].shape[0]
    deep = units // deep_cuts
    step = gain_s.shape[1] // cuts
    down_ring = Ring(down_hbm, down_w, down_sem, deep)
    gate_ring = Ring(gate_hbm, gate_w, gate_sem, step)
    up_ring = Ring(up_hbm, up_w, up_sem, step)
    early = min(WINDOW, deep_cuts, cuts)
    for c in range(min(WINDOW, deep_cuts)):
        down_ring.copy(c).start()

    count, block, cols = back_ref.shape
    rows = query_out.shape[0]
    passages = block - 2 * rows
    token = jnp.concatenate(
        [iota((own, 1), 0) + (mine_ref[0] ^ mask) * own for mask in order], axis=0
    )
    half = tokens // 2
    x_s[:half, :] = x_near[...]
    x_s[half:, :] = x_far[...]
    lane = iota((tokens, passages), 1)
    start = jnp.int32(0)
    member = jnp.zeros((tokens, passages), F32)
    scale = jnp.zeros((tokens, 1), F32)
    for m in range(lengths_ref.shape[0]):
        length = lengths_ref[m]
        inside = jnp.logical_and(token >= start, token < start + length)
        member = jnp.where(jnp.logical_and(inside, lane == m), 1.0, member)
        scale = jnp.where(inside, 1.0 / (jnp.zeros((tokens, 1), F32) + length.astype(F32)), scale)
        start = start + length
    member = member.astype(BF16)
    last = last_ref[0] == 1
    for peer in range(count):
        cut = slice(peer * cols, (peer + 1) * cols)
        piece = back_ref[peer].astype(F32)
        query_out[:, cut] = piece[:rows].astype(BF16)
        passage_out[:, cut] = piece[rows : 2 * rows].astype(BF16)
        spread = jnp.dot(member, piece[2 * rows :].astype(BF16), preferred_element_type=F32)
        pooled = (spread * scale).astype(BF16)
        given = jnp.concatenate([cot_near[:, cut], cot_far[:, cut]], axis=0)
        cot_out[:, cut] = jnp.where(last, pooled, given)

    cot_own_out[...] = cot_out[:own, :]

    def down_step(c, carry):
        slot = lax.rem(c, WINDOW)
        down_ring.copy(c).wait()
        cut = pl.ds(pl.multiple_of(c * deep, deep), deep)
        d_hidden = lax.dot_general(cot_out[...], down_w[slot], NT, preferred_element_type=F32)
        gate, up = gate_ref[:, cut], up_ref[:, cut]
        sigmoid = jax.nn.sigmoid(gate)
        active = gate * sigmoid
        hidden_out[:, cut] = (active * up).astype(BF16)
        d_up = (d_hidden * active).astype(BF16)
        d_gate = (d_hidden * up * sigmoid * (1.0 + gate * (1.0 - sigmoid))).astype(BF16)
        d_up_out[:, cut] = d_up
        d_gate_out[:, cut] = d_gate
        d_up_t[cut, :] = d_up.T
        d_gate_t[cut, :] = d_gate.T
        ahead = c + WINDOW

        @pl.when(ahead < deep_cuts)
        def _():
            down_ring.copy(ahead).start()

        late = c - (deep_cuts - early)

        @pl.when(late >= 0)
        def _():
            gate_ring.copy(late).start()
            up_ring.copy(late).start()

        return carry

    lax.fori_loop(0, deep_cuts, down_step, 0)
    delta_columns(
        cuts,
        (gate_ring, up_ring),
        early,
        x_s,
        d_gate_t,
        d_up_t,
        delta_outs,
        gain_s,
        inverse_s,
    )


def weight_grads(
    normed_ref, d_gate_ref, d_up_ref, hidden_ref, cot_ref, gate_out, up_out, down_out, hidden_t
):
    @pl.when(pl.program_id(0) == 0)
    def _():
        hidden_t[...] = hidden_ref[...].T

    gate_out[...] = lax.dot_general(
        normed_ref[...], d_gate_ref[...], TN, preferred_element_type=F32
    ).astype(BF16)
    up_out[...] = lax.dot_general(
        normed_ref[...], d_up_ref[...], TN, preferred_element_type=F32
    ).astype(BF16)
    down_out[...] = jnp.dot(
        hidden_t[...], cot_ref[...], preferred_element_type=F32
    ).astype(BF16)


def finish(mine_ref, *refs):
    *part_refs, x_ref, cot_ref, gain_ref, input_out, gain_out, tail_s = refs
    owners = len(part_refs)
    own, width = x_ref.shape
    fold = width // own
    for k in range(owners):
        tail_s[mine_ref[0] ^ k] = part_refs[k][:, width:].astype(F32)
    gain = tail_s[0]
    for p in range(1, owners):
        gain += tail_s[p]
    for r in range(own):
        gain_out[:, r * fold : (r + 1) * fold] = gain[r : r + 1]
    delta = part_refs[0][:, :width].astype(F32)
    for k in range(1, owners):
        delta += part_refs[k][:, :width].astype(F32)
    inverse = row_inverse(x_ref, own, True, EPS_RMS)
    unit = x_ref[...].astype(F32) * inverse
    scaled = delta * gain_ref[...]
    mean = jnp.sum(scaled * unit, axis=1, keepdims=True) / width
    input_out[...] = (
        cot_ref[...].astype(F32) + inverse * (scaled - unit * mean)
    ).astype(BF16)


def shape(dims, dtype):
    return jax.ShapeDtypeStruct(dims, dtype)


def local(
    query_cache,
    passage_cache,
    hard_offsets,
    passage_lengths,
    segment_inputs,
    segment_cotangents,
    norm_gain,
    gate_weight,
    up_weight,
    down_weight,
):
    everyone = ("dp", "segment")
    count = lax.axis_size(everyone)
    owners = lax.axis_size("dp")
    sections = lax.axis_size("segment")
    rows, width = query_cache.shape
    pairs = rows * count
    cols = width // count
    passages = passage_lengths.shape[0]
    own = segment_inputs.shape[1]
    tokens = own * owners
    units = gate_weight.shape[2]
    room = min(BIG, 45 + tokens // 16)
    section = lax.axis_index("segment")
    dp = lax.axis_index("dp")
    first_row = (lax.axis_index(everyone) * rows).astype(jnp.int32).reshape(1)
    is_last = (section == sections - 1).astype(jnp.int32).reshape(1)
    mine = dp.astype(jnp.int32).reshape(1)

    assert owners & (owners - 1) == 0 and owners > 1
    x_own, cot_own, gain = segment_inputs[0], segment_cotangents[0], norm_gain
    block1 = 4 * rows
    message = pl.pallas_call(
        pack_rows,
        out_shape=shape((count, block1, cols), BF16),
        in_specs=[anywhere()] * 2,
        out_specs=vmem(),
        scratch_shapes=[
            pltpu.VMEM((rows, width), BF16),
            pltpu.VMEM((rows, width), BF16),
            pltpu.SemaphoreType.DMA((2,)),
        ],
        compiler_params=params(BIG),
        name="pack_rows",
    )(query_cache, passage_cache)
    order = [0]
    x_half, cot_half = x_own, cot_own
    moved = []

    def double(values):
        nonlocal x_half, cot_half
        if len(order) == owners:
            return values
        if moved:
            x_half = jnp.concatenate([x_half, moved[0]], axis=0)
            cot_half = jnp.concatenate([cot_half, moved[1]], axis=0)
        mask = owners // 2 // len(order)
        swap = [(i, i ^ mask) for i in range(owners)]
        x_far = lax.ppermute(x_half, "dp", swap)
        if mask == 1:
            x_far, cot_half = lax.optimization_barrier((x_far, cot_half))
        moved[:] = [x_far, lax.ppermute(cot_half, "dp", swap)]
        order.extend([o ^ mask for o in order])
        return values

    message = double(message)
    message = lax.all_to_all(message, everyone, 0, 0, tiled=True)
    message = double(message)
    parts, unit, inverse = pl.pallas_call(
        partial_scores,
        out_shape=(
            shape((count, rows, pairs), F32),
            shape((2, pairs, cols), F32),
            shape((2, pairs, 1), F32),
        ),
        in_specs=[vmem()],
        out_specs=(vmem(), vmem(), vmem()),
        compiler_params=params(32),
        name="partial_scores",
    )(message)
    parts = lax.all_to_all(parts, everyone, 0, 0, tiled=True)
    parts = double(parts)
    message = pl.pallas_call(
        softmax_rows,
        out_shape=shape((count, 2 * rows, pairs), BF16),
        in_specs=[smem(), vmem(), vmem()],
        out_specs=vmem(),
        compiler_params=params(32),
        name="softmax_rows",
    )(first_row, parts, hard_offsets.T)
    message = lax.all_to_all(message, everyone, 0, 0, tiled=True)
    back = -(-(2 * rows + passages) // 16) * 16
    message = pl.pallas_call(
        lambda *refs: pair_grads((sections - 1) * rows, passages, *refs),
        out_shape=shape((count, back, cols), BF16),
        in_specs=[vmem(), vmem(), vmem()],
        out_specs=vmem(),
        compiler_params=params(48),
        name="pair_grads",
    )(message, unit, inverse)
    message = lax.all_to_all(message, everyone, 0, 0, tiled=True)

    while len(order) < owners:
        message = double(message)
    halves = (x_half, moved[0], cot_half, moved[1])
    whole = lambda dims: pl.BlockSpec(dims, lambda i: (0,) * len(dims))
    ring = pltpu.SemaphoreType.DMA((WINDOW,))
    step = min(1024, width)
    normed, gate, up = pl.pallas_call(
        forward,
        out_shape=(
            shape((tokens, width), BF16),
            shape((tokens, units), F32),
            shape((tokens, units), F32),
        ),
        in_specs=[anywhere(), anywhere(), vmem(), anywhere(), anywhere()],
        out_specs=(vmem(), vmem(), vmem()),
        scratch_shapes=[
            pltpu.VMEM((tokens, width), BF16),
            pltpu.VMEM((2, step, units), BF16),
            pltpu.VMEM((2, step, units), BF16),
            pltpu.SemaphoreType.DMA((2,)),
            pltpu.SemaphoreType.DMA((2,)),
            pltpu.SemaphoreType.DMA((2,)),
        ],
        compiler_params=params(room),
        cost_estimate=pl.CostEstimate(
            flops=4 * tokens * width * units,
            bytes_accessed=4 * width * units,
            transcendentals=0,
        ),
        name="forward",
    )(*halves[:2], gain, gate_weight[0], up_weight[0])

    cuts = max(1, width // 512)
    deep_cuts = units // 256 if units % 256 == 0 else 1
    part_shape = shape((own, width + width // own), BF16)
    block = (WINDOW, width // cuts, units)
    outs = pl.pallas_call(
        lambda *refs: backward(order, cuts, deep_cuts, *refs),
        out_shape=(
            shape((rows, width), BF16),
            shape((rows, width), BF16),
            shape((tokens, units), BF16),
            shape((tokens, units), BF16),
            shape((tokens, units), BF16),
            shape((tokens, width), BF16),
            shape((own, width), BF16),
        )
        + (part_shape,) * owners,
        in_specs=[smem(), smem(), smem()] + [vmem()] * 7 + [anywhere()] * 3,
        out_specs=tuple(vmem() for _ in range(7 + owners)),
        scratch_shapes=[
            pltpu.VMEM(block, BF16),
            pltpu.VMEM(block, BF16),
            pltpu.VMEM((WINDOW, units // deep_cuts, width), BF16),
            pltpu.VMEM((units, tokens), BF16),
            pltpu.VMEM((units, tokens), BF16),
            pltpu.VMEM((tokens, width), BF16),
            pltpu.VMEM((1, width), F32),
            pltpu.VMEM((tokens, 1), F32),
            ring,
            ring,
            ring,
        ],
        compiler_params=params(room),
        cost_estimate=pl.CostEstimate(
            flops=6 * tokens * width * units,
            bytes_accessed=6 * width * units,
            transcendentals=tokens * units,
        ),
        name="backward",
    )(
        is_last,
        mine,
        passage_lengths,
        message,
        *halves,
        gate,
        up,
        gate_weight[0],
        up_weight[0],
        down_weight[0],
    )
    query_grads, passage_grads, hidden, d_up, d_gate, cot, cot_rows = outs[:7]
    by_mask = list(outs[7:])
    for mask in range(1, owners):
        by_mask[mask] = lax.ppermute(
            by_mask[mask], "dp", [(i, i ^ mask) for i in range(owners)]
        )

    step = min(512, width)
    gate_grads, up_grads, down_grads = pl.pallas_call(
        weight_grads,
        grid=(width // step,),
        out_shape=(
            shape((width, units), BF16),
            shape((width, units), BF16),
            shape((units, width), BF16),
        ),
        in_specs=[
            pl.BlockSpec((tokens, step), lambda i: (0, i)),
            whole((tokens, units)),
            whole((tokens, units)),
            whole((tokens, units)),
            pl.BlockSpec((tokens, step), lambda i: (0, i)),
        ],
        out_specs=(
            pl.BlockSpec((step, units), lambda i: (i, 0)),
            pl.BlockSpec((step, units), lambda i: (i, 0)),
            pl.BlockSpec((units, step), lambda i: (0, i)),
        ),
        scratch_shapes=[pltpu.VMEM((units, tokens), BF16)],
        compiler_params=params(BIG),
        cost_estimate=pl.CostEstimate(
            flops=6 * tokens * width * units,
            bytes_accessed=6 * width * units,
            transcendentals=0,
        ),
        name="weight_grads",
    )(normed, d_gate, d_up, hidden, cot)

    input_grads, gain_grads = pl.pallas_call(
        finish,
        out_shape=(shape((own, width), BF16), shape((1, width), F32)),
        in_specs=[smem()] + [vmem()] * (owners + 3),
        out_specs=(vmem(), vmem()),
        scratch_shapes=[pltpu.VMEM((owners, own, width // own), F32)],
        compiler_params=params(32),
        name="finish",
    )(mine, *by_mask, x_own, cot_rows, gain)
    return (
        query_grads,
        passage_grads,
        input_grads[None],
        gate_grads[None],
        up_grads[None],
        down_grads[None],
        gain_grads,
    )


def solution(mesh):
    pair = P(("dp", "segment"), None)
    token = P("segment", "dp", None)
    wide = P("segment", None, "dp")
    return jax.shard_map(
        local,
        mesh=mesh,
        in_specs=(pair, pair, pair, P(), token, token, P("segment", None), wide, wide, token),
        out_specs=(pair, pair, token, wide, wide, token, P("segment", None)),
        check_vma=False,
    )
```
